256 devices in a mesh: row: 8 (over z), col: 8 (over x_hi, y), samp: 4 (over x_lo, core).
Axes of the slice: x: 4 (x_hi: 2, x_lo: 2; x = x_hi * 2 + x_lo), y: 4, z: 8, core: 2. Of those that a mesh axis runs over, the one named last changes fastest.
Arguments:
- pair: bfloat16 [768, 768, 128], P('row', 'col'), may hold values from -6 to 6
- crop_mask: int32 [768], replicated, may hold values 0 or 1
- w_agate: bfloat16 [128, 128], replicated, may hold values from -0.5 to 0.5
- w_aval: bfloat16 [128, 128], replicated, may hold values from -0.5 to 0.5
- w_bgate: bfloat16 [128, 128], replicated, may hold values from -0.5 to 0.5
- w_bval: bfloat16 [128, 128], replicated, may hold values from -0.5 to 0.5
- w_outgate: bfloat16 [128, 128], replicated, may hold values from -0.5 to 0.5
- w_outproj: bfloat16 [128, 128], replicated, may hold values from -0.5 to 0.5
- ln_pair: float32 [128], replicated, may hold values from 0.1 to 1.9
- w_trans_gate: bfloat16 [128, 512], replicated, may hold values from -0.5 to 0.5
- w_trans_up: bfloat16 [128, 512], replicated, may hold values from -0.5 to 0.5
- w_trans_down: bfloat16 [512, 128], replicated, may hold values from -0.25 to 0.25
- ln_bias: float32 [128], replicated, may hold values from 0.1 to 1.9
- w_pairbias: bfloat16 [128, 16], replicated, may hold values from -0.5 to 0.5
- tokens: bfloat16 [16, 768, 768], P('samp', 'row', 'col'), may hold values from -6 to 6
- ln_token: float32 [768], replicated, may hold values from 0.1 to 1.9
- w_query: bfloat16 [768, 768], P(None, 'col'), may hold values from -1 to 1
- w_key: bfloat16 [768, 768], P(None, 'col'), may hold values from -1 to 1
- w_value: bfloat16 [768, 768], P(None, 'col'), may hold values from -0.21875 to 0.21875
- w_gate: bfloat16 [768, 768], P(None, 'col'), may hold values from -0.21875 to 0.21875
- w_output: bfloat16 [768, 768], P('col'), may hold values from -0.21875 to 0.21875
- cotangent: bfloat16 [16, 768, 768], P('samp', 'row', 'col'), may hold values from -6 to 6
Outputs:
- pair_out: bfloat16 [768, 768, 128], P('row', 'col')
- tokens_out: bfloat16 [16, 768, 768], P('samp', 'row', 'col')
- pair_grad: float32 [768, 768, 128], P('row', 'col')
The draws below stay inside these ranges and needn't reach their ends.
All inputs are finite; a program needn't handle non-finite values.
Results may differ from the reference program's by a relative error of at most 0.015.
Values may be sent and summed in bfloat16 or wider, within the bound.
A program may use at most 128 MiB of HBM per device.

```python
import math
import jax
import jax.numpy as jnp
from jax import lax

D = 768
H = 16
HD = 48
CP = 128
HT = 512
ROWS_DEV = 96
N = 768
S = 16
N_ROW = 8


def draw_w_query(key, part):
    key = jax.random.fold_in(key, 11)
    own = jax.random.normal(key, (D, D), jnp.float32)
    mixed = own
    return jnp.clip(mixed / math.sqrt(D), -1.0, 1.0).astype(jnp.bfloat16)


def draw_w_key(key, part):
    key = jax.random.fold_in(key, 12)
    own = jax.random.normal(key, (D, D), jnp.float32)
    mixed = own
    return jnp.clip(mixed / math.sqrt(D), -1.0, 1.0).astype(jnp.bfloat16)


def place_ends(array, rng, low, largest):
    index_at = [jax.random.randint(jax.random.fold_in(rng, axis), (), 0, length) for axis, length in enumerate(array.shape)]
    main_axis = array.shape.index(max(array.shape))
    next_to = index_at[:main_axis] + [(index_at[main_axis] + 1) % array.shape[main_axis]] + index_at[main_axis + 1:]
    return array.at[tuple(index_at)].set(low).at[tuple(next_to)].set(largest)


def level_of(key, dims, pieces, smallest, high):
    factor_of, own = 1.0, jax.random.fold_in(key, 6)
    for position, shards_of in pieces:
        heights = jnp.exp(jax.random.uniform(jax.random.fold_in(own, position), (shards_of,), jnp.float32, smallest / len(pieces), high / len(pieces)))
        factor_of = factor_of * jnp.repeat(heights, dims[position] // shards_of).reshape([-1 if axis == position else 1 for axis in range(len(dims))])
    return factor_of


def normal_values(rng, shape, width, reach, pieces=(), dtype=jnp.bfloat16):
    drawn = width * jax.random.normal(rng, shape, jnp.float32)
    if pieces:
        drawn = drawn * level_of(rng, shape, pieces, -0.22, 0.18)
    return jnp.clip(drawn, -reach, reach).astype(dtype)


def setup_inputs(seed: int = 0) -> dict:
    keys = jax.random.split(jax.random.key(seed), 23)
    return {
        "pair": normal_values(keys[0], (N, N, CP), 1.0, 6.0, ((0, 8), (1, 8))),
        "crop_mask": place_ends((jax.random.randint(keys[1], (N,), 0, 8) < 7).astype(jnp.int32), jax.random.fold_in(keys[1], 1), 0, 1),
        "w_agate": normal_values(keys[2], (CP, CP), CP ** -0.5, 0.5),
        "w_aval": normal_values(keys[3], (CP, CP), CP ** -0.5, 0.5),
        "w_bgate": normal_values(keys[4], (CP, CP), CP ** -0.5, 0.5),
        "w_bval": normal_values(keys[5], (CP, CP), CP ** -0.5, 0.5),
        "w_outgate": normal_values(keys[6], (CP, CP), CP ** -0.5, 0.5),
        "w_outproj": normal_values(keys[7], (CP, CP), CP ** -0.5, 0.5),
        "ln_pair": jnp.clip(1.0 + 0.18 * jax.random.normal(keys[8], (CP,), jnp.float32), 0.1, 1.9),
        "w_trans_gate": normal_values(keys[9], (CP, HT), CP ** -0.5, 0.5),
        "w_trans_up": normal_values(keys[10], (CP, HT), CP ** -0.5, 0.5),
        "w_trans_down": normal_values(keys[11], (HT, CP), HT ** -0.5, 0.25),
        "ln_bias": jnp.clip(1.0 + 0.18 * jax.random.normal(keys[12], (CP,), jnp.float32), 0.1, 1.9),
        "w_pairbias": normal_values(keys[13], (CP, H), CP ** -0.5, 0.5),
        "tokens": normal_values(keys[14], (S, N, D), 1.0, 6.0, ((0, 4), (1, 8), (2, 8))),
        "ln_token": jnp.clip(1.0 + 0.18 * jax.random.normal(keys[15], (D,), jnp.float32), 0.1, 1.9),
        "w_query": draw_w_query(jax.random.fold_in(keys[22], 71), 0),
        "w_key": draw_w_key(jax.random.fold_in(keys[22], 71), 0),
        "w_value": normal_values(keys[18], (D, D), D ** -0.5, 0.21875, ((1, 8),)),
        "w_gate": normal_values(keys[19], (D, D), D ** -0.5, 0.21875, ((1, 8),)),
        "w_output": normal_values(keys[20], (D, D), D ** -0.5, 0.21875, ((0, 8),)),
        "cotangent": normal_values(keys[21], (S, N, D), 1.0, 6.0, ((0, 4), (1, 8), (2, 8))),
    }


def normalize(values):
    center = values - lax.optimization_barrier(jnp.mean(values, axis=-1, keepdims=True))
    return center * lax.rsqrt(lax.optimization_barrier(jnp.mean(center * center, axis=-1, keepdims=True)) + 1e-05)

def pair_transition(pair_rows, w_trans_gate, w_trans_up, w_trans_down):
    trans_in = normalize(pair_rows.astype(jnp.float32)).astype(jnp.bfloat16)
    gate_part = jax.nn.silu(jnp.dot(trans_in, w_trans_gate, preferred_element_type=jnp.float32))
    hidden = (gate_part * jnp.dot(trans_in, w_trans_up, preferred_element_type=jnp.float32)).astype(jnp.bfloat16)
    return (pair_rows.astype(jnp.float32) + jnp.dot(hidden, w_trans_down, preferred_element_type=jnp.float32)).astype(jnp.bfloat16)

def reference(pair, crop_mask, w_agate, w_aval, w_bgate, w_bval, w_outgate, w_outproj, ln_pair, w_trans_gate, w_trans_up, w_trans_down, ln_bias, w_pairbias, tokens, ln_token, w_query, w_key, w_value, w_gate, w_output, cotangent):
    floats = pair.astype(jnp.float32)
    normed = (normalize(floats) * ln_pair.astype(jnp.float32)).astype(jnp.bfloat16)
    keep = crop_mask.astype(jnp.float32)
    pair_keep = (keep[:, None] * keep[None, :])[:, :, None]
    left = (jax.nn.sigmoid(jnp.dot(normed, w_agate, preferred_element_type=jnp.float32)) * jnp.dot(normed, w_aval, preferred_element_type=jnp.float32) * pair_keep).astype(jnp.bfloat16)
    right = (jax.nn.sigmoid(jnp.dot(normed, w_bgate, preferred_element_type=jnp.float32)) * jnp.dot(normed, w_bval, preferred_element_type=jnp.float32) * pair_keep).astype(jnp.bfloat16)
    right_wide = right.astype(jnp.float32)

    def contract(left_rows):
        return jnp.einsum('ikc,jkc->ijc', left_rows, right_wide)
    left_blocks = left.astype(jnp.float32).reshape(N_ROW, ROWS_DEV, N, CP)
    triangle = lax.map(contract, left_blocks).reshape(N, N, CP).astype(jnp.bfloat16)
    tri_norm = normalize(triangle.astype(jnp.float32)).astype(jnp.bfloat16)
    out_gate = jax.nn.sigmoid(jnp.dot(normed, w_outgate, preferred_element_type=jnp.float32))
    updated = (floats + out_gate * jnp.dot(tri_norm, w_outproj, preferred_element_type=jnp.float32)).astype(jnp.bfloat16)

    def transition_rows(pair_rows):
        return pair_transition(pair_rows, w_trans_gate, w_trans_up, w_trans_down)
    pair_out = lax.map(transition_rows, updated.reshape(N_ROW, ROWS_DEV, N, CP)).reshape(N, N, CP)
    final = pair_out.astype(jnp.float32)
    center = final - lax.optimization_barrier(jnp.mean(final, axis=-1, keepdims=True))
    inv_scale = lax.rsqrt(lax.optimization_barrier(jnp.mean(center * center, axis=-1, keepdims=True)) + 1e-05)
    unit = center * inv_scale
    bias_in = (unit * ln_bias.astype(jnp.float32)).astype(jnp.bfloat16)
    head_bias = jnp.transpose(jnp.dot(bias_in, w_pairbias, preferred_element_type=jnp.float32).astype(jnp.bfloat16), (2, 0, 1)).astype(jnp.float32)
    key_mask = (keep - 1.0) * 10000.0
    scale = 1.0 / math.sqrt(HD)

    def sample_step(carry, inputs):
        token_rows, grad_rows = inputs
        token_wide = token_rows.astype(jnp.float32)
        token_norm = (normalize(token_wide) * ln_token.astype(jnp.float32)).astype(jnp.bfloat16)
        query = jnp.dot(token_norm, w_query, preferred_element_type=jnp.float32).astype(jnp.bfloat16).reshape(N, H, HD).astype(jnp.float32)
        keyed = jnp.dot(token_norm, w_key, preferred_element_type=jnp.float32).astype(jnp.bfloat16).reshape(N, H, HD).astype(jnp.float32)
        value = jnp.dot(token_norm, w_value, preferred_element_type=jnp.float32).astype(jnp.bfloat16).reshape(N, H, HD).astype(jnp.float32)
        gate_val = jax.nn.sigmoid(jnp.dot(token_norm, w_gate, preferred_element_type=jnp.float32))
        scores = jnp.einsum('ihd,jhd->hij', query, keyed) * scale + head_bias + key_mask[None, None, :]
        shifted = jnp.exp(scores - lax.optimization_barrier(jnp.max(scores, axis=-1, keepdims=True)))
        probs = shifted / lax.optimization_barrier(jnp.sum(shifted, axis=-1, keepdims=True))
        weights = probs.astype(jnp.bfloat16).astype(jnp.float32)
        attended = jnp.einsum('hij,jhd->ihd', weights, value)
        gated = (gate_val * attended.reshape(N, D)).astype(jnp.bfloat16)
        token_new = (token_wide + jnp.dot(gated, w_output, preferred_element_type=jnp.float32)).astype(jnp.bfloat16)
        d_gated = jnp.dot(grad_rows, jnp.transpose(w_output), preferred_element_type=jnp.float32)
        d_att = (d_gated * gate_val).astype(jnp.bfloat16).reshape(N, H, HD).astype(jnp.float32)
        d_probs = jnp.einsum('ihd,jhd->hij', d_att, value)
        delta = jnp.einsum('ihd,ihd->hi', d_att, attended)[:, :, None]
        d_scores = probs * (d_probs - delta)
        return (carry + d_scores, token_new)
    bias_grad, tokens_out = lax.scan(sample_step, jnp.zeros((H, N, N), jnp.float32), (tokens, cotangent))
    back = jnp.einsum('hij,ch->ijc', bias_grad, w_pairbias.astype(jnp.float32), precision=lax.Precision.HIGHEST)
    scaled = back * ln_bias.astype(jnp.float32)
    pair_grad = inv_scale * (scaled - lax.optimization_barrier(jnp.mean(scaled, axis=-1, keepdims=True)) - unit * lax.optimization_barrier(jnp.mean(scaled * unit, axis=-1, keepdims=True)))
    return (pair_out, tokens_out, pair_grad)
```

```python
import math

import jax
import jax.numpy as jnp
from jax import lax
from jax.experimental import pallas as pl
from jax.experimental.pallas import tpu as pltpu
from jax.sharding import PartitionSpec as P

F32 = jnp.float32
BF16 = jnp.bfloat16
MESH = pl.DeviceIdType.MESH
NR = 8
NC = 8
NS = 4
B = 96
Q = 24
G = 24
CH = 4
RC = 6 * B


def nt(a, b):
    return lax.dot_general(a, b, (((1,), (1,)), ((), ())), preferred_element_type=F32)


def nn(a, b):
    return lax.dot_general(a, b, (((1,), (0,)), ((), ())), preferred_element_type=F32)


def tn(a, b):
    return lax.dot_general(a, b, (((0,), (0,)), ((), ())), preferred_element_type=F32)


def row_means(values, ones):
    high = values.astype(BF16)
    low = (values - high.astype(F32)).astype(BF16)
    return nn(jnp.concatenate([high, low], axis=1), ones)


def centered(values, ones):
    center = values.astype(F32) - nn(values, ones[0:128])
    return center, lax.rsqrt(row_means(center * center, ones) + 1e-05)


def normalize(values, ones):
    center, inv = centered(values, ones)
    return center * inv


def mean_weights():
    return jnp.full((256, 128), 1.0 / 128.0, BF16)


def kernel(
    pair, crop_s, crop_v, w_ag, w_av, w_bg, w_bv, lnp, w_outgate, w_outproj, w_tg, w_tu, w_td,
    lnb, wpbt, tokens, cot, lnt, wq, wk, wv, wg, wo,
    pair_out, tokens_out, bg,
    wt, w_op, xd, cd,
    normed, lf, rf, lm, rslab, part, y_recv, own_sum, x_send, x_recv, tok_slab, cot_slab, q_s, kslab, vslab, gate_s, datt_s,
    tri_send, tri_recv, tri_f, hb_send, hb, bias, acc, pj_send, pj_recv, rs_recv, sg, cg,
    tok_ss, tok_rs, cot_ss, cot_rs, ring_ss, ring_rs, y_ss, y_rs, x_ss, x_rs,
    k_ss, k_rs, v_ss, v_rs, t_ss, t_rs, h_ss, h_rs,
    hg_ss, hg_rs, po_ss, po_rs, pj_ss, pj_rs, g_ss, g_rs, c_ss, c_rs, b_ss, b_rs,
):
    row = lax.axis_index("row")
    col = lax.axis_index("col")
    samp = lax.axis_index("samp")
    xh = col // 4
    yy = col % 4
    xp = (1 - xh) * 4 + yy
    ones = mean_weights()
    right = (row + 1) % NR
    left = (row + NR - 1) % NR

    def copy(src, dst, ss, rs, **where):
        return pltpu.make_async_remote_copy(
            src_ref=src, dst_ref=dst, send_sem=ss, recv_sem=rs, device_id=where, device_id_type=MESH
        )

    barrier = pltpu.get_barrier_semaphore()
    for d in range(1, NC):
        pl.semaphore_signal(barrier, inc=1, device_id={"col": (col + d) % NC}, device_id_type=MESH)
    for d in range(1, NR):
        pl.semaphore_signal(barrier, inc=1, device_id={"row": (row + d) % NR}, device_id_type=MESH)
    for d in range(1, NS):
        pl.semaphore_signal(
            barrier, inc=1, device_id={"samp": (samp + d) % NS}, device_id_type=MESH
        )

    pl.semaphore_wait(barrier, NC + NR + NS - 3)

    def col_all(src_of, slab, ss, rs, d):
        there, here = (col + d) % NC, (col + NC - d) % NC
        return (
            copy(src_of(there), slab.at[col], ss.at[d], rs.at[d], col=there),
            copy(src_of(there), slab.at[here], ss.at[d], rs.at[d], col=there),
        )

    tok_copies = [col_all(lambda _: tokens, tok_slab, tok_ss, tok_rs, d) for d in range(1, NC)]
    cot_copies = [col_all(lambda _: cot, cot_slab, cot_ss, cot_rs, d) for d in range(1, NC)]
    for out, _ in tok_copies + cot_copies:
        out.start()
    tok_slab[col] = tokens[...]
    cot_slab[col] = cot[...]

    for n, w in enumerate((w_ag, w_av, w_bg, w_bv)):
        wt[n] = w[...].astype(F32).T.astype(BF16)
    wp = jnp.concatenate([wt[n, pl.ds(pl.multiple_of(samp * 32, 32), 32), :] for n in range(4)], axis=0)
    tri_f[0:128, :] = w_outproj[...].astype(F32)
    w_op[...] = jnp.concatenate(
        [tri_f[pl.ds(0, 64, stride=2), :], tri_f[pl.ds(1, 64, stride=2), :]], axis=0
    ).astype(BF16)
    keep_cols = jnp.zeros((1, B), F32)
    for b in range(NC):
        here = crop_v[0:1, b * B : b * B + B].astype(F32)
        keep_cols = jnp.where(col == b, here, keep_cols)
    keep_cols = jnp.concatenate([keep_cols, jnp.zeros((1, 32), F32)], axis=1)

    def norm_step(m, carry):
        at = pl.ds(pl.multiple_of(m * 384, 384), 384)
        normed[at, :] = (normalize(pair[at, :], ones) * lnp[...]).astype(BF16)
        return carry

    lax.fori_loop(0, B // 4, norm_step, 0)
    normed[B * B : B * B + 32, :] = jnp.zeros((32, 128), BF16)
    lane = lax.broadcasted_iota(jnp.int32, (8, 128), 1)
    wide = lane < B

    def edge_step(m, carry):
        for e in range(4):
            i = m * 4 + e
            rows = normed[pl.ds(pl.multiple_of(i * B, 32), 128), :]
            o = nt(wp, rows)
            kept = keep_cols * crop_s[row * B + i].astype(F32)
            for first, dest in ((0, lf), (64, rf)):
                edge = jax.nn.sigmoid(o[first : first + 32]) * o[first + 32 : first + 64] * kept
                tail = edge[24:32]
                for q in range(3):
                    packed = jnp.where(
                        wide, edge[8 * q : 8 * q + 8], pltpu.roll(tail, 96 - 32 * q, 1)
                    )
                    dest[pl.ds(i + 8 * B * q, 8, stride=B), :] = packed
        return carry

    lax.fori_loop(0, B // 4, edge_step, 0)

    own = lax.broadcasted_iota(jnp.int32, (B, 128), 1) < B
    for n in range(CH):
        for k in range(6):
            g, q = 2 * n + k // 3, k % 3
            at = pl.ds((q * 8 + g) * B, B)
            rslab[n, row, k * B : k * B + B, :] = rf[at, :].astype(BF16)
            edge = lf[at, :]
            lm[6 * n + k, 0:B, :] = jnp.where(own, edge, 0.0).astype(BF16)
            lm[6 * n + k, B : 2 * B, :] = jnp.where(own, 0.0, edge).astype(BF16)
    for n in range(CH):
        rslab[n, :, RC : RC + 32, :] = jnp.zeros((NR, 32, 128), BF16)

    def token_step(s):
        at = pl.ds(s * B, B)
        x = [tok_slab[b, at, :].astype(F32) for b in range(NC)]
        total = x[0]
        for b in range(1, NC):
            total = total + x[b]
        mean = jnp.sum(total, axis=-1, keepdims=True) * (1.0 / (NC * B))
        x = [v - mean for v in x]
        total = x[0] * x[0]
        for b in range(1, NC):
            total = total + x[b] * x[b]
        scale = lax.rsqrt(jnp.sum(total, axis=-1, keepdims=True) * (1.0 / (NC * B)) + 1e-05)
        for b in range(NC):
            xd[:, b * B : b * B + B] = x[b] * scale
            cd[:, b * B : b * B + B] = cot_slab[b, at, :].astype(F32)
        normal = (xd[...] * lnt[...]).astype(BF16)
        q_s[at, :] = nt(normal, wq[...]).astype(BF16)
        kslab[row, at, :] = nt(normal, wk[...]).astype(BF16)
        vslab[row, at, :] = nt(normal, wv[...]).astype(BF16)
        gate = jax.nn.sigmoid(nt(normal, wg[...]))
        gate_s[at, :] = gate
        d = nt(cd[...].astype(BF16), wo[...])
        datt_s[at, :] = (d * gate).astype(BF16)

    ring = (right, left)
    step_of = (-1, 1)

    def rcopy(n, t, s, inward):
        back = t if inward else t - 1
        block = (row + NR + step_of[s] * back) % NR
        rows = pl.ds(0, RC) if t < 4 else pl.ds(s * (RC // 2), RC // 2)
        at = rslab.at[n, block, rows]
        return copy(at, at, ring_ss.at[n, s, t - 1], ring_rs.at[n, s, t - 1], row=ring[s])

    def product(n, j):
        for gg in range(2):
            tops, tail = [], None
            for q in range(3):
                k = gg * 3 + q
                o = nt(lm[6 * n + k], rslab[n, j, k * B : k * B + 128, :])
                tops.append(o[0:B])
                tail = o[B : 2 * B] if tail is None else tail + o[B : 2 * B]
            for q in range(3):
                k = gg * 3 + q
                packed = jnp.where(own, tops[q], pltpu.roll(tail, 96 - 32 * q, 1))
                part[n, j, k * B : k * B + B, :] = packed.astype(BF16)

    def products(n, back):
        if back in (0, 4):
            product(n, (row + back) % NR)
        else:

            def one(d, carry):
                product(n, (row + NR + (2 * d - 1) * back) % NR)
                return carry

            lax.fori_loop(0, 2, one, 0)

    def ycopy(n, d, x, inward):
        there = (yy + d) % 4
        j = x * 4 + there
        return copy(
            part.at[n, j], y_recv.at[n, d - 1, x], y_ss.at[n, d, x], y_rs.at[n, d, x],
            col=xh * 4 + there,
        )

    def y_sum(n):
        for d in range(1, 4):
            for x in range(2):
                ycopy(n, d, x, True).wait_recv()

        def one(k, carry):
            at = pl.ds(pl.multiple_of(k * B, B), B)

            def total(x):
                v = part[n, x * 4 + yy, at, :].astype(F32)
                for d in range(3):
                    v = v + y_recv[n, d, x, at, :].astype(F32)
                return v

            own_sum[n, at, :] = total(xh)
            x_send[n, at, :] = total(1 - xh).astype(BF16)
            return carry

        lax.fori_loop(0, 6, one, 0)

    def xcopy(n):
        return copy(x_send.at[n], x_recv.at[n], x_ss.at[n], x_rs.at[n], col=xp)

    def samp_copy(src_of, dst_of, ss, rs, d, inward):
        there, here = (samp + d) % NS, (samp + NS - d) % NS
        return copy(src_of(there), dst_of(here if inward else samp), ss.at[d], rs.at[d], samp=there)

    def tcopy(n, d, inward):
        return samp_copy(
            lambda m: tri_send.at[m, n], lambda m: tri_recv.at[m, n], t_ss.at[n], t_rs.at[n], d, inward
        )

    lane96 = lax.broadcasted_iota(jnp.int32, (B, 128), 1)

    def triangle(n):
        xcopy(n).wait_recv()
        found = []
        for gg in range(2):
            c = []
            for q in range(3):
                at = pl.ds((gg * 3 + q) * B, B)
                c.append(own_sum[n, at, :] + x_recv[n, at, :].astype(F32))
            tail = jnp.where(
                lane96 < 32,
                pltpu.roll(c[0], 32, 1),
                jnp.where(lane96 < 64, pltpu.roll(c[1], 64, 1), pltpu.roll(c[2], 96, 1)),
            )
            found.append(c + [tail])
        for q in range(4):
            for m in range(NS):
                both = jnp.concatenate([found[0][q][m * Q : m * Q + Q], found[1][q][m * Q : m * Q + Q]], axis=0)
                tri_send[m, n, q] = both.astype(BF16)
        for d in range(1, NS):
            tcopy(n, d, False).start()

    for k in range(2 * CH + 2):
        for n in range(CH):
            t = k - 2 * n + 1
            if 1 <= t <= 4:
                for s in range(2):
                    if t > 1:
                        rcopy(n, t - 1, s, True).wait_recv()
                    rcopy(n, t, s, False).start()
                products(n, t - 1)
            elif t == 5:
                for s in range(2):
                    rcopy(n, 4, s, True).wait_recv()
                products(n, 4)
                for d in range(1, 4):
                    for x in range(2):
                        ycopy(n, d, x, False).start()
            elif t == 7:
                y_sum(n)
                xcopy(n).start()
            elif t == 8:
                triangle(n)
        if k == 0:
            for _, inc in tok_copies + cot_copies:
                inc.wait_recv()
        if k < 4:
            token_step(k)

    def kvcopy(slab, ss, rs, d, inward):
        at = slab.at[(row + NR - d) % NR if inward else row]
        return copy(at, at, ss.at[d], rs.at[d], row=(row + d) % NR)

    for d in range(1, NR):
        kvcopy(kslab, k_ss, k_rs, d, False).start()
        kvcopy(vslab, v_ss, v_rs, d, False).start()

    n = CH - 1
    for s in range(2):
        rcopy(n, 4, s, True).wait_recv()
    products(n, 4)
    for d in range(1, 4):
        for x in range(2):
            ycopy(n, d, x, False).start()
    for n in range(CH - 2, CH):
        y_sum(n)
        xcopy(n).start()
    for n in range(CH - 2, CH):
        triangle(n)

    def unpack(m):
        for n in range(CH):
            for q in range(4):
                r0 = pl.multiple_of(m * 768, 768) + (q * 4 + n) * 48
                tri_f[pl.ds(r0, 48), :] = tri_recv[m, n, q].astype(F32)

    tri_recv[samp] = tri_send[samp]
    unpack(samp)
    for d in range(1, NS):
        for n in range(CH):
            tcopy(n, d, True).wait_recv()
        unpack((samp + NS - d) % NS)

    row0 = samp * Q

    def post_step(m, carry):
        ups = []
        for e in range(4):
            i = m * 4 + e
            t = jnp.concatenate(
                [tri_f[pl.ds(i, 64, stride=48), :], tri_f[pl.ds(Q + i, 64, stride=48), :]], axis=0
            )
            center = t - jnp.mean(t, axis=0, keepdims=True)
            t = center * lax.rsqrt(jnp.mean(center * center, axis=0, keepdims=True) + 1e-05)
            proj = tn(t.astype(BF16), w_op[...])[0:B]
            at = pl.ds(pl.multiple_of((row0 + i) * B, B), B)
            gate = jax.nn.sigmoid(nn(normed[at, :], w_outgate[...]))
            ups.append((pair[at, :].astype(F32) + gate * proj).astype(BF16))
        updated = jnp.concatenate(ups, axis=0)
        trans_in = normalize(updated, ones).astype(BF16)
        total = updated.astype(F32)
        for n in range(2):
            a = nn(trans_in, w_tg[:, n * 256 : n * 256 + 256])
            u = nn(trans_in, w_tu[:, n * 256 : n * 256 + 256])
            hidden = (a * jax.nn.sigmoid(a) * u).astype(BF16)
            total = total + nn(hidden, w_td[n * 256 : n * 256 + 256, :])
        out = total.astype(BF16)
        pair_out[pl.ds(pl.multiple_of((row0 + m * 4) * B, 4 * B), 4 * B), :] = out
        bias_in = (normalize(out, ones) * lnb[...]).astype(BF16)
        for e in range(4):
            hb_send[pl.ds(m * 4 + e, 16, stride=Q), 0:B] = nt(
                wpbt[...], bias_in[e * B : e * B + B]
            ).astype(BF16).astype(F32)
        return carry

    lax.fori_loop(0, Q // 4, post_step, 0)

    def hcopy(d, inward):
        there, here = (col + d) % NC, (col + NC - d) % NC
        src = hb_send.at[pl.ds(pl.multiple_of(there * 48, 48), 48)]
        return copy(src, hb.at[here if inward else col, samp], h_ss.at[d], h_rs.at[d], col=there)

    for d in range(1, NC):
        hcopy(d, False).start()
    hb[col, samp] = hb_send[pl.ds(pl.multiple_of(col * 48, 48), 48), :]
    for d in range(1, NC):
        hcopy(d, True).wait_recv()

    def hgcopy(d, inward):
        return samp_copy(lambda _: hb.at[:, samp], lambda n: hb.at[:, n], hg_ss, hg_rs, d, inward)

    def pocopy(d, inward):
        def rows_of(n):
            return pair_out.at[pl.ds(pl.multiple_of(n * (Q * B), Q * B), Q * B)]

        return samp_copy(lambda _: rows_of(samp), rows_of, po_ss, po_rs, d, inward)

    for d in range(1, NS):
        hgcopy(d, False).start()
    for d in range(1, NS):
        pocopy(d, False).start()
    for d in range(1, NR):
        kvcopy(kslab, k_ss, k_rs, d, True).wait_recv()
        kvcopy(vslab, v_ss, v_rs, d, True).wait_recv()
    for d in range(1, NS):
        hgcopy(d, True).wait_recv()

    for b in range(NC):
        key_mask = (crop_v[0:1, b * B : b * B + B].astype(F32) - 1.0) * 10000.0
        for h in range(2):
            whole = jnp.concatenate([hb[b, n, h * Q : h * Q + Q, 0:B] for n in range(NS)], axis=0)
            bias[b, h] = whole + key_mask
            acc[b, h] = jnp.zeros((B, 128), F32)
    feature = lax.broadcasted_iota(jnp.int32, (1, B), 1)
    head_masks = [(feature < 48).astype(F32), (feature >= 48).astype(F32)]
    scale = 1.0 / math.sqrt(48)

    def att_step(s, carry):
        at = pl.ds(pl.multiple_of(s * B, B), B)
        attended = jnp.zeros((B, B), F32)
        for h in range(2):
            mask = head_masks[h].astype(BF16)
            query = q_s[at, :] * mask
            datt = datt_s[at, :] * mask
            scores = [nt(query, kslab[b, at, :]) * scale + bias[b, h] for b in range(NR)]
            top = scores[0]
            for b in range(1, NR):
                top = jnp.maximum(top, scores[b])
            top = jnp.max(top, axis=-1, keepdims=True)
            shifted = [jnp.exp(v - top) for v in scores]
            total = shifted[0]
            for b in range(1, NR):
                total = total + shifted[b]
            inv = 1.0 / jnp.sum(total, axis=-1, keepdims=True)
            probs = [v * inv for v in shifted]
            got = nn(probs[0].astype(BF16), vslab[0, at, :])
            for b in range(1, NR):
                got = got + nn(probs[b].astype(BF16), vslab[b, at, :])
            got = got * head_masks[h]
            attended = attended + got
            delta = jnp.sum(datt.astype(F32) * got, axis=-1, keepdims=True)
            for b in range(NR):
                grad = probs[b] * (nt(datt, vslab[b, at, :]) - delta)
                acc[b, h, :, 0:B] = acc[b, h, :, 0:B] + grad
        gated = (gate_s[at, :] * attended).astype(BF16)
        xd[...] = nn(gated, wo[...])
        for b in range(NC):
            pj_send[b, at, :] = xd[:, b * B : b * B + B].astype(BF16)
        return carry

    lax.fori_loop(0, 4, att_step, 0)

    def gcopy(d, inward):
        def part(n):
            return acc.at[:, :, pl.ds(pl.multiple_of(n * Q, Q), Q), :]

        return samp_copy(part, lambda n: rs_recv.at[n], g_ss, g_rs, d, inward)

    for d in range(1, NS):
        gcopy(d, False).start()
    pj_copies = [col_all(lambda n: pj_send.at[n], pj_recv, pj_ss, pj_rs, d) for d in range(1, NC)]
    for out, _ in pj_copies:
        out.start()
    for d in range(1, NS):
        gcopy(d, True).wait_recv()

    others = [(samp + d) % NS for d in range(1, NS)]

    def sum_step(b, carry):
        for h in range(2):
            total = acc[b, h, pl.ds(pl.multiple_of(samp * Q, 8), Q), :]
            for n in others:
                total = total + rs_recv[n, b, h]
            sg[b, h * Q : h * Q + Q, :] = total
        return carry

    lax.fori_loop(0, NC, sum_step, 0)

    def ccopy(d, inward):
        there, here = (col + d) % NC, (col + NC - d) % NC
        at = here if inward else col
        dst = cg.at[pl.ds(pl.multiple_of(at * 48, 48), 48)]
        return copy(sg.at[there], dst, c_ss.at[d], c_rs.at[d], col=there)

    for d in range(1, NC):
        ccopy(d, False).start()
    cg[pl.ds(pl.multiple_of(col * 48, 48), 48), :] = sg[col]
    for d in range(1, NC):
        ccopy(d, True).wait_recv()

    for i in range(Q):
        bg[samp, i] = cg[pl.ds(i, 16, stride=Q), :]

    def bcopy(d, inward):
        return samp_copy(lambda _: bg.at[samp], lambda n: bg.at[n], b_ss, b_rs, d, inward)

    for d in range(1, NS):
        bcopy(d, False).start()

    for _, inc in pj_copies:
        inc.wait_recv()
    pj_recv[col] = pj_send[col]

    def out_step(s, carry):
        at = pl.ds(pl.multiple_of(s * B, B), B)
        total = pj_recv[0, at, :].astype(F32)
        for b in range(1, NC):
            total = total + pj_recv[b, at, :].astype(F32)
        tokens_out[at, :] = (tokens[at, :].astype(F32) + total).astype(BF16)
        return carry

    lax.fori_loop(0, 4, out_step, 0)
    for d in range(1, NS):
        pocopy(d, True).wait_recv()
    for d in range(1, NS):
        bcopy(d, True).wait_recv()

    for out, _ in tok_copies + cot_copies + pj_copies:
        out.wait_send()

    for n in range(CH):
        for s in range(2):
            for t in range(1, 5):
                rcopy(n, t, s, False).wait_send()
        for d in range(1, 4):
            for x in range(2):
                ycopy(n, d, x, False).wait_send()
            tcopy(n, d, False).wait_send()
        xcopy(n).wait_send()
    for d in range(1, NR):
        kvcopy(kslab, k_ss, k_rs, d, False).wait_send()
        kvcopy(vslab, v_ss, v_rs, d, False).wait_send()
    for d in range(1, NC):
        hcopy(d, False).wait_send()
        ccopy(d, False).wait_send()
    for d in range(1, NS):
        hgcopy(d, False).wait_send()
        pocopy(d, False).wait_send()
        gcopy(d, False).wait_send()
        bcopy(d, False).wait_send()


def split(v):
    high = v.astype(BF16)
    rest = v - high.astype(F32)
    mid = rest.astype(BF16)
    return high, mid, (rest - mid.astype(F32)).astype(BF16)


def finish(pair_rows, token_rows, bg, lnb, wpbt, pair_out, tokens_out, pair_grad):
    @pl.when(pl.program_id(0) == 0)
    def _():
        tokens_out[...] = token_rows[...]

    pair_out[...] = pair_rows[...]
    ones = mean_weights()
    weights = wpbt[...].astype(F32) * lnb[...]
    weights = weights - jnp.mean(weights, axis=-1, keepdims=True)
    high, mid, low = split(weights)
    weights = jnp.concatenate([high, mid, high, mid, low, high], axis=0)
    for e in range(8):
        high, mid, low = split(bg[e])
        scaled = tn(jnp.concatenate([high, high, mid, mid, high, low], axis=0), weights)[0:B]
        center, inv = centered(pair_rows[e * B : e * B + B, :], ones)
        unit = center * inv
        pair_grad[e * B : e * B + B, :] = inv * (scaled - unit * row_means(scaled * unit, ones))


def per_device(
    pair, crop_mask, w_agate, w_aval, w_bgate, w_bval, w_outgate, w_outproj, ln_pair,
    w_trans_gate, w_trans_up, w_trans_down, ln_bias, w_pairbias, tokens, ln_token,
    w_query, w_key, w_value, w_gate, w_output, cotangent,
):
    wpbt = w_pairbias.T
    lnb = ln_bias.reshape(1, 128)
    args = (
        pair.reshape(B * B, 128), crop_mask, crop_mask.reshape(1, NC * B),
        w_agate, w_aval, w_bgate, w_bval, ln_pair.reshape(1, 128), w_outgate, w_outproj,
        w_trans_gate, w_trans_up, w_trans_down, lnb, wpbt,
        tokens.reshape(4 * B, B), cotangent.reshape(4 * B, B), ln_token.reshape(1, NC * B),
        w_query.T, w_key.T, w_value.T, w_gate.T, w_output,
    )
    vm = pltpu.VMEM
    dma = pltpu.SemaphoreType.DMA
    scratch = [
        vm((4, 128, 128), BF16),
        vm((128, 128), BF16),
        vm((B, NC * B), F32),
        vm((B, NC * B), F32),
        vm((B * B + 32, 128), BF16),
        vm((G * B, 128), F32),
        vm((G * B, 128), F32),
        vm((G, 2 * B, 128), BF16),
        vm((CH, NR, RC + 32, 128), BF16),
        vm((CH, NR, RC, 128), BF16),
        vm((CH, 3, 2, RC, 128), BF16),
        vm((CH, RC, 128), F32),
        vm((CH, RC, 128), BF16),
        vm((CH, RC, 128), BF16),
        vm((NC, 4 * B, B), BF16),
        vm((NC, 4 * B, B), BF16),
        vm((4 * B, B), BF16),
        vm((NR, 4 * B, B), BF16),
        vm((NR, 4 * B, B), BF16),
        vm((4 * B, B), F32),
        vm((4 * B, B), BF16),
        vm((NS, CH, 4, 48, 128), BF16),
        vm((NS, CH, 4, 48, 128), BF16),
        vm((64 * 48, 128), F32),
        vm((16 * Q, 128), F32),
        vm((NC, NS, 48, 128), F32),
        vm((NC, 2, B, B), F32),
        vm((NC, 2, B, 128), F32),
        vm((NC, 4 * B, B), BF16),
        vm((NC, 4 * B, B), BF16),
        vm((NS, NC, 2, Q, 128), F32),
        vm((NC, 48, 128), F32),
        vm((16 * Q, 128), F32),
    ]
    sems = [(8,)] * 4 + [(CH, 2, 4)] * 2 + [(CH, 4, 2)] * 2 + [(CH,)] * 2
    sems += [(8,)] * 4 + [(CH, 4)] * 2 + [(8,)] * 2 + [(4,)] * 4 + [(8,)] * 2 + [(4,)] * 2 + [(8,)] * 2
    sems += [(4,)] * 2
    scratch += [dma(s) for s in sems]
    spec = pl.BlockSpec(memory_space=pltpu.VMEM)
    specs = [spec] * len(args)
    specs[1] = pl.BlockSpec(memory_space=pltpu.SMEM)
    pair_rows, token_rows, bg = pl.pallas_call(
        kernel,
        out_shape=(
            jax.ShapeDtypeStruct((B * B, 128), BF16),
            jax.ShapeDtypeStruct((4 * B, B), BF16),
            jax.ShapeDtypeStruct((NS, Q, 16, 128), F32),
        ),
        in_specs=specs,
        out_specs=(spec,) * 3,
        scratch_shapes=scratch,
        compiler_params=pltpu.CompilerParams(
            collective_id=0, has_side_effects=True, vmem_limit_bytes=56 * 1024 * 1024
        ),
    )(*args)
    rows = pl.BlockSpec((8 * B, 128), lambda i: (i, 0))
    whole = pl.BlockSpec((4 * B, B), lambda i: (0, 0))
    outs = pl.pallas_call(
        finish,
        grid=(B // 8,),
        out_shape=(
            jax.ShapeDtypeStruct((B * B, 128), BF16),
            jax.ShapeDtypeStruct((4 * B, B), BF16),
            jax.ShapeDtypeStruct((B * B, 128), F32),
        ),
        in_specs=[
            rows,
            whole,
            pl.BlockSpec((8, 16, 128), lambda i: (i, 0, 0)),
            pl.BlockSpec((1, 128), lambda i: (0, 0)),
            pl.BlockSpec((16, 128), lambda i: (0, 0)),
        ],
        out_specs=(rows, whole, rows),
    )(pair_rows, token_rows, bg.reshape(B, 16, 128), lnb, wpbt)
    return (
        outs[0].reshape(B, B, 128),
        outs[1].reshape(4, B, B),
        outs[2].reshape(B, B, 128),
    )


def solution(mesh):
    placed = (
        P("row", "col", None),
        P(), P(), P(), P(), P(), P(), P(), P(), P(), P(), P(), P(), P(),
        P("samp", "row", "col"),
        P(),
        P(None, "col"),
        P(None, "col"),
        P(None, "col"),
        P(None, "col"),
        P("col", None),
        P("samp", "row", "col"),
    )
    return jax.shard_map(
        per_device,
        mesh=mesh,
        in_specs=placed,
        out_specs=(P("row", "col", None), P("samp", "row", "col"), P("row", "col", None)),
        check_vma=False,
    )
```

```python
import math

import jax
import jax.numpy as jnp
from jax import lax
from jax.experimental import pallas as pl
from jax.experimental.pallas import tpu as pltpu
from jax.sharding import PartitionSpec as P

F32 = jnp.float32
BF16 = jnp.bfloat16
MESH = pl.DeviceIdType.MESH
NR = 8
NC = 8
NS = 4
B = 96
Q = 24
G = 24
CH = 8
RC = 3 * B


def nt(a, b):
    return lax.dot_general(a, b, (((1,), (1,)), ((), ())), preferred_element_type=F32)


def nn(a, b):
    return lax.dot_general(a, b, (((1,), (0,)), ((), ())), preferred_element_type=F32)


def tn(a, b):
    return lax.dot_general(a, b, (((0,), (0,)), ((), ())), preferred_element_type=F32)


def row_means(values, ones):
    high = values.astype(BF16)
    low = (values - high.astype(F32)).astype(BF16)
    return nn(jnp.concatenate([high, low], axis=1), ones)


def centered(values, ones):
    center = values.astype(F32) - nn(values, ones[0:128])
    return center, lax.rsqrt(row_means(center * center, ones) + 1e-05)


def normalize(values, ones):
    center, inv = centered(values, ones)
    return center * inv


def mean_weights():
    return jnp.full((256, 128), 1.0 / 128.0, BF16)


def kernel(
    pair, crop_s, crop_v, w_ag, w_av, w_bg, w_bv, lnp, w_outgate, w_outproj, w_tg, w_tu, w_td,
    lnb, wpbt, tokens, cot, lnt, wq, wk, wv, wg, wo,
    pair_out, tokens_out, bg,
    wt, w_op, xd, cd,
    normed, lf, rf, lm, rslab, part, z_recv, y_recv, own_sum, x_send, x_recv, slab, q_s, kslab,
    vslab, gate_s, datt_s, tri_send, tri_recv, tri_f, hb_f, hb_send, hb, bias, acc, g_send, g_recv,
    pj_send, py_recv, px_own, px_send, px_recv, sg, cg, cg_f,
    slab_ss, slab_rs, ring_ss, ring_rs, z_ss, z_rs, y_ss, y_rs, x_ss, x_rs,
    k_ss, k_rs, v_ss, v_rs, t_ss, t_rs, h_ss, h_rs, hg_ss, hg_rs, po_ss, po_rs, pr_ss, pr_rs,
    py_ss, py_rs, px_ss, px_rs, g_ss, g_rs, c_ss, c_rs, b_ss, b_rs,
):
    row = lax.axis_index("row")
    col = lax.axis_index("col")
    samp = lax.axis_index("samp")
    xh = col // 4
    yy = col % 4
    xp = (1 - xh) * 4 + yy
    ones = mean_weights()
    right = (row + 1) % NR
    left = (row + NR - 1) % NR

    def copy(src, dst, ss, rs, **where):
        return pltpu.make_async_remote_copy(
            src_ref=src, dst_ref=dst, send_sem=ss, recv_sem=rs, device_id=where, device_id_type=MESH
        )

    barrier = pltpu.get_barrier_semaphore()
    for d in range(1, NC):
        pl.semaphore_signal(barrier, inc=1, device_id={"col": (col + d) % NC}, device_id_type=MESH)
    for d in range(1, NR):
        pl.semaphore_signal(barrier, inc=1, device_id={"row": (row + d) % NR}, device_id_type=MESH)
    for d in range(1, NS):
        pl.semaphore_signal(
            barrier, inc=1, device_id={"samp": (samp + d) % NS}, device_id_type=MESH
        )

    pl.semaphore_wait(barrier, NC + NR + NS - 3)

    def around(d):
        return (yy + d) % 4

    def slab_copy(block, k, there):
        at = slab.at[block]
        return copy(at, at, slab_ss.at[k], slab_rs.at[k], col=there)

    slab_own = [slab_copy(col, d, xh * 4 + around(d)) for d in range(1, 4)]
    slab_own_in = [slab_copy(xh * 4 + around(4 - d), d, xh * 4 + around(d)) for d in range(1, 4)]
    slab_x = slab_copy(col, 0, xp)
    slab_x_in = slab_copy(xp, 0, xp)
    slab_on = [slab_copy(xp, 3 + d, xh * 4 + around(d)) for d in range(1, 4)]
    slab_on_in = [
        slab_copy((1 - xh) * 4 + around(4 - d), 3 + d, xh * 4 + around(d)) for d in range(1, 4)
    ]
    slab[col, 0] = tokens[...]
    slab[col, 1] = cot[...]
    for c in [slab_x] + slab_own:
        c.start()

    for n, w in enumerate((w_ag, w_av, w_bg, w_bv)):
        wt[n] = w[...].astype(F32).T.astype(BF16)
    wp = jnp.concatenate([wt[n, pl.ds(pl.multiple_of(samp * 32, 32), 32), :] for n in range(4)], axis=0)
    tri_f[0:128, :] = w_outproj[...].astype(F32)
    w_op[...] = jnp.concatenate(
        [tri_f[pl.ds(0, 64, stride=2), :], tri_f[pl.ds(1, 64, stride=2), :]], axis=0
    ).astype(BF16)
    keep_cols = jnp.zeros((1, B), F32)
    for b in range(NC):
        here = crop_v[0:1, b * B : b * B + B].astype(F32)
        keep_cols = jnp.where(col == b, here, keep_cols)
    keep_cols = jnp.concatenate([keep_cols, jnp.zeros((1, 32), F32)], axis=1)

    def norm_step(m, carry):
        for e in range(4):
            at = pl.ds(pl.multiple_of(m * 1536 + e * 384, 384), 384)
            normed[at, :] = (normalize(pair[at, :], ones) * lnp[...]).astype(BF16)
        return carry

    lax.fori_loop(0, 6, norm_step, 0)
    slab_x_in.wait_recv()
    for c in slab_on:
        c.start()
    normed[B * B : B * B + 32, :] = jnp.zeros((32, 128), BF16)
    lane = lax.broadcasted_iota(jnp.int32, (8, 128), 1)
    wide = lane < B

    def edges(weights, dest):
        def step(m, carry):
            for e in range(8):
                i = m * 8 + e
                rows = normed[pl.ds(pl.multiple_of(i * B, 32), 128), :]
                o = nt(weights, rows)
                kept = keep_cols * crop_s[row * B + i].astype(F32)
                edge = jax.nn.sigmoid(o[0:32]) * o[32:64] * kept
                tail = edge[24:32]
                for q in range(3):
                    packed = jnp.where(
                        wide, edge[8 * q : 8 * q + 8], pltpu.roll(tail, 96 - 32 * q, 1)
                    )
                    dest[pl.ds(i + 8 * B * q, 8, stride=B), :] = packed
            return carry

        lax.fori_loop(0, B // 8, step, 0)

    edges(wp[64:128], rf)
    own = lax.broadcasted_iota(jnp.int32, (B, 128), 1) < B
    carriers = [(n, k, pl.ds((k * 8 + n) * B, B)) for n in range(CH) for k in range(3)]
    for n, k, at in carriers:
        rslab[n, row, k * B : k * B + B, :] = rf[at, :].astype(BF16)
    for n in range(CH):
        rslab[n, :, RC : RC + 32, :] = jnp.zeros((NR, 32, 128), BF16)

    ring = (right, left)
    step_of = (-1, 1)

    def rcopy(n, t, s, inward):
        back = t if inward else t - 1
        block = (row + NR + step_of[s] * back) % NR
        rows = pl.ds(0, RC) if t < 4 else pl.ds(s * (RC // 2), RC // 2)
        at = rslab.at[n, block, rows]
        return copy(at, at, ring_ss.at[n, s, t - 1], ring_rs.at[n, s, t - 1], row=ring[s])

    for n in range(3):
        for s in range(2):
            rcopy(n, 1, s, False).start()
    edges(wp[0:64], lf)
    for n, k, at in carriers:
        edge = lf[at, :]
        lm[3 * n + k, 0:B, :] = jnp.where(own, edge, 0.0).astype(BF16)
        lm[3 * n + k, B : 2 * B, :] = jnp.where(own, 0.0, edge).astype(BF16)

    def token_step(pair_of):
        at = pl.ds(pair_of * 2 * B, 2 * B)
        x = [slab[b, 0, at, :].astype(F32) for b in range(NC)]
        total = x[0]
        for b in range(1, NC):
            total = total + x[b]
        mean = jnp.sum(total, axis=-1, keepdims=True) * (1.0 / (NC * B))
        x = [v - mean for v in x]
        total = x[0] * x[0]
        for b in range(1, NC):
            total = total + x[b] * x[b]
        inv = lax.rsqrt(jnp.sum(total, axis=-1, keepdims=True) * (1.0 / (NC * B)) + 1e-05)
        for b in range(NC):
            xd[:, b * B : b * B + B] = x[b] * inv
            cd[:, b * B : b * B + B] = slab[b, 1, at, :].astype(F32)
        normal = (xd[...] * lnt[...]).astype(BF16)
        q_s[at, :] = nt(normal, wq[...]).astype(BF16)
        tokens_at = pl.ds(pl.multiple_of(row * B, B), B)
        for w, dest in ((wk, kslab), (wv, vslab)):
            out = nt(normal, w[...]).astype(BF16)
            for e in range(2):
                dest[pair_of * 2 + e, tokens_at, :] = out[e * B : e * B + B]
        gate = jax.nn.sigmoid(nt(normal, wg[...]))
        gate_s[at, :] = gate
        d = nt(cd[...].astype(BF16), wo[...])
        datt_s[at, :] = (d * gate).astype(BF16)

    def product(n, j):
        tops, tail = [], None
        for q in range(3):
            o = nt(lm[3 * n + q], rslab[n, j, q * B : q * B + 128, :])
            tops.append(o[0:B])
            tail = o[B : 2 * B] if tail is None else tail + o[B : 2 * B]
        for q in range(3):
            packed = jnp.where(own, tops[q], pltpu.roll(tail, 96 - 32 * q, 1))
            part[n, j, q * B : q * B + B, :] = packed.astype(BF16)

    def products(n, back):
        if back in (0, 4):
            product(n, (row + back) % NR)
        else:

            def one(d, carry):
                product(n, (row + NR + (2 * d - 1) * back) % NR)
                return carry

            lax.fori_loop(0, 2, one, 0)

    sides = (xh * 4 + (yy + 1) % 4, xh * 4 + (yy + 3) % 4)

    def zcopy(n, s, x):
        src = part.at[n, x * 4 + (yy + 2) % 4, pl.ds(s * (RC // 2), RC // 2)]
        return copy(src, z_recv.at[n, s, x], z_ss.at[n, s, x], z_rs.at[n, s, x], col=sides[s])

    def ycopy(n, s, x):
        src = part.at[n, x * 4 + (yy + 1 + 2 * s) % 4]
        return copy(src, y_recv.at[n, s, x], y_ss.at[n, s, x], y_rs.at[n, s, x], col=sides[s])

    each = [(s, x) for s in range(2) for x in range(2)]

    def z_start(n):
        for s, x in each:
            zcopy(n, s, x).start()

    def y_start(n):
        for s, x in each:
            zcopy(n, s, x).wait_recv()
            j = x * 4 + (yy + 1 + 2 * s) % 4
            at = pl.ds(s * (RC // 2), RC // 2)
            more = z_recv[n, s, x].astype(F32)
            part[n, j, at, :] = (part[n, j, at, :].astype(F32) + more).astype(BF16)
            ycopy(n, s, x).start()

    def y_sum(n):
        for s, x in each:
            ycopy(n, s, x).wait_recv()

        def one(k, carry):
            at = pl.ds(pl.multiple_of(k * B, B), B)

            def total(x):
                v = part[n, x * 4 + yy, at, :].astype(F32)
                for s in range(2):
                    v = v + y_recv[n, s, x, at, :].astype(F32)
                return v

            own_sum[n, at, :] = total(xh)
            x_send[n, at, :] = total(1 - xh).astype(BF16)
            return carry

        lax.fori_loop(0, 3, one, 0)
        xcopy(n).start()

    def xcopy(n):
        return copy(x_send.at[n], x_recv.at[n], x_ss.at[n], x_rs.at[n], col=xp)

    def samp_copy(src_of, dst_of, ss, rs, d, inward):
        there, here = (samp + d) % NS, (samp + NS - d) % NS
        return copy(src_of(there), dst_of(here if inward else samp), ss.at[d], rs.at[d], samp=there)

    def tcopy(n, d, inward):
        return samp_copy(
            lambda m: tri_send.at[m, n], lambda m: tri_recv.at[m, n], t_ss.at[n], t_rs.at[n], d, inward
        )

    lane96 = lax.broadcasted_iota(jnp.int32, (B, 128), 1)

    def triangle(n):
        xcopy(n).wait_recv()
        c = []
        for q in range(3):
            at = pl.ds(q * B, B)
            c.append(own_sum[n, at, :] + x_recv[n, at, :].astype(F32))
        tail = jnp.where(
            lane96 < 32,
            pltpu.roll(c[0], 32, 1),
            jnp.where(lane96 < 64, pltpu.roll(c[1], 64, 1), pltpu.roll(c[2], 96, 1)),
        )
        c.append(tail)
        for h in range(2):
            for m in range(NS):
                both = [v[m * Q : m * Q + Q] for v in c[2 * h : 2 * h + 2]]
                tri_send[m, n, h] = jnp.concatenate(both, axis=0).astype(BF16)
        for d in range(1, NS):
            tcopy(n, d, False).start()

    def kvcopy(slab, ss, rs, d, inward):
        block = (row + NR - d) % NR if inward else row
        at = slab.at[:, pl.ds(pl.multiple_of(block * B, B), B), :]
        return copy(at, at, ss.at[d], rs.at[d], row=(row + d) % NR)

    for k in range(CH + 7):
        active = [(n, k - n + 1) for n in range(CH)]
        for n, t in active:
            if 1 <= t <= 5:
                for s in range(2):
                    if t > 1:
                        rcopy(n, t - 1, s, True).wait_recv()
                    if t < 5 and not (t == 1 and n < 3):
                        rcopy(n, t, s, False).start()
        if k == CH + 2:
            for d in range(1, NR):
                kvcopy(kslab, k_ss, k_rs, d, False).start()
                kvcopy(vslab, v_ss, v_rs, d, False).start()
        for n, t in active:
            if t == 5:
                products(n, 4)
                z_start(n)
            elif t == 6:
                y_start(n)
            elif t == 7:
                y_sum(n)
            elif t == 8:
                triangle(n)
        for n, t in active:
            if 1 <= t <= 4:
                products(n, t - 1)
        if k == 1:
            for c in slab_own_in + slab_on_in:
                c.wait_recv()
        if k in (1, 3):
            token_step(k // 2)

    def unpack(m):
        for n in range(CH):
            for h in range(2):
                both = tri_recv[m, n, h].astype(F32)
                for e in range(2):
                    c = (2 * h + e) * 8 + n
                    r0 = pl.multiple_of(m * 768, 768) + c // 2 * 48 + c % 2 * Q
                    tri_f[pl.ds(r0, Q), :] = both[e * Q : e * Q + Q]

    tri_recv[samp] = tri_send[samp]
    unpack(samp)
    for d in range(1, NS):
        for n in range(CH):
            tcopy(n, d, True).wait_recv()
        unpack((samp + NS - d) % NS)

    row0 = samp * Q
    sib, oth = samp + 1 - 2 * (samp % 2), (samp + 2) % NS
    diag = (sib + 2) % NS

    def part_of(n, m):
        return pair_out.at[pl.ds(pl.multiple_of((n * Q + m * 4) * B, 4 * B), 4 * B)]

    def pocopy(k, m, inward):
        there = (sib, oth)[k]
        at = part_of(there if inward else samp, m)
        return copy(at, at, po_ss.at[k, m], po_rs.at[k, m], samp=there)

    def prcopy(inward):
        n = diag if inward else oth
        at = pair_out.at[pl.ds(pl.multiple_of(n * (Q * B), Q * B), Q * B)]
        return copy(at, at, pr_ss, pr_rs, samp=sib)


    def post_step(m, carry):
        cols = []
        for e in range(4):
            i = m * 4 + e
            cols.append(
                jnp.concatenate(
                    [tri_f[pl.ds(i, 64, stride=48), :], tri_f[pl.ds(Q + i, 64, stride=48), :]], axis=0
                )
            )
        t = jnp.concatenate(cols, axis=1)
        center = t - jnp.mean(t, axis=0, keepdims=True)
        t = center * lax.rsqrt(jnp.mean(center * center, axis=0, keepdims=True) + 1e-05)
        proj = tn(t.astype(BF16), w_op[...])
        proj = jnp.concatenate([proj[e * 128 : e * 128 + B] for e in range(4)], axis=0)
        at = pl.ds(pl.multiple_of((row0 + m * 4) * B, 4 * B), 4 * B)
        gate = jax.nn.sigmoid(nn(normed[at, :], w_outgate[...]))
        updated = (pair[at, :].astype(F32) + gate * proj).astype(BF16)
        trans_in = normalize(updated, ones).astype(BF16)
        total = updated.astype(F32)
        for n in range(2):
            a = nn(trans_in, w_tg[:, n * 256 : n * 256 + 256])
            u = nn(trans_in, w_tu[:, n * 256 : n * 256 + 256])
            hidden = (a * jax.nn.sigmoid(a) * u).astype(BF16)
            total = total + nn(hidden, w_td[n * 256 : n * 256 + 256, :])
        out = total.astype(BF16)
        pair_out[at, :] = out
        for k in range(2):
            pocopy(k, m, False).start()
        bias_in = (normalize(out, ones) * lnb[...]).astype(BF16)
        o = nt(wpbt[...], bias_in)
        for e in range(4):
            hb_f[pl.ds(m * 4 + e, 16, stride=Q), 0:B] = o[:, e * B : e * B + B]
        return carry

    lax.fori_loop(0, Q // 4, post_step, 0)

    for c in range(NC):
        hb_send[c] = hb_f[c * 48 : c * 48 + 48, :].astype(BF16)

    def hcopy(d, inward):
        there, here = (col + d) % NC, (col + NC - d) % NC
        dst = hb.at[here if inward else col, samp]
        return copy(hb_send.at[there], dst, h_ss.at[d], h_rs.at[d], col=there)

    for d in range(1, NC):
        hcopy(d, False).start()
    hb[col, samp] = hb_send[col]
    for d in range(1, NC):
        hcopy(d, True).wait_recv()

    def hgcopy(d, inward):
        return samp_copy(lambda _: hb.at[:, samp], lambda n: hb.at[:, n], hg_ss, hg_rs, d, inward)

    for d in range(1, NS):
        hgcopy(d, False).start()
    for d in range(1, NR):
        kvcopy(kslab, k_ss, k_rs, d, True).wait_recv()
        kvcopy(vslab, v_ss, v_rs, d, True).wait_recv()
    for d in range(1, NS):
        hgcopy(d, True).wait_recv()

    for b in range(NC):
        key_mask = (crop_v[0:1, b * B : b * B + B].astype(F32) - 1.0) * 10000.0
        quarters = [hb[b, n].astype(F32) for n in range(NS)]
        for h in range(2):
            whole = jnp.concatenate([v[h * Q : h * Q + Q, 0:B] for v in quarters], axis=0)
            bias[h * B : h * B + B, b * B : b * B + B] = whole + key_mask
    acc[...] = jnp.zeros((2 * B, NC * B), F32)
    feature = lax.broadcasted_iota(jnp.int32, (1, B), 1)
    head_masks = [(feature < 48).astype(F32), (feature >= 48).astype(F32)]
    scale = 1.0 / math.sqrt(48)

    def att_step(s, carry):
        at = pl.ds(pl.multiple_of(s * B, B), B)
        query, datt = q_s[at, :], datt_s[at, :]
        query = jnp.concatenate([query * m.astype(BF16) for m in head_masks], axis=0)
        datt = jnp.concatenate([datt * m.astype(BF16) for m in head_masks], axis=0)
        scores = nt(query, kslab[s]) * scale + bias[...]
        shifted = jnp.exp(scores - jnp.max(scores, axis=-1, keepdims=True))
        probs = shifted * (1.0 / jnp.sum(shifted, axis=-1, keepdims=True))
        got = nn(probs.astype(BF16), vslab[s])
        delta = jnp.sum(datt.astype(F32) * got, axis=-1, keepdims=True)
        acc[...] = acc[...] + probs * (nt(datt, vslab[s]) - delta)
        attended = got[0:B] * head_masks[0] + got[B : 2 * B] * head_masks[1]
        gated = (gate_s[at, :] * attended).astype(BF16)
        xd[0:B, :] = nn(gated, wo[...])
        for b in range(NC):
            pj_send[b, at, :] = xd[0:B, b * B : b * B + B].astype(BF16)
        return carry

    lax.fori_loop(0, 4, att_step, 0)
    for m in range(6):
        pocopy(1, m, True).wait_recv()
    prcopy(False).start()

    for b in range(NC):
        heads = [acc[h * B : h * B + B, b * B : b * B + B] for h in range(2)]
        for n in range(NS):
            both = jnp.concatenate([v[n * Q : n * Q + Q] for v in heads], axis=0)
            g_send[n, b, :, 0:B] = both.astype(BF16)

    def gcopy(d, inward):
        return samp_copy(lambda n: g_send.at[n], lambda n: g_recv.at[n], g_ss, g_rs, d, inward)

    for d in range(1, NS):
        gcopy(d, False).start()

    def pycopy(d, x):
        src = pj_send.at[x * 4 + around(d)]
        return copy(src, py_recv.at[d - 1, x], py_ss.at[d, x], py_rs.at[d, x], col=xh * 4 + around(d))

    pys = [(d, x) for d in range(1, 4) for x in range(2)]
    for d, x in pys:
        pycopy(d, x).start()
    g_recv[samp] = g_send[samp]
    for d in range(1, NS):
        gcopy(d, True).wait_recv()

    def sum_step(b, carry):
        total = g_recv[0, b].astype(F32)
        for n in range(1, NS):
            total = total + g_recv[n, b].astype(F32)
        sg[b] = total.astype(BF16)
        return carry

    lax.fori_loop(0, NC, sum_step, 0)

    def ccopy(d, inward):
        there, here = (col + d) % NC, (col + NC - d) % NC
        return copy(sg.at[there], cg.at[here if inward else col], c_ss.at[d], c_rs.at[d], col=there)

    for d in range(1, NC):
        ccopy(d, False).start()
    cg[col] = sg[col]

    for d, x in pys:
        pycopy(d, x).wait_recv()

    def py_step(s, carry):
        at = pl.ds(pl.multiple_of(s * B, B), B)

        def total(x):
            v = pj_send[x * 4 + yy, at, :].astype(F32)
            for d in range(3):
                v = v + py_recv[d, x, at, :].astype(F32)
            return v

        px_own[at, :] = total(xh) + tokens[at, :].astype(F32)
        px_send[at, :] = total(1 - xh).astype(BF16)
        return carry

    lax.fori_loop(0, 4, py_step, 0)
    px = copy(px_send, px_recv, px_ss, px_rs, col=xp)
    px.start()
    for d in range(1, NC):
        ccopy(d, True).wait_recv()
    for c in range(NC):
        cg_f[c * 48 : c * 48 + 48, :] = cg[c].astype(F32)
    for i in range(Q):
        bg[samp, i] = cg_f[pl.ds(i, 16, stride=Q), :].astype(BF16)

    def bcopy(d, inward):
        return samp_copy(lambda _: bg.at[samp], lambda n: bg.at[n], b_ss, b_rs, d, inward)

    for d in range(1, NS):
        bcopy(d, False).start()
    px.wait_recv()
    tokens_out[...] = (px_own[...] + px_recv[...].astype(F32)).astype(BF16)
    for m in range(6):
        pocopy(0, m, True).wait_recv()
    prcopy(True).wait_recv()
    for d in range(1, NS):
        bcopy(d, True).wait_recv()

    for c in [slab_x, px, prcopy(False)] + slab_own + slab_on:
        c.wait_send()
    for d, x in pys:
        pycopy(d, x).wait_send()
    for m in range(6):
        for k in range(2):
            pocopy(k, m, False).wait_send()

    for n in range(CH):
        for s in range(2):
            for t in range(1, 5):
                rcopy(n, t, s, False).wait_send()
        for s, x in each:
            zcopy(n, s, x).wait_send()
            ycopy(n, s, x).wait_send()
        for d in range(1, NS):
            tcopy(n, d, False).wait_send()
        xcopy(n).wait_send()
    for d in range(1, NR):
        kvcopy(kslab, k_ss, k_rs, d, False).wait_send()
        kvcopy(vslab, v_ss, v_rs, d, False).wait_send()
    for d in range(1, NC):
        hcopy(d, False).wait_send()
        ccopy(d, False).wait_send()
    for d in range(1, NS):
        hgcopy(d, False).wait_send()
        gcopy(d, False).wait_send()
        bcopy(d, False).wait_send()


def split(v):
    high = v.astype(BF16)
    rest = v - high.astype(F32)
    mid = rest.astype(BF16)
    return high, mid, (rest - mid.astype(F32)).astype(BF16)


def finish(pair_rows, token_rows, bg, lnb, wpbt, pair_out, tokens_out, pair_grad):
    @pl.when(pl.program_id(0) == 0)
    def _():
        tokens_out[...] = token_rows[...]

    pair_out[...] = pair_rows[...]
    ones = mean_weights()
    weights = wpbt[...].astype(F32) * lnb[...]
    weights = weights - jnp.mean(weights, axis=-1, keepdims=True)
    weights = jnp.concatenate(split(weights), axis=0)
    for e in range(2):
        at = slice(e * 4 * B, e * 4 * B + 4 * B)
        grads = jnp.concatenate([bg[e * 4 + i] for i in range(4)], axis=1)
        scaled = tn(jnp.concatenate([grads, grads, grads], axis=0), weights)
        scaled = jnp.concatenate([scaled[i * 128 : i * 128 + B] for i in range(4)], axis=0)
        center, inv = centered(pair_rows[at, :], ones)
        unit = center * inv
        pair_grad[at, :] = inv * (scaled - unit * row_means(scaled * unit, ones))


def per_device(
    pair, crop_mask, w_agate, w_aval, w_bgate, w_bval, w_outgate, w_outproj, ln_pair,
    w_trans_gate, w_trans_up, w_trans_down, ln_bias, w_pairbias, tokens, ln_token,
    w_query, w_key, w_value, w_gate, w_output, cotangent,
):
    wpbt = w_pairbias.T
    lnb = ln_bias.reshape(1, 128)
    args = (
        pair.reshape(B * B, 128), crop_mask, crop_mask.reshape(1, NC * B),
        w_agate, w_aval, w_bgate, w_bval, ln_pair.reshape(1, 128), w_outgate, w_outproj,
        w_trans_gate, w_trans_up, w_trans_down, lnb, wpbt,
        tokens.reshape(4 * B, B), cotangent.reshape(4 * B, B), ln_token.reshape(1, NC * B),
        w_query.T, w_key.T, w_value.T, w_gate.T, w_output,
    )
    vm = pltpu.VMEM
    dma = pltpu.SemaphoreType.DMA
    scratch = [
        vm((4, 128, 128), BF16),
        vm((128, 128), BF16),
        vm((2 * B, NC * B), F32),
        vm((2 * B, NC * B), F32),
        vm((B * B + 32, 128), BF16),
        vm((G * B, 128), F32),
        vm((G * B, 128), F32),
        vm((G, 2 * B, 128), BF16),
        vm((CH, NR, RC + 32, 128), BF16),
        vm((CH, NR, RC, 128), BF16),
        vm((CH, 2, 2, RC // 2, 128), BF16),
        vm((CH, 2, 2, RC, 128), BF16),
        vm((CH, RC, 128), F32),
        vm((CH, RC, 128), BF16),
        vm((CH, RC, 128), BF16),
        vm((NC, 2, 4 * B, B), BF16),
        vm((4 * B, B), BF16),
        vm((4, NR * B, B), BF16),
        vm((4, NR * B, B), BF16),
        vm((4 * B, B), F32),
        vm((4 * B, B), BF16),
        vm((NS, CH, 2, 48, 128), BF16),
        vm((NS, CH, 2, 48, 128), BF16),
        vm((64 * 48, 128), F32),
        vm((16 * Q, 128), F32),
        vm((NC, 48, 128), BF16),
        vm((NC, NS, 48, 128), BF16),
        vm((2 * B, NC * B), F32),
        vm((2 * B, NC * B), F32),
        vm((NS, NC, 48, 128), BF16),
        vm((NS, NC, 48, 128), BF16),
        vm((NC, 4 * B, B), BF16),
        vm((3, 2, 4 * B, B), BF16),
        vm((4 * B, B), F32),
        vm((4 * B, B), BF16),
        vm((4 * B, B), BF16),
        vm((NC, 48, 128), BF16),
        vm((NC, 48, 128), BF16),
        vm((16 * Q, 128), F32),
    ]
    sems = [(7,)] * 2 + [(CH, 2, 4)] * 2 + [(CH, 2, 2)] * 4 + [(CH,)] * 2
    sems += [(8,)] * 4 + [(CH, 4)] * 2 + [(8,)] * 2 + [(4,)] * 2 + [(2, 6)] * 2 + [None] * 2
    sems += [(4, 2)] * 2 + [None] * 2 + [(4,)] * 2 + [(8,)] * 2 + [(4,)] * 2
    scratch += [dma if s is None else dma(s) for s in sems]
    spec = pl.BlockSpec(memory_space=pltpu.VMEM)
    specs = [spec] * len(args)
    specs[1] = pl.BlockSpec(memory_space=pltpu.SMEM)
    pair_rows, token_rows, bg = pl.pallas_call(
        kernel,
        out_shape=(
            jax.ShapeDtypeStruct((B * B, 128), BF16),
            jax.ShapeDtypeStruct((4 * B, B), BF16),
            jax.ShapeDtypeStruct((NS, Q, 16, 128), BF16),
        ),
        in_specs=specs,
        out_specs=(spec,) * 3,
        scratch_shapes=scratch,
        compiler_params=pltpu.CompilerParams(
            collective_id=0, has_side_effects=True, vmem_limit_bytes=56 * 1024 * 1024
        ),
    )(*args)
    rows = pl.BlockSpec((8 * B, 128), lambda i: (i, 0))
    whole = pl.BlockSpec((4 * B, B), lambda i: (0, 0))
    outs = pl.pallas_call(
        finish,
        grid=(B // 8,),
        out_shape=(
            jax.ShapeDtypeStruct((B * B, 128), BF16),
            jax.ShapeDtypeStruct((4 * B, B), BF16),
            jax.ShapeDtypeStruct((B * B, 128), F32),
        ),
        in_specs=[
            rows,
            whole,
            pl.BlockSpec((8, 16, 128), lambda i: (i, 0, 0)),
            pl.BlockSpec((1, 128), lambda i: (0, 0)),
            pl.BlockSpec((16, 128), lambda i: (0, 0)),
        ],
        out_specs=(rows, whole, rows),
    )(pair_rows, token_rows, bg.reshape(B, 16, 128), lnb, wpbt)
    return (
        outs[0].reshape(B, B, 128),
        outs[1].reshape(4, B, B),
        outs[2].reshape(B, B, 128),
    )


def solution(mesh):
    placed = (
        P("row", "col", None),
        P(), P(), P(), P(), P(), P(), P(), P(), P(), P(), P(), P(), P(),
        P("samp", "row", "col"),
        P(),
        P(None, "col"),
        P(None, "col"),
        P(None, "col"),
        P(None, "col"),
        P("col", None),
        P("samp", "row", "col"),
    )
    return jax.shard_map(
        per_device,
        mesh=mesh,
        in_specs=placed,
        out_specs=(P("row", "col", None), P("samp", "row", "col"), P("row", "col", None)),
        check_vma=False,
    )
```

```python
import math

import jax
import jax.numpy as jnp
from jax import lax
from jax.experimental import pallas as pl
from jax.experimental.pallas import tpu as pltpu
from jax.sharding import PartitionSpec as P

F32 = jnp.float32
BF16 = jnp.bfloat16
MESH = pl.DeviceIdType.MESH
NR = 8
NC = 8
NS = 4
B = 96
Q = 24
G = 24
CH = 8
RC = 3 * B
CR = 16 * B + 32


def nt(a, b):
    return lax.dot_general(a, b, (((1,), (1,)), ((), ())), preferred_element_type=F32)


def nn(a, b):
    return lax.dot_general(a, b, (((1,), (0,)), ((), ())), preferred_element_type=F32)


def tn(a, b):
    return lax.dot_general(a, b, (((0,), (0,)), ((), ())), preferred_element_type=F32)


def row_means(values, ones):
    half = values.shape[0] // 2
    out = nn(jnp.concatenate([values[:half], values[half:]], axis=1), ones)
    return jnp.concatenate([out[:, :128], out[:, 128:]], axis=0)


def centered(values, ones):
    center = values.astype(F32) - row_means(values, ones)
    return center, lax.rsqrt(row_means((center * center).astype(BF16), ones) + 1e-05)


def normalize(values, ones):
    center, inv = centered(values, ones)
    return center * inv


def mean_weights():
    first = lax.broadcasted_iota(jnp.int32, (256, 256), 0) < 128
    second = lax.broadcasted_iota(jnp.int32, (256, 256), 1) < 128
    return jnp.where(first == second, 1.0 / 128.0, 0.0).astype(BF16)


def kernel(
    pair, crop_s, crop_v, w_ag, w_av, w_bg, w_bv, lnp, w_outgate, w_outproj, w_tg, w_tu, w_td,
    lnb, wpbt, tokens, cot, lnt, wq, wk, wv, wg, wo,
    pair_out, tokens_out, bg,
    wt, w_op, xd, cd,
    ones_ref, normed, made, lf, rf, lm2, lm1, rslab, part, z_recv, y_recv, own_sum, x_send, x_recv, slab, q_s, kslab,
    vslab, gate_s, datt_s, tri_send, tri_recv, tri_f, hb_f, hb_send, hb, bias, raw, d_probs, acc, g_send, g_recv,
    pj_send, py_recv, px_own, px_send, px_recv, sg, cg, cg_f,
    slab_ss, slab_rs, ring_ss, ring_rs, z_ss, z_rs, y_ss, y_rs, x_ss, x_rs,
    kv_ss, kv_rs, t_ss, t_rs, h_ss, h_rs, hg_ss, hg_rs, po_ss, po_rs, pr_ss, pr_rs,
    py_ss, py_rs, px_ss, px_rs, g_ss, g_rs, c_ss, c_rs, b_ss, b_rs,
):
    row = lax.axis_index("row")
    col = lax.axis_index("col")
    samp = lax.axis_index("samp")
    xh = col // 4
    yy = col % 4
    xp = (1 - xh) * 4 + yy
    ones_ref[...] = mean_weights()
    ones = ones_ref[...]
    right = (row + 1) % NR
    left = (row + NR - 1) % NR

    def copy(src, dst, ss, rs, **where):
        return pltpu.make_async_remote_copy(
            src_ref=src, dst_ref=dst, send_sem=ss, recv_sem=rs, device_id=where, device_id_type=MESH
        )

    barrier = pltpu.get_barrier_semaphore()
    for d in range(1, NC):
        pl.semaphore_signal(barrier, inc=1, device_id={"col": (col + d) % NC}, device_id_type=MESH)
    for d in range(1, NR):
        pl.semaphore_signal(barrier, inc=1, device_id={"row": (row + d) % NR}, device_id_type=MESH)
    for d in range(1, NS):
        pl.semaphore_signal(
            barrier, inc=1, device_id={"samp": (samp + d) % NS}, device_id_type=MESH
        )

    def around(d):
        return (yy + d) % 4

    def slab_copy(block, k, there):
        at = slab.at[block]
        return copy(at, at, slab_ss.at[k], slab_rs.at[k], col=there)

    slab_own = [slab_copy(col, d, xh * 4 + around(d)) for d in range(1, 4)]
    slab_own_in = [slab_copy(xh * 4 + around(4 - d), d, xh * 4 + around(d)) for d in range(1, 4)]
    slab_x = slab_copy(col, 0, xp)
    slab_x_in = slab_copy(xp, 0, xp)
    slab_on = [slab_copy(xp, 3 + d, xh * 4 + around(d)) for d in range(1, 4)]
    slab_on_in = [
        slab_copy((1 - xh) * 4 + around(4 - d), 3 + d, xh * 4 + around(d)) for d in range(1, 4)
    ]
    slab[col, 0] = tokens[...]
    slab[col, 1] = cot[...]

    for n, w in enumerate((w_ag, w_av, w_bg, w_bv)):
        wt[n] = w[...].astype(F32).T.astype(BF16)
    wp = jnp.concatenate([wt[n, pl.ds(pl.multiple_of(samp * 32, 32), 32), :] for n in range(4)], axis=0)
    tri_f[0:128, :] = w_outproj[...].astype(F32)
    w_op[...] = jnp.concatenate(
        [tri_f[pl.ds(0, 64, stride=2), :], tri_f[pl.ds(1, 64, stride=2), :]], axis=0
    ).astype(BF16)
    crop = jnp.concatenate([crop_v[i : i + 1, :] for i in range(6)], axis=1).astype(F32)
    token_gain = jnp.concatenate([lnt[i : i + 1, :] for i in range(6)], axis=1)
    keep_cols = jnp.zeros((1, B), F32)
    for b in range(NC):
        keep_cols = jnp.where(col == b, crop[:, b * B : b * B + B], keep_cols)
    keep_cols = jnp.concatenate([keep_cols, jnp.zeros((1, 32), F32)], axis=1)

    for m in range(6):
        normed[m * CR + 16 * B : m * CR + CR, :] = jnp.zeros((32, 128), BF16)
    lane = lax.broadcasted_iota(jnp.int32, (8, 128), 1)
    wide = lane < B

    def norm_chunk(m):
        src = pl.ds(pl.multiple_of(m * (16 * B), 16 * B), 16 * B)
        dst = pl.ds(pl.multiple_of(m * CR, 32), 16 * B)
        normed[dst, :] = (normalize(pair[src, :], ones) * lnp[...]).astype(BF16)

    def edge_chunk(m):
        made[...] = nt(normed[pl.ds(pl.multiple_of(m * CR, 32), CR), :], wp)
        for e in range(16):
            i = m * 16 + e
            o = made[e * B : e * B + 128, :].T
            kept = keep_cols * crop_s[row * B + i].astype(F32)
            for first, dest in ((0, lf), (64, rf)):
                edge = jax.nn.sigmoid(o[first : first + 32]) * o[first + 32 : first + 64] * kept
                tail = edge[24:32]
                for q in range(3):
                    packed = jnp.where(wide, edge[8 * q : 8 * q + 8], pltpu.roll(tail, 96 - 32 * q, 1))
                    dest[pl.ds(i + 8 * B * q, 8, stride=B), :] = packed

    norm_chunk(0)

    pl.semaphore_wait(barrier, NC + NR + NS - 3)
    for c in [slab_x] + slab_own:
        c.start()

    def front_step(m, carry):
        edge_chunk(m)
        norm_chunk(m + 1)
        return carry

    lax.fori_loop(0, 5, front_step, 0)
    edge_chunk(5)
    slab_x_in.wait_recv()
    for c in slab_on:
        c.start()
    own = lax.broadcasted_iota(jnp.int32, (B, 128), 1) < B
    carriers = [(n, k, pl.ds((k * 8 + n) * B, B)) for n in range(CH) for k in range(3)]
    for n, k, at in carriers:
        rslab[n, row, k * B : k * B + B, :] = rf[at, :].astype(BF16)
    for n in range(CH):
        rslab[n, :, RC : RC + 32, :] = jnp.zeros((NR, 32, 128), BF16)

    ring = (right, left)
    step_of = (-1, 1)

    def rcopy(n, t, s, inward):
        back = t if inward else t - 1
        block = (row + NR + step_of[s] * back) % NR
        rows = pl.ds(0, RC) if t < 4 else pl.ds(s * (RC // 2), RC // 2)
        at = rslab.at[n, block, rows]
        return copy(at, at, ring_ss.at[n, s, t - 1], ring_rs.at[n, s, t - 1], row=ring[s])

    for n in range(3):
        for s in range(2):
            rcopy(n, 1, s, False).start()
    empty = jnp.zeros((B, 128), BF16)
    for n, k, at in carriers:
        edge = lf[at, :]
        mine = jnp.where(own, edge, 0.0).astype(BF16)
        rest = jnp.where(own, 0.0, edge).astype(BF16)
        if k < 2:
            lm2[n, k * B : k * B + B, k * 128 : k * 128 + 128] = mine
            lm2[n, k * B : k * B + B, (1 - k) * 128 : (1 - k) * 128 + 128] = empty
            lm2[n, 2 * B : 3 * B, k * 128 : k * 128 + 128] = rest
        else:
            lm1[n, 0:B, :] = mine
            lm1[n, B : 2 * B, :] = rest

    def token_step(pair_of):
        at = pl.ds(pair_of * 2 * B, 2 * B)
        x = [slab[b, 0, at, :].astype(F32) for b in range(NC)]
        total = x[0]
        for b in range(1, NC):
            total = total + x[b]
        mean = jnp.sum(total, axis=-1, keepdims=True) * (1.0 / (NC * B))
        x = [v - mean for v in x]
        total = x[0] * x[0]
        for b in range(1, NC):
            total = total + x[b] * x[b]
        inv = lax.rsqrt(jnp.sum(total, axis=-1, keepdims=True) * (1.0 / (NC * B)) + 1e-05)
        for b in range(NC):
            xd[:, b * B : b * B + B] = x[b] * inv
            cd[:, b * B : b * B + B] = slab[b, 1, at, :].astype(F32)
        normal = (xd[...] * token_gain).astype(BF16)
        q_s[at, :] = nt(normal, wq[...]).astype(BF16)
        tokens_at = pl.ds(pl.multiple_of(row * B, B), B)
        for w, dest in ((wk, kslab), (wv, vslab)):
            out = nt(normal, w[...]).astype(BF16)
            for e in range(2):
                dest[pair_of * 2 + e, tokens_at, :] = out[e * B : e * B + B]
        gate = jax.nn.sigmoid(nt(normal, wg[...]))
        gate_s[at, :] = gate
        d = nt(cd[...].astype(BF16), wo[...])
        datt_s[at, :] = (d * gate).astype(BF16)

    def products(n, back):
        if back in (0, 4):
            blocks = [(row + back) % NR]
        else:
            blocks = [(row + NR + step * back) % NR for step in (-1, 1)]
        rights = [
            jnp.concatenate([rslab[n, j, q * B : q * B + 128, :] for j in blocks], axis=0)
            for q in range(3)
        ]
        two = nt(lm2[n], jnp.concatenate(rights[:2], axis=1))
        one = nt(lm1[n], rights[2])
        for e, j in enumerate(blocks):
            at = slice(e * 128, e * 128 + 128)
            tops = [two[0:B, at], two[B : 2 * B, at], one[0:B, at]]
            tail = two[2 * B : 3 * B, at] + one[B : 2 * B, at]
            for q in range(3):
                packed = jnp.where(own, tops[q], pltpu.roll(tail, 96 - 32 * q, 1))
                part[n, j, q * B : q * B + B, :] = packed.astype(BF16)

    sides = (xh * 4 + (yy + 1) % 4, xh * 4 + (yy + 3) % 4)

    def zcopy(n, s, x):
        src = part.at[n, x * 4 + (yy + 2) % 4, pl.ds(s * (RC // 2), RC // 2)]
        return copy(src, z_recv.at[n, s, x], z_ss.at[n, s, x], z_rs.at[n, s, x], col=sides[s])

    def ycopy(n, s, x):
        src = part.at[n, x * 4 + (yy + 1 + 2 * s) % 4]
        return copy(src, y_recv.at[n, s, x], y_ss.at[n, s, x], y_rs.at[n, s, x], col=sides[s])

    each = [(s, x) for s in range(2) for x in range(2)]

    def z_start(n):
        for s, x in each:
            zcopy(n, s, x).start()

    def y_start(n):
        for s, x in each:
            zcopy(n, s, x).wait_recv()
            j = x * 4 + (yy + 1 + 2 * s) % 4
            at = pl.ds(s * (RC // 2), RC // 2)
            more = z_recv[n, s, x].astype(F32)
            part[n, j, at, :] = (part[n, j, at, :].astype(F32) + more).astype(BF16)
            ycopy(n, s, x).start()

    def y_sum(n):
        for s, x in each:
            ycopy(n, s, x).wait_recv()

        def one(k, carry):
            at = pl.ds(pl.multiple_of(k * B, B), B)

            def total(x):
                v = part[n, x * 4 + yy, at, :].astype(F32)
                for s in range(2):
                    v = v + y_recv[n, s, x, at, :].astype(F32)
                return v

            own_sum[n, at, :] = total(xh)
            x_send[n, at, :] = total(1 - xh).astype(BF16)
            return carry

        lax.fori_loop(0, 3, one, 0)
        xcopy(n).start()

    def xcopy(n):
        return copy(x_send.at[n], x_recv.at[n], x_ss.at[n], x_rs.at[n], col=xp)

    def samp_copy(src_of, dst_of, ss, rs, d, inward):
        there, here = (samp + d) % NS, (samp + NS - d) % NS
        return copy(src_of(there), dst_of(here if inward else samp), ss.at[d], rs.at[d], samp=there)

    def tcopy(n, d, inward):
        return samp_copy(
            lambda m: tri_send.at[m, n], lambda m: tri_recv.at[m, n], t_ss.at[n], t_rs.at[n], d, inward
        )

    lane96 = lax.broadcasted_iota(jnp.int32, (B, 128), 1)

    def triangle(n):
        xcopy(n).wait_recv()
        c = []
        for q in range(3):
            at = pl.ds(q * B, B)
            c.append(own_sum[n, at, :] + x_recv[n, at, :].astype(F32))
        tail = jnp.where(
            lane96 < 32,
            pltpu.roll(c[0], 32, 1),
            jnp.where(lane96 < 64, pltpu.roll(c[1], 64, 1), pltpu.roll(c[2], 96, 1)),
        )
        c.append(tail)
        for h in range(2):
            for m in range(NS):
                both = [v[m * Q : m * Q + Q] for v in c[2 * h : 2 * h + 2]]
                tri_send[m, n, h] = jnp.concatenate(both, axis=0).astype(BF16)
        for d in range(1, NS):
            tcopy(n, d, False).start()

    def kvcopies(t, s, inward):
        back = t if inward else t - 1
        block = (row + NR + step_of[s] * back) % NR
        rows = pl.ds(pl.multiple_of(block * B, B), B)
        both = [(0, kslab), (1, vslab)]
        return [
            copy(v.at[:, rows, :], v.at[:, rows, :], kv_ss.at[n, s, t - 1], kv_rs.at[n, s, t - 1], row=ring[s])
            for n, v in (both if t < 4 else both[s : s + 1])
        ]

    for k in range(CH + 7):
        active = [(n, k - n + 1) for n in range(CH)]
        for n, t in active:
            if 1 <= t <= 5:
                for s in range(2):
                    if t > 1:
                        rcopy(n, t - 1, s, True).wait_recv()
                    if t < 5 and not (t == 1 and n < 3):
                        rcopy(n, t, s, False).start()
        t = k - CH + 1
        if 1 <= t <= 5:
            for s in range(2):
                if t > 1:
                    for c in kvcopies(t - 1, s, True):
                        c.wait_recv()
                if t < 5:
                    for c in kvcopies(t, s, False):
                        c.start()
        for n, t in active:
            if t == 5:
                products(n, 4)
                z_start(n)
            elif t == 6:
                y_start(n)
            elif t == 7:
                y_sum(n)
            elif t == 8:
                triangle(n)
        for n, t in active:
            if 1 <= t <= 4:
                products(n, t - 1)
        if k == 1:
            for c in slab_own_in + slab_on_in:
                c.wait_recv()
        if k in (1, 3):
            token_step(k // 2)

    def unpack(m):
        for n in range(CH):
            for h in range(2):
                both = tri_recv[m, n, h].astype(F32)
                for e in range(2):
                    c = (2 * h + e) * 8 + n
                    r0 = pl.multiple_of(m * 768, 768) + c // 2 * 48 + c % 2 * Q
                    tri_f[pl.ds(r0, Q), :] = both[e * Q : e * Q + Q]

    tri_recv[samp] = tri_send[samp]
    unpack(samp)
    for d in range(1, NS):
        for n in range(CH):
            tcopy(n, d, True).wait_recv()
        unpack((samp + NS - d) % NS)

    row0 = samp * Q
    sib, oth = samp + 1 - 2 * (samp % 2), (samp + 2) % NS
    diag = (sib + 2) % NS

    def part_of(n, m):
        return pair_out.at[pl.ds(pl.multiple_of((n * Q + m * 4) * B, 4 * B), 4 * B)]

    def pocopy(k, m, inward):
        there = (sib, oth)[k]
        at = part_of(there if inward else samp, m)
        return copy(at, at, po_ss.at[k, m], po_rs.at[k, m], samp=there)

    def prcopy(inward):
        n = diag if inward else oth
        at = pair_out.at[pl.ds(pl.multiple_of(n * (Q * B), Q * B), Q * B)]
        return copy(at, at, pr_ss, pr_rs, samp=sib)


    def post_rows(m):
        cols = []
        for e in range(4):
            i = m * 4 + e
            cols.append(
                jnp.concatenate(
                    [tri_f[pl.ds(i, 64, stride=48), :], tri_f[pl.ds(Q + i, 64, stride=48), :]], axis=0
                )
            )
        t = jnp.concatenate(cols, axis=1)
        center = t - jnp.mean(t, axis=0, keepdims=True)
        t = center * lax.rsqrt(jnp.mean(center * center, axis=0, keepdims=True) + 1e-05)
        proj = tn(t.astype(BF16), w_op[...])
        proj = jnp.concatenate([proj[e * 128 : e * 128 + B] for e in range(4)], axis=0)
        first = row0 + m * 4
        at = pl.ds(pl.multiple_of(first * B, 4 * B), 4 * B)
        norm_at = pl.ds(pl.multiple_of(first // 16 * CR + first % 16 * B, 32), 4 * B)
        gate = jax.nn.sigmoid(nn(normed[norm_at, :], w_outgate[...]))
        updated = (pair[at, :].astype(F32) + gate * proj).astype(BF16)
        trans_in = normalize(updated, ones).astype(BF16)
        total = updated.astype(F32)
        for n in range(2):
            a = nn(trans_in, w_tg[:, n * 256 : n * 256 + 256])
            u = nn(trans_in, w_tu[:, n * 256 : n * 256 + 256])
            hidden = (a * jax.nn.sigmoid(a) * u).astype(BF16)
            total = total + nn(hidden, w_td[n * 256 : n * 256 + 256, :])
        out = total.astype(BF16)
        bias_in = (normalize(out, ones) * lnb[...]).astype(BF16)
        return at, out, nt(wpbt[...], bias_in)

    def post_step(m, carry):
        done = [post_rows(m * 2 + n) for n in range(2)]
        for n, (at, out, heads) in enumerate(done):
            pair_out[at, :] = out
            for e in range(4):
                hb_f[pl.ds((m * 2 + n) * 4 + e, 16, stride=Q), 0:B] = heads[:, e * B : e * B + B]
        for n in range(2):
            for k in range(2):
                pocopy(k, m * 2 + n, False).start()
        return carry

    lax.fori_loop(0, Q // 8, post_step, 0)
    for c in range(NC):
        hb_send[c] = hb_f[c * 48 : c * 48 + 48, :].astype(BF16)

    def hcopy(d, inward):
        there, here = (col + d) % NC, (col + NC - d) % NC
        dst = hb.at[here if inward else col, samp]
        return copy(hb_send.at[there], dst, h_ss.at[d], h_rs.at[d], col=there)

    for d in range(1, NC):
        hcopy(d, False).start()
    hb[col, samp] = hb_send[col]

    feature = lax.broadcasted_iota(jnp.int32, (1, B), 1)
    head_masks = [(feature < 48).astype(F32), (feature >= 48).astype(F32)]
    scale = 1.0 / math.sqrt(48)

    def per_head(v):
        return jnp.concatenate([v * m.astype(BF16) for m in head_masks], axis=0)

    def before_bias(s):
        at = slice(s * B, s * B + B)
        raw[s] = nt(per_head(q_s[at, :]), kslab[s]) * scale
        d_probs[s] = nt(per_head(datt_s[at, :]), vslab[s])

    before_bias(0)
    before_bias(1)
    for d in range(1, NC):
        hcopy(d, True).wait_recv()

    def hgcopy(d, inward):
        return samp_copy(lambda _: hb.at[:, samp], lambda n: hb.at[:, n], hg_ss, hg_rs, d, inward)

    for d in range(1, NS):
        hgcopy(d, False).start()
    before_bias(2)
    before_bias(3)
    for d in range(1, NS):
        hgcopy(d, True).wait_recv()

    for b in range(NC):
        key_mask = (crop[:, b * B : b * B + B] - 1.0) * 10000.0
        quarters = [hb[b, n].astype(F32) for n in range(NS)]
        for h in range(2):
            whole = jnp.concatenate([v[h * Q : h * Q + Q, 0:B] for v in quarters], axis=0)
            bias[h * B : h * B + B, b * B : b * B + B] = whole + key_mask
    acc[...] = jnp.zeros((2 * B, NC * B), F32)
    def att_rows(s):
        at = pl.ds(pl.multiple_of(s * B, B), B)
        scores = raw[s] + bias[...]
        shifted = jnp.exp(scores - jnp.max(scores, axis=-1, keepdims=True))
        probs = shifted * (1.0 / jnp.sum(shifted, axis=-1, keepdims=True))
        got = nn(probs.astype(BF16), vslab[s])
        delta = jnp.sum(per_head(datt_s[at, :]).astype(F32) * got, axis=-1, keepdims=True)
        attended = got[0:B] * head_masks[0] + got[B : 2 * B] * head_masks[1]
        return (gate_s[at, :] * attended).astype(BF16), probs * (d_probs[s] - delta)

    def att_step(m, carry):
        done = [att_rows(m * 2 + e) for e in range(2)]
        acc[...] = acc[...] + (done[0][1] + done[1][1])
        gated = jnp.concatenate([v for v, _ in done], axis=0)
        at = pl.ds(pl.multiple_of(m * 2 * B, 2 * B), 2 * B)
        xd[...] = nn(gated, wo[...])
        for b in range(NC):
            pj_send[b, at, :] = xd[:, b * B : b * B + B].astype(BF16)
        return carry

    lax.fori_loop(0, 2, att_step, 0)
    for m in range(6):
        pocopy(1, m, True).wait_recv()
    prcopy(False).start()

    for b in range(NC):
        heads = [acc[h * B : h * B + B, b * B : b * B + B] for h in range(2)]
        for n in range(NS):
            both = jnp.concatenate([v[n * Q : n * Q + Q] for v in heads], axis=0)
            g_send[n, b, :, 0:B] = both.astype(BF16)

    def gcopy(d, inward):
        return samp_copy(lambda n: g_send.at[n], lambda n: g_recv.at[n], g_ss, g_rs, d, inward)

    for d in range(1, NS):
        gcopy(d, False).start()

    def pycopy(d, x):
        src = pj_send.at[x * 4 + around(d)]
        return copy(src, py_recv.at[d - 1, x], py_ss.at[d, x], py_rs.at[d, x], col=xh * 4 + around(d))

    pys = [(d, x) for d in range(1, 4) for x in range(2)]
    for d, x in pys:
        pycopy(d, x).start()
    g_recv[samp] = g_send[samp]
    for d in range(1, NS):
        gcopy(d, True).wait_recv()

    def sum_step(b, carry):
        total = g_recv[0, b].astype(F32)
        for n in range(1, NS):
            total = total + g_recv[n, b].astype(F32)
        sg[b] = total.astype(BF16)
        return carry

    lax.fori_loop(0, NC, sum_step, 0)

    def ccopy(d, inward):
        there, here = (col + d) % NC, (col + NC - d) % NC
        return copy(sg.at[there], cg.at[here if inward else col], c_ss.at[d], c_rs.at[d], col=there)

    for d in range(1, NC):
        ccopy(d, False).start()
    cg[col] = sg[col]

    for d, x in pys:
        pycopy(d, x).wait_recv()

    def py_step(s, carry):
        at = pl.ds(pl.multiple_of(s * B, B), B)

        def total(x):
            v = pj_send[x * 4 + yy, at, :].astype(F32)
            for d in range(3):
                v = v + py_recv[d, x, at, :].astype(F32)
            return v

        px_own[at, :] = total(xh) + tokens[at, :].astype(F32)
        px_send[at, :] = total(1 - xh).astype(BF16)
        return carry

    lax.fori_loop(0, 4, py_step, 0)
    px = copy(px_send, px_recv, px_ss, px_rs, col=xp)
    px.start()
    for d in range(1, NC):
        ccopy(d, True).wait_recv()
    for c in range(NC):
        cg_f[c * 48 : c * 48 + 48, :] = cg[c].astype(F32)
    for i in range(Q):
        bg[samp, i] = cg_f[pl.ds(i, 16, stride=Q), :].astype(BF16)

    def bcopy(d, inward):
        return samp_copy(lambda _: bg.at[samp], lambda n: bg.at[n], b_ss, b_rs, d, inward)

    for d in range(1, NS):
        bcopy(d, False).start()
    px.wait_recv()
    tokens_out[...] = (px_own[...] + px_recv[...].astype(F32)).astype(BF16)
    for m in range(6):
        pocopy(0, m, True).wait_recv()
    prcopy(True).wait_recv()
    for d in range(1, NS):
        bcopy(d, True).wait_recv()

    for c in [slab_x, px, prcopy(False)] + slab_own + slab_on:
        c.wait_send()
    for d, x in pys:
        pycopy(d, x).wait_send()
    for m in range(6):
        for k in range(2):
            pocopy(k, m, False).wait_send()

    for n in range(CH):
        for s in range(2):
            for t in range(1, 5):
                rcopy(n, t, s, False).wait_send()
        for s, x in each:
            zcopy(n, s, x).wait_send()
            ycopy(n, s, x).wait_send()
        for d in range(1, NS):
            tcopy(n, d, False).wait_send()
        xcopy(n).wait_send()
    for t in range(1, 5):
        for s in range(2):
            for c in kvcopies(t, s, False):
                c.wait_send()
    for d in range(1, NC):
        hcopy(d, False).wait_send()
        ccopy(d, False).wait_send()
    for d in range(1, NS):
        hgcopy(d, False).wait_send()
        gcopy(d, False).wait_send()
        bcopy(d, False).wait_send()


def split(v):
    high = v.astype(BF16)
    rest = v - high.astype(F32)
    mid = rest.astype(BF16)
    return high, mid, (rest - mid.astype(F32)).astype(BF16)


def finish(pair_rows, token_rows, bg, lnb, wpbt, pair_out, tokens_out, pair_grad):
    @pl.when(pl.program_id(0) == 0)
    def _():
        tokens_out[...] = token_rows[...]

    pair_out[...] = pair_rows[...]
    ones = mean_weights()
    weights = wpbt[...].astype(F32) * lnb[...]
    weights = weights - jnp.mean(weights, axis=-1, keepdims=True)
    weights = jnp.concatenate(split(weights), axis=0)
    empty = jnp.zeros((48, 128), BF16)
    weights = jnp.concatenate(
        [jnp.concatenate([weights, empty], axis=1), jnp.concatenate([empty, weights], axis=1)], axis=0
    )
    for e in range(4):
        at = slice(e * 4 * B, e * 4 * B + 4 * B)
        even, odd = [
            jnp.concatenate([bg[e * 4 + n], bg[e * 4 + 2 + n]], axis=1) for n in range(2)
        ]
        both = tn(jnp.concatenate([even] * 3 + [odd] * 3, axis=0), weights)
        scaled = jnp.concatenate(
            [both[0:B, :128], both[0:B, 128:], both[128 : 128 + B, :128], both[128 : 128 + B, 128:]], axis=0
        )
        center, inv = centered(pair_rows[at, :], ones)
        unit = center * inv
        pair_grad[at, :] = inv * (scaled - unit * row_means((scaled * unit).astype(BF16), ones))


def per_device(
    pair, crop_mask, w_agate, w_aval, w_bgate, w_bval, w_outgate, w_outproj, ln_pair,
    w_trans_gate, w_trans_up, w_trans_down, ln_bias, w_pairbias, tokens, ln_token,
    w_query, w_key, w_value, w_gate, w_output, cotangent,
):
    wpbt = w_pairbias.T
    lnb = ln_bias.reshape(1, 128)
    args = (
        pair.reshape(B * B, 128), crop_mask, crop_mask.reshape(6, 128),
        w_agate, w_aval, w_bgate, w_bval, ln_pair.reshape(1, 128), w_outgate, w_outproj,
        w_trans_gate, w_trans_up, w_trans_down, lnb, wpbt,
        tokens.reshape(4 * B, B), cotangent.reshape(4 * B, B), ln_token.reshape(6, 128),
        w_query.T, w_key.T, w_value.T, w_gate.T, w_output,
    )
    vm = pltpu.VMEM
    dma = pltpu.SemaphoreType.DMA
    scratch = [
        vm((4, 128, 128), BF16),
        vm((128, 128), BF16),
        vm((2 * B, NC * B), F32),
        vm((2 * B, NC * B), F32),
        vm((256, 256), BF16),
        vm((6 * CR, 128), BF16),
        vm((CR, 128), F32),
        vm((G * B, 128), F32),
        vm((G * B, 128), F32),
        vm((CH, 3 * B, 256), BF16),
        vm((CH, 2 * B, 128), BF16),
        vm((CH, NR, RC + 32, 128), BF16),
        vm((CH, NR, RC, 128), BF16),
        vm((CH, 2, 2, RC // 2, 128), BF16),
        vm((CH, 2, 2, RC, 128), BF16),
        vm((CH, RC, 128), F32),
        vm((CH, RC, 128), BF16),
        vm((CH, RC, 128), BF16),
        vm((NC, 2, 4 * B, B), BF16),
        vm((4 * B, B), BF16),
        vm((4, NR * B, B), BF16),
        vm((4, NR * B, B), BF16),
        vm((4 * B, B), F32),
        vm((4 * B, B), BF16),
        vm((NS, CH, 2, 48, 128), BF16),
        vm((NS, CH, 2, 48, 128), BF16),
        vm((64 * 48, 128), F32),
        vm((16 * Q, 128), F32),
        vm((NC, 48, 128), BF16),
        vm((NC, NS, 48, 128), BF16),
        vm((2 * B, NC * B), F32),
        vm((4, 2 * B, NC * B), F32),
        vm((4, 2 * B, NC * B), F32),
        vm((2 * B, NC * B), F32),
        vm((NS, NC, 48, 128), BF16),
        vm((NS, NC, 48, 128), BF16),
        vm((NC, 4 * B, B), BF16),
        vm((3, 2, 4 * B, B), BF16),
        vm((4 * B, B), F32),
        vm((4 * B, B), BF16),
        vm((4 * B, B), BF16),
        vm((NC, 48, 128), BF16),
        vm((NC, 48, 128), BF16),
        vm((16 * Q, 128), F32),
    ]
    sems = [(7,)] * 2 + [(CH, 2, 4)] * 2 + [(CH, 2, 2)] * 4 + [(CH,)] * 2
    sems += [(2, 2, 4)] * 2 + [(CH, 4)] * 2 + [(8,)] * 2 + [(4,)] * 2 + [(2, 6)] * 2 + [None] * 2
    sems += [(4, 2)] * 2 + [None] * 2 + [(4,)] * 2 + [(8,)] * 2 + [(4,)] * 2
    scratch += [dma if s is None else dma(s) for s in sems]
    spec = pl.BlockSpec(memory_space=pltpu.VMEM)
    specs = [spec] * len(args)
    specs[1] = pl.BlockSpec(memory_space=pltpu.SMEM)
    pair_rows, token_rows, bg = pl.pallas_call(
        kernel,
        out_shape=(
            jax.ShapeDtypeStruct((B * B, 128), BF16),
            jax.ShapeDtypeStruct((4 * B, B), BF16),
            jax.ShapeDtypeStruct((NS, Q, 16, 128), BF16),
        ),
        in_specs=specs,
        out_specs=(spec,) * 3,
        scratch_shapes=scratch,
        compiler_params=pltpu.CompilerParams(
            collective_id=0, has_side_effects=True, vmem_limit_bytes=56 * 1024 * 1024
        ),
    )(*args)
    rows = pl.BlockSpec((16 * B, 128), lambda i: (i, 0))
    whole = pl.BlockSpec((4 * B, B), lambda i: (0, 0))
    outs = pl.pallas_call(
        finish,
        grid=(B // 16,),
        out_shape=(
            jax.ShapeDtypeStruct((B * B, 128), BF16),
            jax.ShapeDtypeStruct((4 * B, B), BF16),
            jax.ShapeDtypeStruct((B * B, 128), F32),
        ),
        in_specs=[
            rows,
            whole,
            pl.BlockSpec((16, 16, 128), lambda i: (i, 0, 0)),
            pl.BlockSpec((1, 128), lambda i: (0, 0)),
            pl.BlockSpec((16, 128), lambda i: (0, 0)),
        ],
        out_specs=(rows, whole, rows),
    )(pair_rows, token_rows, bg.reshape(B, 16, 128), lnb, wpbt)
    return (
        outs[0].reshape(B, B, 128),
        outs[1].reshape(4, B, B),
        outs[2].reshape(B, B, 128),
    )


def solution(mesh):
    placed = (
        P("row", "col", None),
        P(), P(), P(), P(), P(), P(), P(), P(), P(), P(), P(), P(), P(),
        P("samp", "row", "col"),
        P(),
        P(None, "col"),
        P(None, "col"),
        P(None, "col"),
        P(None, "col"),
        P("col", None),
        P("samp", "row", "col"),
    )
    return jax.shard_map(
        per_device,
        mesh=mesh,
        in_specs=placed,
        out_specs=(P("row", "col", None), P("samp", "row", "col"), P("row", "col", None)),
        check_vma=False,
    )
```

```python
import math

import jax
import jax.numpy as jnp
from jax import lax
from jax.experimental import pallas as pl
from jax.experimental.pallas import tpu as pltpu
from jax.sharding import PartitionSpec as P

F32 = jnp.float32
BF16 = jnp.bfloat16
MESH = pl.DeviceIdType.MESH
NR = 8
NC = 8
NS = 4
B = 96
Q = 24
G = 24
CH = 8
RC = 3 * B
CR = 16 * B + 32


def nt(a, b):
    return lax.dot_general(a, b, (((1,), (1,)), ((), ())), preferred_element_type=F32)


def nn(a, b):
    return lax.dot_general(a, b, (((1,), (0,)), ((), ())), preferred_element_type=F32)


def tn(a, b):
    return lax.dot_general(a, b, (((0,), (0,)), ((), ())), preferred_element_type=F32)


def row_means(values, ones):
    half = values.shape[0] // 2
    out = nn(jnp.concatenate([values[:half], values[half:]], axis=1), ones)
    return jnp.concatenate([out[:, :128], out[:, 128:]], axis=0)


def centered(values, ones):
    center = values.astype(F32) - row_means(values, ones)
    return center, lax.rsqrt(row_means((center * center).astype(BF16), ones) + 1e-05)


def normalize(values, ones):
    center, inv = centered(values, ones)
    return center * inv


def mean_weights():
    first = lax.broadcasted_iota(jnp.int32, (256, 256), 0) < 128
    second = lax.broadcasted_iota(jnp.int32, (256, 256), 1) < 128
    return jnp.where(first == second, 1.0 / 128.0, 0.0).astype(BF16)


def kernel(
    pair, crop_s, crop_v, w_ag, w_av, w_bg, w_bv, lnp, w_outgate, w_outproj, w_tg, w_tu, w_td,
    lnb, wpbt, tokens, cot, lnt, wq, wk, wv, wg, wo,
    pair_out, tokens_out, bg,
    wt, w_op, xd, cd,
    ones_ref, normed, made, lf, rf, lm2, lm1, rslab, part, z_recv, y_recv, own_sum, x_send, x_recv, slab, q_s, kslab,
    vslab, gate_s, datt_s, tri_send, tri_recv, tri_f, hb_f, hb_send, hb, bias, raw, d_probs, acc, g_send, g_recv,
    pj_send, py_recv, px_own, px_send, px_recv, sg, cg, cg_f,
    slab_ss, slab_rs, ring_ss, ring_rs, z_ss, z_rs, y_ss, y_rs, x_ss, x_rs,
    kv_ss, kv_rs, t_ss, t_rs, h_ss, h_rs, hg_ss, hg_rs, po_ss, po_rs, pr_ss, pr_rs,
    py_ss, py_rs, px_ss, px_rs, g_ss, g_rs, c_ss, c_rs, b_ss, b_rs,
):
    row = lax.axis_index("row")
    col = lax.axis_index("col")
    samp = lax.axis_index("samp")
    xh = col // 4
    yy = col % 4
    xp = (1 - xh) * 4 + yy
    ones_ref[...] = mean_weights()
    ones = ones_ref[...]
    right = (row + 1) % NR
    left = (row + NR - 1) % NR

    def copy(src, dst, ss, rs, **where):
        return pltpu.make_async_remote_copy(
            src_ref=src, dst_ref=dst, send_sem=ss, recv_sem=rs, device_id=where, device_id_type=MESH
        )

    barrier = pltpu.get_barrier_semaphore()
    for d in range(1, NC):
        pl.semaphore_signal(barrier, inc=1, device_id={"col": (col + d) % NC}, device_id_type=MESH)
    for d in range(1, NR):
        pl.semaphore_signal(barrier, inc=1, device_id={"row": (row + d) % NR}, device_id_type=MESH)
    for d in range(1, NS):
        pl.semaphore_signal(
            barrier, inc=1, device_id={"samp": (samp + d) % NS}, device_id_type=MESH
        )

    def around(d):
        return (yy + d) % 4

    def slab_copy(block, k, there):
        at = slab.at[block]
        return copy(at, at, slab_ss.at[k], slab_rs.at[k], col=there)

    slab_own = [slab_copy(col, d, xh * 4 + around(d)) for d in range(1, 4)]
    slab_own_in = [slab_copy(xh * 4 + around(4 - d), d, xh * 4 + around(d)) for d in range(1, 4)]
    slab_x = slab_copy(col, 0, xp)
    slab_x_in = slab_copy(xp, 0, xp)
    slab_on = [slab_copy(xp, 3 + d, xh * 4 + around(d)) for d in range(1, 4)]
    slab_on_in = [
        slab_copy((1 - xh) * 4 + around(4 - d), 3 + d, xh * 4 + around(d)) for d in range(1, 4)
    ]
    slab[col, 0] = tokens[...]
    slab[col, 1] = cot[...]

    for n, w in enumerate((w_ag, w_av, w_bg, w_bv)):
        wt[n] = w[...].astype(F32).T.astype(BF16)
    wp = jnp.concatenate([wt[n, pl.ds(pl.multiple_of(samp * 32, 32), 32), :] for n in range(4)], axis=0)
    tri_f[0:128, :] = w_outproj[...].astype(F32)
    w_op[...] = jnp.concatenate(
        [tri_f[pl.ds(0, 64, stride=2), :], tri_f[pl.ds(1, 64, stride=2), :]], axis=0
    ).astype(BF16)
    crop = jnp.concatenate([crop_v[i : i + 1, :] for i in range(6)], axis=1).astype(F32)
    token_gain = jnp.concatenate([lnt[i : i + 1, :] for i in range(6)], axis=1)
    keep_cols = jnp.zeros((1, B), F32)
    for b in range(NC):
        keep_cols = jnp.where(col == b, crop[:, b * B : b * B + B], keep_cols)
    keep_cols = jnp.concatenate([keep_cols, jnp.zeros((1, 32), F32)], axis=1)

    for m in range(6):
        normed[m * CR + 16 * B : m * CR + CR, :] = jnp.zeros((32, 128), BF16)
    lane = lax.broadcasted_iota(jnp.int32, (8, 128), 1)
    wide = lane < B

    def norm_chunk(m):
        src = pl.ds(pl.multiple_of(m * (16 * B), 16 * B), 16 * B)
        dst = pl.ds(pl.multiple_of(m * CR, 32), 16 * B)
        normed[dst, :] = (normalize(pair[src, :], ones) * lnp[...]).astype(BF16)

    def edge_chunk(m):
        made[...] = nt(normed[pl.ds(pl.multiple_of(m * CR, 32), CR), :], wp)
        for e in range(16):
            i = m * 16 + e
            o = made[e * B : e * B + 128, :].T
            kept = keep_cols * crop_s[row * B + i].astype(F32)
            for first, dest in ((0, lf), (64, rf)):
                edge = jax.nn.sigmoid(o[first : first + 32]) * o[first + 32 : first + 64] * kept
                tail = edge[24:32]
                for q in range(3):
                    packed = jnp.where(wide, edge[8 * q : 8 * q + 8], pltpu.roll(tail, 96 - 32 * q, 1))
                    dest[pl.ds(i + 8 * B * q, 8, stride=B), :] = packed

    norm_chunk(0)

    pl.semaphore_wait(barrier, NC + NR + NS - 3)
    for c in [slab_x] + slab_own:
        c.start()

    def front_step(m, carry):
        edge_chunk(m)
        norm_chunk(m + 1)
        return carry

    lax.fori_loop(0, 5, front_step, 0)
    edge_chunk(5)
    slab_x_in.wait_recv()
    for c in slab_on:
        c.start()
    own = lax.broadcasted_iota(jnp.int32, (B, 128), 1) < B
    carriers = [(n, k, pl.ds((k * 8 + n) * B, B)) for n in range(CH) for k in range(3)]
    for n, k, at in carriers:
        rslab[n, row, k * B : k * B + B, :] = rf[at, :].astype(BF16)
    for n in range(CH):
        rslab[n, :, RC : RC + 32, :] = jnp.zeros((NR, 32, 128), BF16)

    ring = (right, left)
    step_of = (-1, 1)

    def rcopy(n, t, s, inward):
        back = t if inward else t - 1
        block = (row + NR + step_of[s] * back) % NR
        rows = pl.ds(0, RC) if t < 4 else pl.ds(s * (RC // 2), RC // 2)
        at = rslab.at[n, block, rows]
        return copy(at, at, ring_ss.at[n, s, t - 1], ring_rs.at[n, s, t - 1], row=ring[s])

    for n in range(3):
        for s in range(2):
            rcopy(n, 1, s, False).start()
    empty = jnp.zeros((B, 128), BF16)
    for n, k, at in carriers:
        edge = lf[at, :]
        mine = jnp.where(own, edge, 0.0).astype(BF16)
        rest = jnp.where(own, 0.0, edge).astype(BF16)
        if k < 2:
            lm2[n, k * B : k * B + B, k * 128 : k * 128 + 128] = mine
            lm2[n, k * B : k * B + B, (1 - k) * 128 : (1 - k) * 128 + 128] = empty
            lm2[n, 2 * B : 3 * B, k * 128 : k * 128 + 128] = rest
        else:
            lm1[n, 0:B, :] = mine
            lm1[n, B : 2 * B, :] = rest

    def token_step(pair_of):
        at = pl.ds(pair_of * 2 * B, 2 * B)
        x = [slab[b, 0, at, :].astype(F32) for b in range(NC)]
        total = x[0]
        for b in range(1, NC):
            total = total + x[b]
        mean = jnp.sum(total, axis=-1, keepdims=True) * (1.0 / (NC * B))
        x = [v - mean for v in x]
        total = x[0] * x[0]
        for b in range(1, NC):
            total = total + x[b] * x[b]
        inv = lax.rsqrt(jnp.sum(total, axis=-1, keepdims=True) * (1.0 / (NC * B)) + 1e-05)
        for b in range(NC):
            xd[:, b * B : b * B + B] = x[b] * inv
            cd[:, b * B : b * B + B] = slab[b, 1, at, :].astype(F32)
        normal = (xd[...] * token_gain).astype(BF16)
        q_s[at, :] = nt(normal, wq[...]).astype(BF16)
        tokens_at = pl.ds(pl.multiple_of(row * B, B), B)
        for w, dest in ((wk, kslab), (wv, vslab)):
            out = nt(normal, w[...]).astype(BF16)
            for e in range(2):
                dest[pair_of * 2 + e, tokens_at, :] = out[e * B : e * B + B]
        gate = jax.nn.sigmoid(nt(normal, wg[...]))
        gate_s[at, :] = gate
        d = nt(cd[...].astype(BF16), wo[...])
        datt_s[at, :] = (d * gate).astype(BF16)

    def products(n, back):
        if back in (0, 4):
            blocks = [(row + back) % NR]
        else:
            blocks = [(row + NR + step * back) % NR for step in (-1, 1)]
        rights = [
            jnp.concatenate([rslab[n, j, q * B : q * B + 128, :] for j in blocks], axis=0)
            for q in range(3)
        ]
        two = nt(lm2[n], jnp.concatenate(rights[:2], axis=1))
        one = nt(lm1[n], rights[2])
        for e, j in enumerate(blocks):
            at = slice(e * 128, e * 128 + 128)
            tops = [two[0:B, at], two[B : 2 * B, at], one[0:B, at]]
            tail = two[2 * B : 3 * B, at] + one[B : 2 * B, at]
            for q in range(3):
                packed = jnp.where(own, tops[q], pltpu.roll(tail, 96 - 32 * q, 1))
                part[n, j % 4, j // 4, q * B : q * B + B, :] = packed.astype(BF16)

    sides = (xh * 4 + (yy + 1) % 4, xh * 4 + (yy + 3) % 4)

    def zcopy(n, s):
        src = part.at[n, (yy + 2) % 4, :, pl.ds(s * (RC // 2), RC // 2)]
        return copy(src, z_recv.at[n, s], z_ss.at[n, s], z_rs.at[n, s], col=sides[s])

    def ycopy(n, s):
        there = (yy + (1, 3, 2)[s]) % 4
        return copy(
            part.at[n, there], y_recv.at[n, s], y_ss.at[n, s], y_rs.at[n, s], col=xh * 4 + there
        )

    def y_ways(n):
        return (0, 1, 2) if n >= CH - 2 else (0, 1)

    def z_start(n):
        for s in range(2):
            zcopy(n, s).start()

    def y_start(n):
        for s in range(2):
            zcopy(n, s).wait_recv()
            for x in range(2):
                at = pl.ds(s * (RC // 2), RC // 2)
                more = z_recv[n, s, x].astype(F32)
                there = (yy + 1 + 2 * s) % 4
                part[n, there, x, at, :] = (part[n, there, x, at, :].astype(F32) + more).astype(BF16)
            ycopy(n, s).start()

    def y_sum(n):
        for s in y_ways(n):
            ycopy(n, s).wait_recv()

        def one(k, carry):
            at = pl.ds(pl.multiple_of(k * B, B), B)

            def total(x):
                v = part[n, yy, x, at, :].astype(F32)
                for s in y_ways(n):
                    v = v + y_recv[n, s, x, at, :].astype(F32)
                return v

            own_sum[n, at, :] = total(xh)
            x_send[n, at, :] = total(1 - xh).astype(BF16)
            return carry

        lax.fori_loop(0, 3, one, 0)
        xcopy(n).start()

    def xcopy(n):
        return copy(x_send.at[n], x_recv.at[n], x_ss.at[n], x_rs.at[n], col=xp)

    def samp_copy(src_of, dst_of, ss, rs, d, inward):
        there, here = (samp + d) % NS, (samp + NS - d) % NS
        return copy(src_of(there), dst_of(here if inward else samp), ss.at[d], rs.at[d], samp=there)

    def tcopy(n, d, inward):
        return samp_copy(
            lambda m: tri_send.at[m, n], lambda m: tri_recv.at[m, n], t_ss.at[n], t_rs.at[n], d, inward
        )

    lane96 = lax.broadcasted_iota(jnp.int32, (B, 128), 1)

    def triangle(n):
        xcopy(n).wait_recv()
        c = []
        for q in range(3):
            at = pl.ds(q * B, B)
            c.append(own_sum[n, at, :] + x_recv[n, at, :].astype(F32))
        tail = jnp.where(
            lane96 < 32,
            pltpu.roll(c[0], 32, 1),
            jnp.where(lane96 < 64, pltpu.roll(c[1], 64, 1), pltpu.roll(c[2], 96, 1)),
        )
        c.append(tail)
        for h in range(2):
            for m in range(NS):
                both = [v[m * Q : m * Q + Q] for v in c[2 * h : 2 * h + 2]]
                tri_send[m, n, h] = jnp.concatenate(both, axis=0).astype(BF16)
        for d in range(1, NS):
            tcopy(n, d, False).start()

    def kvcopies(t, s, inward):
        back = t if inward else t - 1
        block = (row + NR + step_of[s] * back) % NR
        rows = pl.ds(pl.multiple_of(block * B, B), B)
        both = [(0, kslab), (1, vslab)]
        return [
            copy(v.at[:, rows, :], v.at[:, rows, :], kv_ss.at[n, s, t - 1], kv_rs.at[n, s, t - 1], row=ring[s])
            for n, v in (both if t < 4 else both[s : s + 1])
        ]

    for k in range(CH + 6):
        active = [(n, k - n + 1) for n in range(CH)]
        for n, t in active:
            if 1 <= t <= 5:
                for s in range(2):
                    if t > 1:
                        rcopy(n, t - 1, s, True).wait_recv()
                    if t < 5 and not (t == 1 and n < 3):
                        rcopy(n, t, s, False).start()
        t = k - CH + 1
        if 1 <= t <= 5:
            for s in range(2):
                if t > 1:
                    for c in kvcopies(t - 1, s, True):
                        c.wait_recv()
                if t < 5:
                    for c in kvcopies(t, s, False):
                        c.start()
        for n, t in active:
            straight = n >= CH - 2
            if t == 5:
                products(n, 4)
                if straight:
                    for s in y_ways(n):
                        ycopy(n, s).start()
                else:
                    z_start(n)
            elif t == 6 and not straight:
                y_start(n)
            elif t == 7 - straight:
                y_sum(n)
            elif t == 8 - straight:
                triangle(n)
        for n, t in active:
            if 1 <= t <= 4:
                products(n, t - 1)
        if k == 4:
            for c in slab_own_in + slab_on_in:
                c.wait_recv()
        if k in (4, 6):
            token_step(k // 2 - 2)

    def unpack(m):
        for n in range(CH):
            for h in range(2):
                both = tri_recv[m, n, h].astype(F32)
                for e in range(2):
                    c = (2 * h + e) * 8 + n
                    r0 = pl.multiple_of(m * 768, 768) + c // 2 * 48 + c % 2 * Q
                    tri_f[pl.ds(r0, Q), :] = both[e * Q : e * Q + Q]

    tri_recv[samp] = tri_send[samp]
    unpack(samp)
    for d in range(1, NS):
        for n in range(CH):
            tcopy(n, d, True).wait_recv()
        unpack((samp + NS - d) % NS)

    row0 = samp * Q
    sib, oth = samp + 1 - 2 * (samp % 2), (samp + 2) % NS
    diag = (sib + 2) % NS

    def part_of(n, m):
        return pair_out.at[pl.ds(pl.multiple_of((n * Q + m * 4) * B, 4 * B), 4 * B)]

    def pocopy(k, m, inward):
        there = (sib, oth)[k]
        at = part_of(there if inward else samp, m)
        return copy(at, at, po_ss.at[k, m], po_rs.at[k, m], samp=there)

    def prcopy(inward):
        n = diag if inward else oth
        at = pair_out.at[pl.ds(pl.multiple_of(n * (Q * B), Q * B), Q * B)]
        return copy(at, at, pr_ss, pr_rs, samp=sib)


    def post_rows(m):
        cols = []
        for e in range(4):
            i = m * 4 + e
            cols.append(
                jnp.concatenate(
                    [tri_f[pl.ds(i, 64, stride=48), :], tri_f[pl.ds(Q + i, 64, stride=48), :]], axis=0
                )
            )
        t = jnp.concatenate(cols, axis=1)
        center = t - jnp.mean(t, axis=0, keepdims=True)
        t = center * lax.rsqrt(jnp.mean(center * center, axis=0, keepdims=True) + 1e-05)
        proj = tn(t.astype(BF16), w_op[...])
        proj = jnp.concatenate([proj[e * 128 : e * 128 + B] for e in range(4)], axis=0)
        first = row0 + m * 4
        at = pl.ds(pl.multiple_of(first * B, 4 * B), 4 * B)
        norm_at = pl.ds(pl.multiple_of(first // 16 * CR + first % 16 * B, 32), 4 * B)
        gate = jax.nn.sigmoid(nn(normed[norm_at, :], w_outgate[...]))
        updated = (pair[at, :].astype(F32) + gate * proj).astype(BF16)
        trans_in = normalize(updated, ones).astype(BF16)
        total = updated.astype(F32)
        for n in range(2):
            a = nn(trans_in, w_tg[:, n * 256 : n * 256 + 256])
            u = nn(trans_in, w_tu[:, n * 256 : n * 256 + 256])
            hidden = (a * jax.nn.sigmoid(a) * u).astype(BF16)
            total = total + nn(hidden, w_td[n * 256 : n * 256 + 256, :])
        out = total.astype(BF16)
        bias_in = (normalize(out, ones) * lnb[...]).astype(BF16)
        return at, out, nt(wpbt[...], bias_in)

    def post_step(m, carry):
        done = [post_rows(m * 2 + n) for n in range(2)]
        for n, (at, out, heads) in enumerate(done):
            pair_out[at, :] = out
            for e in range(4):
                hb_f[pl.ds((m * 2 + n) * 4 + e, 16, stride=Q), 0:B] = heads[:, e * B : e * B + B]
        for n in range(2):
            for k in range(2):
                pocopy(k, m * 2 + n, False).start()
        return carry

    lax.fori_loop(0, Q // 8, post_step, 0)
    for c in range(NC):
        hb_send[c] = hb_f[c * 48 : c * 48 + 48, :].astype(BF16)

    def hcopy(d, inward):
        there, here = (col + d) % NC, (col + NC - d) % NC
        dst = hb.at[here if inward else col, samp]
        return copy(hb_send.at[there], dst, h_ss.at[d], h_rs.at[d], col=there)

    for d in range(1, NC):
        hcopy(d, False).start()
    hb[col, samp] = hb_send[col]

    feature = lax.broadcasted_iota(jnp.int32, (1, B), 1)
    head_masks = [(feature < 48).astype(F32), (feature >= 48).astype(F32)]
    scale = 1.0 / math.sqrt(48)

    def per_head(v):
        return jnp.concatenate([v * m.astype(BF16) for m in head_masks], axis=0)

    def before_bias(s):
        at = slice(s * B, s * B + B)
        raw[s] = nt(per_head(q_s[at, :]), kslab[s]) * scale
        d_probs[s] = nt(per_head(datt_s[at, :]), vslab[s])

    before_bias(0)
    before_bias(1)
    for d in range(1, NC):
        hcopy(d, True).wait_recv()

    def hgcopy(d, inward):
        return samp_copy(lambda _: hb.at[:, samp], lambda n: hb.at[:, n], hg_ss, hg_rs, d, inward)

    for d in range(1, NS):
        hgcopy(d, False).start()
    before_bias(2)
    before_bias(3)
    for d in range(1, NS):
        hgcopy(d, True).wait_recv()

    for b in range(NC):
        key_mask = (crop[:, b * B : b * B + B] - 1.0) * 10000.0
        quarters = [hb[b, n].astype(F32) for n in range(NS)]
        for h in range(2):
            whole = jnp.concatenate([v[h * Q : h * Q + Q, 0:B] for v in quarters], axis=0)
            bias[h * B : h * B + B, b * B : b * B + B] = whole + key_mask
    acc[...] = jnp.zeros((2 * B, NC * B), F32)
    def att_rows(s):
        at = pl.ds(pl.multiple_of(s * B, B), B)
        scores = raw[s] + bias[...]
        shifted = jnp.exp(scores - jnp.max(scores, axis=-1, keepdims=True))
        probs = shifted * (1.0 / jnp.sum(shifted, axis=-1, keepdims=True))
        got = nn(probs.astype(BF16), vslab[s])
        delta = jnp.sum(per_head(datt_s[at, :]).astype(F32) * got, axis=-1, keepdims=True)
        attended = got[0:B] * head_masks[0] + got[B : 2 * B] * head_masks[1]
        return (gate_s[at, :] * attended).astype(BF16), probs * (d_probs[s] - delta)

    def att_step(m, carry):
        done = [att_rows(m * 2 + e) for e in range(2)]
        acc[...] = acc[...] + (done[0][1] + done[1][1])
        gated = jnp.concatenate([v for v, _ in done], axis=0)
        at = pl.ds(pl.multiple_of(m * 2 * B, 2 * B), 2 * B)
        xd[...] = nn(gated, wo[...])
        for b in range(NC):
            pj_send[b, at, :] = xd[:, b * B : b * B + B].astype(BF16)
        return carry

    lax.fori_loop(0, 2, att_step, 0)
    for m in range(6):
        pocopy(1, m, True).wait_recv()
    prcopy(False).start()

    for b in range(NC):
        heads = [acc[h * B : h * B + B, b * B : b * B + B] for h in range(2)]
        for n in range(NS):
            both = jnp.concatenate([v[n * Q : n * Q + Q] for v in heads], axis=0)
            g_send[n, b, :, 0:B] = both.astype(BF16)

    def gcopy(d, inward):
        return samp_copy(lambda n: g_send.at[n], lambda n: g_recv.at[n], g_ss, g_rs, d, inward)

    for d in range(1, NS):
        gcopy(d, False).start()

    def pycopy(d, x):
        src = pj_send.at[x * 4 + around(d)]
        return copy(src, py_recv.at[d - 1, x], py_ss.at[d, x], py_rs.at[d, x], col=xh * 4 + around(d))

    pys = [(d, x) for d in range(1, 4) for x in range(2)]
    for d, x in pys:
        pycopy(d, x).start()
    g_recv[samp] = g_send[samp]
    for d in range(1, NS):
        gcopy(d, True).wait_recv()

    def sum_step(b, carry):
        total = g_recv[0, b].astype(F32)
        for n in range(1, NS):
            total = total + g_recv[n, b].astype(F32)
        sg[b] = total.astype(BF16)
        return carry

    lax.fori_loop(0, NC, sum_step, 0)

    def ccopy(d, inward):
        there, here = (col + d) % NC, (col + NC - d) % NC
        return copy(sg.at[there], cg.at[here if inward else col], c_ss.at[d], c_rs.at[d], col=there)

    for d in range(1, NC):
        ccopy(d, False).start()
    cg[col] = sg[col]

    for d, x in pys:
        pycopy(d, x).wait_recv()

    def py_step(s, carry):
        at = pl.ds(pl.multiple_of(s * B, B), B)

        def total(x):
            v = pj_send[x * 4 + yy, at, :].astype(F32)
            for d in range(3):
                v = v + py_recv[d, x, at, :].astype(F32)
            return v

        px_own[at, :] = total(xh) + tokens[at, :].astype(F32)
        px_send[at, :] = total(1 - xh).astype(BF16)
        return carry

    lax.fori_loop(0, 4, py_step, 0)
    px = copy(px_send, px_recv, px_ss, px_rs, col=xp)
    px.start()
    for d in range(1, NC):
        ccopy(d, True).wait_recv()
    for c in range(NC):
        cg_f[c * 48 : c * 48 + 48, :] = cg[c].astype(F32)
    for i in range(Q):
        bg[samp, i] = cg_f[pl.ds(i, 16, stride=Q), :].astype(BF16)

    def bcopy(d, inward):
        return samp_copy(lambda _: bg.at[samp], lambda n: bg.at[n], b_ss, b_rs, d, inward)

    for d in range(1, NS):
        bcopy(d, False).start()
    px.wait_recv()
    tokens_out[...] = (px_own[...] + px_recv[...].astype(F32)).astype(BF16)
    for m in range(6):
        pocopy(0, m, True).wait_recv()
    prcopy(True).wait_recv()
    for d in range(1, NS):
        bcopy(d, True).wait_recv()

    for c in [slab_x, px, prcopy(False)] + slab_own + slab_on:
        c.wait_send()
    for d, x in pys:
        pycopy(d, x).wait_send()
    for m in range(6):
        for k in range(2):
            pocopy(k, m, False).wait_send()

    for n in range(CH):
        for s in range(2):
            for t in range(1, 5):
                rcopy(n, t, s, False).wait_send()
        for s in y_ways(n):
            ycopy(n, s).wait_send()
        if n < CH - 2:
            for s in range(2):
                zcopy(n, s).wait_send()
        for d in range(1, NS):
            tcopy(n, d, False).wait_send()
        xcopy(n).wait_send()
    for t in range(1, 5):
        for s in range(2):
            for c in kvcopies(t, s, False):
                c.wait_send()
    for d in range(1, NC):
        hcopy(d, False).wait_send()
        ccopy(d, False).wait_send()
    for d in range(1, NS):
        hgcopy(d, False).wait_send()
        gcopy(d, False).wait_send()
        bcopy(d, False).wait_send()


def split(v):
    high = v.astype(BF16)
    rest = v - high.astype(F32)
    mid = rest.astype(BF16)
    return high, mid, (rest - mid.astype(F32)).astype(BF16)


def finish(pair_rows, token_rows, bg, lnb, wpbt, pair_out, tokens_out, pair_grad):
    @pl.when(pl.program_id(0) == 0)
    def _():
        tokens_out[...] = token_rows[...]

    pair_out[...] = pair_rows[...]
    ones = mean_weights()
    weights = wpbt[...].astype(F32) * lnb[...]
    weights = weights - jnp.mean(weights, axis=-1, keepdims=True)
    weights = jnp.concatenate(split(weights), axis=0)
    empty = jnp.zeros((48, 128), BF16)
    weights = jnp.concatenate(
        [jnp.concatenate([weights, empty], axis=1), jnp.concatenate([empty, weights], axis=1)], axis=0
    )
    for e in range(4):
        at = slice(e * 4 * B, e * 4 * B + 4 * B)
        even, odd = [
            jnp.concatenate([bg[e * 4 + n], bg[e * 4 + 2 + n]], axis=1) for n in range(2)
        ]
        both = tn(jnp.concatenate([even] * 3 + [odd] * 3, axis=0), weights)
        scaled = jnp.concatenate(
            [both[0:B, :128], both[0:B, 128:], both[128 : 128 + B, :128], both[128 : 128 + B, 128:]], axis=0
        )
        center, inv = centered(pair_rows[at, :], ones)
        unit = center * inv
        pair_grad[at, :] = inv * (scaled - unit * row_means((scaled * unit).astype(BF16), ones))


def per_device(
    pair, crop_mask, w_agate, w_aval, w_bgate, w_bval, w_outgate, w_outproj, ln_pair,
    w_trans_gate, w_trans_up, w_trans_down, ln_bias, w_pairbias, tokens, ln_token,
    w_query, w_key, w_value, w_gate, w_output, cotangent,
):
    wpbt = w_pairbias.T
    lnb = ln_bias.reshape(1, 128)
    args = (
        pair.reshape(B * B, 128), crop_mask, crop_mask.reshape(6, 128),
        w_agate, w_aval, w_bgate, w_bval, ln_pair.reshape(1, 128), w_outgate, w_outproj,
        w_trans_gate, w_trans_up, w_trans_down, lnb, wpbt,
        tokens.reshape(4 * B, B), cotangent.reshape(4 * B, B), ln_token.reshape(6, 128),
        w_query.T, w_key.T, w_value.T, w_gate.T, w_output,
    )
    vm = pltpu.VMEM
    dma = pltpu.SemaphoreType.DMA
    scratch = [
        vm((4, 128, 128), BF16),
        vm((128, 128), BF16),
        vm((2 * B, NC * B), F32),
        vm((2 * B, NC * B), F32),
        vm((256, 256), BF16),
        vm((6 * CR, 128), BF16),
        vm((CR, 128), F32),
        vm((G * B, 128), F32),
        vm((G * B, 128), F32),
        vm((CH, 3 * B, 256), BF16),
        vm((CH, 2 * B, 128), BF16),
        vm((CH, NR, RC + 32, 128), BF16),
        vm((CH, 4, 2, RC, 128), BF16),
        vm((CH, 2, 2, RC // 2, 128), BF16),
        vm((CH, 3, 2, RC, 128), BF16),
        vm((CH, RC, 128), F32),
        vm((CH, RC, 128), BF16),
        vm((CH, RC, 128), BF16),
        vm((NC, 2, 4 * B, B), BF16),
        vm((4 * B, B), BF16),
        vm((4, NR * B, B), BF16),
        vm((4, NR * B, B), BF16),
        vm((4 * B, B), F32),
        vm((4 * B, B), BF16),
        vm((NS, CH, 2, 48, 128), BF16),
        vm((NS, CH, 2, 48, 128), BF16),
        vm((64 * 48, 128), F32),
        vm((16 * Q, 128), F32),
        vm((NC, 48, 128), BF16),
        vm((NC, NS, 48, 128), BF16),
        vm((2 * B, NC * B), F32),
        vm((4, 2 * B, NC * B), F32),
        vm((4, 2 * B, NC * B), F32),
        vm((2 * B, NC * B), F32),
        vm((NS, NC, 48, 128), BF16),
        vm((NS, NC, 48, 128), BF16),
        vm((NC, 4 * B, B), BF16),
        vm((3, 2, 4 * B, B), BF16),
        vm((4 * B, B), F32),
        vm((4 * B, B), BF16),
        vm((4 * B, B), BF16),
        vm((NC, 48, 128), BF16),
        vm((NC, 48, 128), BF16),
        vm((16 * Q, 128), F32),
    ]
    sems = [(7,)] * 2 + [(CH, 2, 4)] * 2 + [(CH, 2)] * 2 + [(CH, 3)] * 2 + [(CH,)] * 2
    sems += [(2, 2, 4)] * 2 + [(CH, 4)] * 2 + [(8,)] * 2 + [(4,)] * 2 + [(2, 6)] * 2 + [None] * 2
    sems += [(4, 2)] * 2 + [None] * 2 + [(4,)] * 2 + [(8,)] * 2 + [(4,)] * 2
    scratch += [dma if s is None else dma(s) for s in sems]
    spec = pl.BlockSpec(memory_space=pltpu.VMEM)
    specs = [spec] * len(args)
    specs[1] = pl.BlockSpec(memory_space=pltpu.SMEM)
    pair_rows, token_rows, bg = pl.pallas_call(
        kernel,
        out_shape=(
            jax.ShapeDtypeStruct((B * B, 128), BF16),
            jax.ShapeDtypeStruct((4 * B, B), BF16),
            jax.ShapeDtypeStruct((NS, Q, 16, 128), BF16),
        ),
        in_specs=specs,
        out_specs=(spec,) * 3,
        scratch_shapes=scratch,
        compiler_params=pltpu.CompilerParams(
            collective_id=0, has_side_effects=True, vmem_limit_bytes=56 * 1024 * 1024
        ),
    )(*args)
    rows = pl.BlockSpec((16 * B, 128), lambda i: (i, 0))
    whole = pl.BlockSpec((4 * B, B), lambda i: (0, 0))
    outs = pl.pallas_call(
        finish,
        grid=(B // 16,),
        out_shape=(
            jax.ShapeDtypeStruct((B * B, 128), BF16),
            jax.ShapeDtypeStruct((4 * B, B), BF16),
            jax.ShapeDtypeStruct((B * B, 128), F32),
        ),
        in_specs=[
            rows,
            whole,
            pl.BlockSpec((16, 16, 128), lambda i: (i, 0, 0)),
            pl.BlockSpec((1, 128), lambda i: (0, 0)),
            pl.BlockSpec((16, 128), lambda i: (0, 0)),
        ],
        out_specs=(rows, whole, rows),
    )(pair_rows, token_rows, bg.reshape(B, 16, 128), lnb, wpbt)
    return (
        outs[0].reshape(B, B, 128),
        outs[1].reshape(4, B, B),
        outs[2].reshape(B, B, 128),
    )


def solution(mesh):
    placed = (
        P("row", "col", None),
        P(), P(), P(), P(), P(), P(), P(), P(), P(), P(), P(), P(), P(),
        P("samp", "row", "col"),
        P(),
        P(None, "col"),
        P(None, "col"),
        P(None, "col"),
        P(None, "col"),
        P("col", None),
        P("samp", "row", "col"),
    )
    return jax.shard_map(
        per_device,
        mesh=mesh,
        in_specs=placed,
        out_specs=(P("row", "col", None), P("samp", "row", "col"), P("row", "col", None)),
        check_vma=False,
    )
```

```python
import math

import jax
import jax.numpy as jnp
from jax import lax
from jax.experimental import pallas as pl
from jax.experimental.pallas import tpu as pltpu
from jax.sharding import PartitionSpec as P

F32 = jnp.float32
BF16 = jnp.bfloat16
MESH = pl.DeviceIdType.MESH
NR = 8
NC = 8
NS = 4
B = 96
Q = 24
G = 24
CH = 8
RC = 3 * B
CR = 16 * B + 32


def nt(a, b):
    return lax.dot_general(a, b, (((1,), (1,)), ((), ())), preferred_element_type=F32)


def nn(a, b):
    return lax.dot_general(a, b, (((1,), (0,)), ((), ())), preferred_element_type=F32)


def tn(a, b):
    return lax.dot_general(a, b, (((0,), (0,)), ((), ())), preferred_element_type=F32)


def row_means(values, ones):
    half = values.shape[0] // 2
    out = nn(jnp.concatenate([values[:half], values[half:]], axis=1), ones)
    return jnp.concatenate([out[:, :128], out[:, 128:]], axis=0)


def centered(values, ones):
    center = values.astype(F32) - row_means(values, ones)
    return center, lax.rsqrt(row_means((center * center).astype(BF16), ones) + 1e-05)


def normalize(values, ones):
    center, inv = centered(values, ones)
    return center * inv


def mean_weights():
    first = lax.broadcasted_iota(jnp.int32, (256, 256), 0) < 128
    second = lax.broadcasted_iota(jnp.int32, (256, 256), 1) < 128
    return jnp.where(first == second, 1.0 / 128.0, 0.0).astype(BF16)


def kernel(
    pair, crop_s, crop_v, w_ag, w_av, w_bg, w_bv, lnp, w_outgate, w_outproj, w_tg, w_tu, w_td,
    lnb, wpbt, tokens, cot, lnt, wq, wk, wv, wg, wo,
    pair_out, tokens_out, bg,
    wt, w_op, xd, cd,
    ones_ref, normed, made, lf, rf, lm2, lm1, rslab, part, z_recv, y_recv, own_sum, x_send, x_recv, slab, q_s, kslab,
    vslab, gate_s, datt_s, tri_send, tri_recv, tri_f, hb_f, hb_send, hb, bias, raw, d_probs, acc, g_send, g_recv,
    pj_send, py_recv, px_own, px_send, px_recv, sg, cg, cg_f,
    slab_ss, slab_rs, ring_ss, ring_rs, z_ss, z_rs, y_ss, y_rs, x_ss, x_rs,
    kv_ss, kv_rs, t_ss, t_rs, h_ss, h_rs, hg_ss, hg_rs, po_ss, po_rs, pr_ss, pr_rs,
    py_ss, py_rs, px_ss, px_rs, g_ss, g_rs, c_ss, c_rs, b_ss, b_rs,
):
    row = lax.axis_index("row")
    col = lax.axis_index("col")
    samp = lax.axis_index("samp")
    xh = col // 4
    yy = col % 4
    xp = (1 - xh) * 4 + yy
    ones_ref[...] = mean_weights()
    ones = ones_ref[...]
    right = (row + 1) % NR
    left = (row + NR - 1) % NR

    def copy(src, dst, ss, rs, **where):
        return pltpu.make_async_remote_copy(
            src_ref=src, dst_ref=dst, send_sem=ss, recv_sem=rs, device_id=where, device_id_type=MESH
        )

    barrier = pltpu.get_barrier_semaphore()
    for d in range(1, NC):
        pl.semaphore_signal(barrier, inc=1, device_id={"col": (col + d) % NC}, device_id_type=MESH)
    for d in range(1, NR):
        pl.semaphore_signal(barrier, inc=1, device_id={"row": (row + d) % NR}, device_id_type=MESH)
    for d in range(1, NS):
        pl.semaphore_signal(
            barrier, inc=1, device_id={"samp": (samp + d) % NS}, device_id_type=MESH
        )

    def around(d):
        return (yy + d) % 4

    def slab_copy(block, k, there):
        at = slab.at[block]
        return copy(at, at, slab_ss.at[k], slab_rs.at[k], col=there)

    slab_own = [slab_copy(col, d, xh * 4 + around(d)) for d in range(1, 4)]
    slab_own_in = [slab_copy(xh * 4 + around(4 - d), d, xh * 4 + around(d)) for d in range(1, 4)]
    slab_x = slab_copy(col, 0, xp)
    slab_x_in = slab_copy(xp, 0, xp)
    slab_on = [slab_copy(xp, 3 + d, xh * 4 + around(d)) for d in range(1, 4)]
    slab_on_in = [
        slab_copy((1 - xh) * 4 + around(4 - d), 3 + d, xh * 4 + around(d)) for d in range(1, 4)
    ]
    slab[col, 0] = tokens[...]
    slab[col, 1] = cot[...]

    for n, w in enumerate((w_ag, w_av, w_bg, w_bv)):
        wt[n] = w[...].astype(F32).T.astype(BF16)
    wp = jnp.concatenate([wt[n, pl.ds(pl.multiple_of(samp * 32, 32), 32), :] for n in range(4)], axis=0)
    tri_f[0:128, :] = w_outproj[...].astype(F32)
    w_op[...] = jnp.concatenate(
        [tri_f[pl.ds(0, 64, stride=2), :], tri_f[pl.ds(1, 64, stride=2), :]], axis=0
    ).astype(BF16)
    crop = jnp.concatenate([crop_v[i : i + 1, :] for i in range(6)], axis=1).astype(F32)
    token_gain = jnp.concatenate([lnt[i : i + 1, :] for i in range(6)], axis=1)
    keep_cols = jnp.zeros((1, B), F32)
    for b in range(NC):
        keep_cols = jnp.where(col == b, crop[:, b * B : b * B + B], keep_cols)
    keep_cols = jnp.concatenate([keep_cols, jnp.zeros((1, 32), F32)], axis=1)

    for m in range(6):
        normed[m * CR + 16 * B : m * CR + CR, :] = jnp.zeros((32, 128), BF16)
    lane = lax.broadcasted_iota(jnp.int32, (8, 128), 1)
    wide = lane < B

    def norm_chunk(m):
        src = pl.ds(pl.multiple_of(m * (16 * B), 16 * B), 16 * B)
        dst = pl.ds(pl.multiple_of(m * CR, 32), 16 * B)
        normed[dst, :] = (normalize(pair[src, :], ones) * lnp[...]).astype(BF16)

    def edge_chunk(m):
        made[...] = nt(normed[pl.ds(pl.multiple_of(m * CR, 32), CR), :], wp)
        for e in range(16):
            i = m * 16 + e
            o = made[e * B : e * B + 128, :].T
            kept = keep_cols * crop_s[row * B + i].astype(F32)
            for first, dest in ((0, lf), (64, rf)):
                edge = jax.nn.sigmoid(o[first : first + 32]) * o[first + 32 : first + 64] * kept
                tail = edge[24:32]
                for q in range(3):
                    packed = jnp.where(wide, edge[8 * q : 8 * q + 8], pltpu.roll(tail, 96 - 32 * q, 1))
                    dest[pl.ds(i + 8 * B * q, 8, stride=B), :] = packed

    norm_chunk(0)

    pl.semaphore_wait(barrier, NC + NR + NS - 3)
    for c in [slab_x] + slab_own:
        c.start()

    def front_step(m, carry):
        edge_chunk(m)
        norm_chunk(m + 1)
        return carry

    lax.fori_loop(0, 5, front_step, 0)
    edge_chunk(5)
    slab_x_in.wait_recv()
    for c in slab_on:
        c.start()
    own = lax.broadcasted_iota(jnp.int32, (B, 128), 1) < B
    carriers = [(n, k, pl.ds((k * 8 + n) * B, B)) for n in range(CH) for k in range(3)]
    for n, k, at in carriers:
        rslab[n, row, k * B : k * B + B, :] = rf[at, :].astype(BF16)
    for n in range(CH):
        rslab[n, :, RC : RC + 32, :] = jnp.zeros((NR, 32, 128), BF16)

    ring = (right, left)
    step_of = (-1, 1)

    def rcopy(n, t, s, inward):
        back = t if inward else t - 1
        block = (row + NR + step_of[s] * back) % NR
        rows = pl.ds(0, RC) if t < 4 else pl.ds(s * (RC // 2), RC // 2)
        at = rslab.at[n, block, rows]
        return copy(at, at, ring_ss.at[n, s, t - 1], ring_rs.at[n, s, t - 1], row=ring[s])

    for n in range(3):
        for s in range(2):
            rcopy(n, 1, s, False).start()
    empty = jnp.zeros((B, 128), BF16)
    for n, k, at in carriers:
        edge = lf[at, :]
        mine = jnp.where(own, edge, 0.0).astype(BF16)
        rest = jnp.where(own, 0.0, edge).astype(BF16)
        if k < 2:
            lm2[n, k * B : k * B + B, k * 128 : k * 128 + 128] = mine
            lm2[n, k * B : k * B + B, (1 - k) * 128 : (1 - k) * 128 + 128] = empty
            lm2[n, 2 * B : 3 * B, k * 128 : k * 128 + 128] = rest
        else:
            lm1[n, 0:B, :] = mine
            lm1[n, B : 2 * B, :] = rest

    def token_rows(pair_of):
        at = pl.ds(pair_of * 2 * B, 2 * B)
        x = [slab[b, 0, at, :].astype(F32) for b in range(NC)]
        total = x[0]
        for b in range(1, NC):
            total = total + x[b]
        mean = jnp.sum(total, axis=-1, keepdims=True) * (1.0 / (NC * B))
        x = [v - mean for v in x]
        total = x[0] * x[0]
        for b in range(1, NC):
            total = total + x[b] * x[b]
        inv = lax.rsqrt(jnp.sum(total, axis=-1, keepdims=True) * (1.0 / (NC * B)) + 1e-05)
        for b in range(NC):
            xd[:, b * B : b * B + B] = x[b] * inv
            cd[:, b * B : b * B + B] = slab[b, 1, at, :].astype(F32)

    def token_keys(pair_of):
        normal = (xd[...] * token_gain).astype(BF16)
        tokens_at = pl.ds(pl.multiple_of(row * B, B), B)
        for w, dest in ((wk, kslab), (wv, vslab)):
            out = nt(normal, w[...]).astype(BF16)
            for e in range(2):
                dest[pair_of * 2 + e, tokens_at, :] = out[e * B : e * B + B]

    def token_queries(pair_of):
        at = pl.ds(pair_of * 2 * B, 2 * B)
        normal = (xd[...] * token_gain).astype(BF16)
        q_s[at, :] = nt(normal, wq[...]).astype(BF16)
        gate = jax.nn.sigmoid(nt(normal, wg[...]))
        gate_s[at, :] = gate
        d = nt(cd[...].astype(BF16), wo[...])
        datt_s[at, :] = (d * gate).astype(BF16)

    def products(n, back):
        if back in (0, 4):
            blocks = [(row + back) % NR]
        else:
            blocks = [(row + NR + step * back) % NR for step in (-1, 1)]
        rights = [
            jnp.concatenate([rslab[n, j, q * B : q * B + 128, :] for j in blocks], axis=0)
            for q in range(3)
        ]
        two = nt(lm2[n], jnp.concatenate(rights[:2], axis=1))
        one = nt(lm1[n], rights[2])
        for e, j in enumerate(blocks):
            at = slice(e * 128, e * 128 + 128)
            tops = [two[0:B, at], two[B : 2 * B, at], one[0:B, at]]
            tail = two[2 * B : 3 * B, at] + one[B : 2 * B, at]
            for q in range(3):
                packed = jnp.where(own, tops[q], pltpu.roll(tail, 96 - 32 * q, 1))
                part[n, j % 4, j // 4, q * B : q * B + B, :] = packed.astype(BF16)

    sides = (xh * 4 + (yy + 1) % 4, xh * 4 + (yy + 3) % 4)

    def zcopy(n, s):
        src = part.at[n, (yy + 2) % 4, :, pl.ds(s * (RC // 2), RC // 2)]
        return copy(src, z_recv.at[n, s], z_ss.at[n, s], z_rs.at[n, s], col=sides[s])

    def ycopy(n, s):
        there = (yy + (1, 3, 2)[s]) % 4
        return copy(
            part.at[n, there], y_recv.at[n, s], y_ss.at[n, s], y_rs.at[n, s], col=xh * 4 + there
        )

    def y_ways(n):
        return (0, 1, 2) if n >= CH - 2 else (0, 1)

    def z_start(n):
        for s in range(2):
            zcopy(n, s).start()

    def y_start(n):
        for s in range(2):
            zcopy(n, s).wait_recv()
            for x in range(2):
                at = pl.ds(s * (RC // 2), RC // 2)
                more = z_recv[n, s, x].astype(F32)
                there = (yy + 1 + 2 * s) % 4
                part[n, there, x, at, :] = (part[n, there, x, at, :].astype(F32) + more).astype(BF16)
            ycopy(n, s).start()

    def y_sum(n):
        for s in y_ways(n):
            ycopy(n, s).wait_recv()

        def one(k, carry):
            at = pl.ds(pl.multiple_of(k * B, B), B)

            def total(x):
                v = part[n, yy, x, at, :].astype(F32)
                for s in y_ways(n):
                    v = v + y_recv[n, s, x, at, :].astype(F32)
                return v

            own_sum[n, at, :] = total(xh)
            x_send[n, at, :] = total(1 - xh).astype(BF16)
            return carry

        lax.fori_loop(0, 3, one, 0)
        xcopy(n).start()

    def xcopy(n):
        return copy(x_send.at[n], x_recv.at[n], x_ss.at[n], x_rs.at[n], col=xp)

    def samp_copy(src_of, dst_of, ss, rs, d, inward):
        there, here = (samp + d) % NS, (samp + NS - d) % NS
        return copy(src_of(there), dst_of(here if inward else samp), ss.at[d], rs.at[d], samp=there)

    def tcopy(n, d, inward):
        return samp_copy(
            lambda m: tri_send.at[m, n], lambda m: tri_recv.at[m, n], t_ss.at[n], t_rs.at[n], d, inward
        )

    lane96 = lax.broadcasted_iota(jnp.int32, (B, 128), 1)

    def triangle(n):
        xcopy(n).wait_recv()
        c = []
        for q in range(3):
            at = pl.ds(q * B, B)
            c.append(own_sum[n, at, :] + x_recv[n, at, :].astype(F32))
        tail = jnp.where(
            lane96 < 32,
            pltpu.roll(c[0], 32, 1),
            jnp.where(lane96 < 64, pltpu.roll(c[1], 64, 1), pltpu.roll(c[2], 96, 1)),
        )
        c.append(tail)
        for h in range(2):
            for m in range(NS):
                both = [v[m * Q : m * Q + Q] for v in c[2 * h : 2 * h + 2]]
                tri_send[m, n, h] = jnp.concatenate(both, axis=0).astype(BF16)
        for d in range(1, NS):
            tcopy(n, d, False).start()

    def kvcopies(t, s, inward):
        back = t if inward else t - 1
        block = (row + NR + step_of[s] * back) % NR
        rows = pl.ds(pl.multiple_of(block * B, B), B)
        both = [(0, kslab), (1, vslab)]
        return [
            copy(v.at[:, rows, :], v.at[:, rows, :], kv_ss.at[n, s, t - 1], kv_rs.at[n, s, t - 1], row=ring[s])
            for n, v in (both if t < 4 else both[s : s + 1])
        ]

    def ring_slot(n, t):
        for s in range(2):
            if t > 1:
                rcopy(n, t - 1, s, True).wait_recv()
            if t < 5 and not (t == 1 and n < 3):
                rcopy(n, t, s, False).start()
        products(n, t - 1)
        if t == 5 and n >= CH - 2:
            for s in y_ways(n):
                ycopy(n, s).start()
        elif t == 5:
            z_start(n)

    def kv_slot(t):
        for s in range(2):
            if t > 1:
                for c in kvcopies(t - 1, s, True):
                    c.wait_recv()
            if t < 5:
                for c in kvcopies(t, s, False):
                    c.start()

    def token_wait(_):
        for c in slab_own_in + slab_on_in:
            c.wait_recv()

    for k in range(CH + 6):
        between = []
        for n in range(CH):
            t = k - n + 1 + (n >= CH - 2)
            if t == 8:
                between.append((triangle, n))
            elif t == 7:
                between.append((y_sum, n))
            elif t == 6 and n < CH - 2:
                between.append((y_start, n))
        if k == 4:
            between.append((token_wait, 0))
        if k in (4, 5):
            between += [(f, k - 4) for f in (token_rows, token_keys, token_queries)]
        for n in range(CH):
            if 1 <= k - n + 1 <= 5:
                ring_slot(n, k - n + 1)
                if between:
                    f, arg = between.pop(0)
                    f(arg)
        if 1 <= k - CH + 1 <= 5:
            kv_slot(k - CH + 1)
        for f, arg in between:
            f(arg)

    def unpack(m):
        for n in range(CH):
            for h in range(2):
                both = tri_recv[m, n, h].astype(F32)
                for e in range(2):
                    c = (2 * h + e) * 8 + n
                    r0 = pl.multiple_of(m * 768, 768) + c // 2 * 48 + c % 2 * Q
                    tri_f[pl.ds(r0, Q), :] = both[e * Q : e * Q + Q]

    tri_recv[samp] = tri_send[samp]
    unpack(samp)
    for d in range(1, NS):
        for n in range(CH):
            tcopy(n, d, True).wait_recv()
        unpack((samp + NS - d) % NS)

    row0 = samp * Q
    sib, oth = samp + 1 - 2 * (samp % 2), (samp + 2) % NS
    diag = (sib + 2) % NS

    def part_of(n, m):
        return pair_out.at[pl.ds(pl.multiple_of((n * Q + m * 4) * B, 4 * B), 4 * B)]

    def pocopy(k, m, inward):
        there = (sib, oth)[k]
        at = part_of(there if inward else samp, m)
        return copy(at, at, po_ss.at[k, m], po_rs.at[k, m], samp=there)

    def prcopy(inward):
        n = diag if inward else oth
        at = pair_out.at[pl.ds(pl.multiple_of(n * (Q * B), Q * B), Q * B)]
        return copy(at, at, pr_ss, pr_rs, samp=sib)


    def post_rows(m):
        cols = []
        for e in range(4):
            i = m * 4 + e
            cols.append(
                jnp.concatenate(
                    [tri_f[pl.ds(i, 64, stride=48), :], tri_f[pl.ds(Q + i, 64, stride=48), :]], axis=0
                )
            )
        t = jnp.concatenate(cols, axis=1)
        center = t - jnp.mean(t, axis=0, keepdims=True)
        t = center * lax.rsqrt(jnp.mean(center * center, axis=0, keepdims=True) + 1e-05)
        proj = tn(t.astype(BF16), w_op[...])
        proj = jnp.concatenate([proj[e * 128 : e * 128 + B] for e in range(4)], axis=0)
        first = row0 + m * 4
        at = pl.ds(pl.multiple_of(first * B, 4 * B), 4 * B)
        norm_at = pl.ds(pl.multiple_of(first // 16 * CR + first % 16 * B, 32), 4 * B)
        gate = jax.nn.sigmoid(nn(normed[norm_at, :], w_outgate[...]))
        updated = (pair[at, :].astype(F32) + gate * proj).astype(BF16)
        trans_in = normalize(updated, ones).astype(BF16)
        total = updated.astype(F32)
        for n in range(2):
            a = nn(trans_in, w_tg[:, n * 256 : n * 256 + 256])
            u = nn(trans_in, w_tu[:, n * 256 : n * 256 + 256])
            hidden = (a * jax.nn.sigmoid(a) * u).astype(BF16)
            total = total + nn(hidden, w_td[n * 256 : n * 256 + 256, :])
        out = total.astype(BF16)
        bias_in = (normalize(out, ones) * lnb[...]).astype(BF16)
        return at, out, nt(wpbt[...], bias_in)

    def post_step(m, carry):
        done = [post_rows(m * 2 + n) for n in range(2)]
        for n, (at, out, heads) in enumerate(done):
            pair_out[at, :] = out
            for e in range(4):
                hb_f[pl.ds((m * 2 + n) * 4 + e, 16, stride=Q), 0:B] = heads[:, e * B : e * B + B]
        for n in range(2):
            for k in range(2):
                pocopy(k, m * 2 + n, False).start()
        return carry

    lax.fori_loop(0, Q // 8, post_step, 0)
    for c in range(NC):
        hb_send[c] = hb_f[c * 48 : c * 48 + 48, :].astype(BF16)

    def hcopy(d, inward):
        there, here = (col + d) % NC, (col + NC - d) % NC
        dst = hb.at[here if inward else col, samp]
        return copy(hb_send.at[there], dst, h_ss.at[d], h_rs.at[d], col=there)

    for d in range(1, NC):
        hcopy(d, False).start()
    hb[col, samp] = hb_send[col]

    feature = lax.broadcasted_iota(jnp.int32, (1, B), 1)
    head_masks = [(feature < 48).astype(F32), (feature >= 48).astype(F32)]
    scale = 1.0 / math.sqrt(48)

    def per_head(v):
        return jnp.concatenate([v * m.astype(BF16) for m in head_masks], axis=0)

    def before_bias(s):
        at = slice(s * B, s * B + B)
        raw[s] = nt(per_head(q_s[at, :]), kslab[s]) * scale
        d_probs[s] = nt(per_head(datt_s[at, :]), vslab[s])

    before_bias(0)
    before_bias(1)
    for d in range(1, NC):
        hcopy(d, True).wait_recv()

    def hgcopy(d, inward):
        return samp_copy(lambda _: hb.at[:, samp], lambda n: hb.at[:, n], hg_ss, hg_rs, d, inward)

    for d in range(1, NS):
        hgcopy(d, False).start()
    before_bias(2)
    before_bias(3)
    for d in range(1, NS):
        hgcopy(d, True).wait_recv()

    for b in range(NC):
        key_mask = (crop[:, b * B : b * B + B] - 1.0) * 10000.0
        quarters = [hb[b, n].astype(F32) for n in range(NS)]
        for h in range(2):
            whole = jnp.concatenate([v[h * Q : h * Q + Q, 0:B] for v in quarters], axis=0)
            bias[h * B : h * B + B, b * B : b * B + B] = whole + key_mask
    acc[...] = jnp.zeros((2 * B, NC * B), F32)
    def att_rows(s):
        at = pl.ds(pl.multiple_of(s * B, B), B)
        scores = raw[s] + bias[...]
        shifted = jnp.exp(scores - jnp.max(scores, axis=-1, keepdims=True))
        probs = shifted * (1.0 / jnp.sum(shifted, axis=-1, keepdims=True))
        got = nn(probs.astype(BF16), vslab[s])
        delta = jnp.sum(per_head(datt_s[at, :]).astype(F32) * got, axis=-1, keepdims=True)
        attended = got[0:B] * head_masks[0] + got[B : 2 * B] * head_masks[1]
        return (gate_s[at, :] * attended).astype(BF16), probs * (d_probs[s] - delta)

    def att_step(m, carry):
        done = [att_rows(m * 2 + e) for e in range(2)]
        acc[...] = acc[...] + (done[0][1] + done[1][1])
        gated = jnp.concatenate([v for v, _ in done], axis=0)
        at = pl.ds(pl.multiple_of(m * 2 * B, 2 * B), 2 * B)
        xd[...] = nn(gated, wo[...])
        for b in range(NC):
            pj_send[b, at, :] = xd[:, b * B : b * B + B].astype(BF16)
        return carry

    lax.fori_loop(0, 2, att_step, 0)
    for m in range(6):
        pocopy(1, m, True).wait_recv()
    prcopy(False).start()

    for b in range(NC):
        heads = [acc[h * B : h * B + B, b * B : b * B + B] for h in range(2)]
        for n in range(NS):
            both = jnp.concatenate([v[n * Q : n * Q + Q] for v in heads], axis=0)
            g_send[n, b, :, 0:B] = both.astype(BF16)

    def gcopy(d, inward):
        return samp_copy(lambda n: g_send.at[n], lambda n: g_recv.at[n], g_ss, g_rs, d, inward)

    for d in range(1, NS):
        gcopy(d, False).start()

    def pycopy(d, x):
        src = pj_send.at[x * 4 + around(d)]
        return copy(src, py_recv.at[d - 1, x], py_ss.at[d, x], py_rs.at[d, x], col=xh * 4 + around(d))

    pys = [(d, x) for d in range(1, 4) for x in range(2)]
    for d, x in pys:
        pycopy(d, x).start()
    g_recv[samp] = g_send[samp]
    for d in range(1, NS):
        gcopy(d, True).wait_recv()

    def sum_step(b, carry):
        total = g_recv[0, b].astype(F32)
        for n in range(1, NS):
            total = total + g_recv[n, b].astype(F32)
        sg[b] = total.astype(BF16)
        return carry

    lax.fori_loop(0, NC, sum_step, 0)

    def ccopy(d, inward):
        there, here = (col + d) % NC, (col + NC - d) % NC
        return copy(sg.at[there], cg.at[here if inward else col], c_ss.at[d], c_rs.at[d], col=there)

    for d in range(1, NC):
        ccopy(d, False).start()
    cg[col] = sg[col]

    for d, x in pys:
        pycopy(d, x).wait_recv()

    def py_step(s, carry):
        at = pl.ds(pl.multiple_of(s * B, B), B)

        def total(x):
            v = pj_send[x * 4 + yy, at, :].astype(F32)
            for d in range(3):
                v = v + py_recv[d, x, at, :].astype(F32)
            return v

        px_own[at, :] = total(xh) + tokens[at, :].astype(F32)
        px_send[at, :] = total(1 - xh).astype(BF16)
        return carry

    lax.fori_loop(0, 4, py_step, 0)
    px = copy(px_send, px_recv, px_ss, px_rs, col=xp)
    px.start()
    for d in range(1, NC):
        ccopy(d, True).wait_recv()
    for c in range(NC):
        cg_f[c * 48 : c * 48 + 48, :] = cg[c].astype(F32)
    for i in range(Q):
        bg[samp, i] = cg_f[pl.ds(i, 16, stride=Q), :].astype(BF16)

    def bcopy(d, inward):
        return samp_copy(lambda _: bg.at[samp], lambda n: bg.at[n], b_ss, b_rs, d, inward)

    for d in range(1, NS):
        bcopy(d, False).start()
    px.wait_recv()
    tokens_out[...] = (px_own[...] + px_recv[...].astype(F32)).astype(BF16)
    for m in range(6):
        pocopy(0, m, True).wait_recv()
    prcopy(True).wait_recv()
    for d in range(1, NS):
        bcopy(d, True).wait_recv()

    for c in [slab_x, px, prcopy(False)] + slab_own + slab_on:
        c.wait_send()
    for d, x in pys:
        pycopy(d, x).wait_send()
    for m in range(6):
        for k in range(2):
            pocopy(k, m, False).wait_send()

    for n in range(CH):
        for s in range(2):
            for t in range(1, 5):
                rcopy(n, t, s, False).wait_send()
        for s in y_ways(n):
            ycopy(n, s).wait_send()
        if n < CH - 2:
            for s in range(2):
                zcopy(n, s).wait_send()
        for d in range(1, NS):
            tcopy(n, d, False).wait_send()
        xcopy(n).wait_send()
    for t in range(1, 5):
        for s in range(2):
            for c in kvcopies(t, s, False):
                c.wait_send()
    for d in range(1, NC):
        hcopy(d, False).wait_send()
        ccopy(d, False).wait_send()
    for d in range(1, NS):
        hgcopy(d, False).wait_send()
        gcopy(d, False).wait_send()
        bcopy(d, False).wait_send()


def split(v):
    high = v.astype(BF16)
    rest = v - high.astype(F32)
    mid = rest.astype(BF16)
    return high, mid, (rest - mid.astype(F32)).astype(BF16)


def finish(pair_rows, token_rows, bg, lnb, wpbt, pair_out, tokens_out, pair_grad):
    @pl.when(pl.program_id(0) == 0)
    def _():
        tokens_out[...] = token_rows[...]

    pair_out[...] = pair_rows[...]
    ones = mean_weights()
    weights = wpbt[...].astype(F32) * lnb[...]
    weights = weights - jnp.mean(weights, axis=-1, keepdims=True)
    weights = jnp.concatenate(split(weights), axis=0)
    empty = jnp.zeros((48, 128), BF16)
    weights = jnp.concatenate(
        [jnp.concatenate([weights, empty], axis=1), jnp.concatenate([empty, weights], axis=1)], axis=0
    )
    for e in range(4):
        at = slice(e * 4 * B, e * 4 * B + 4 * B)
        even, odd = [
            jnp.concatenate([bg[e * 4 + n], bg[e * 4 + 2 + n]], axis=1) for n in range(2)
        ]
        both = tn(jnp.concatenate([even] * 3 + [odd] * 3, axis=0), weights)
        scaled = jnp.concatenate(
            [both[0:B, :128], both[0:B, 128:], both[128 : 128 + B, :128], both[128 : 128 + B, 128:]], axis=0
        )
        center, inv = centered(pair_rows[at, :], ones)
        unit = center * inv
        pair_grad[at, :] = inv * (scaled - unit * row_means((scaled * unit).astype(BF16), ones))


def per_device(
    pair, crop_mask, w_agate, w_aval, w_bgate, w_bval, w_outgate, w_outproj, ln_pair,
    w_trans_gate, w_trans_up, w_trans_down, ln_bias, w_pairbias, tokens, ln_token,
    w_query, w_key, w_value, w_gate, w_output, cotangent,
):
    wpbt = w_pairbias.T
    lnb = ln_bias.reshape(1, 128)
    args = (
        pair.reshape(B * B, 128), crop_mask, crop_mask.reshape(6, 128),
        w_agate, w_aval, w_bgate, w_bval, ln_pair.reshape(1, 128), w_outgate, w_outproj,
        w_trans_gate, w_trans_up, w_trans_down, lnb, wpbt,
        tokens.reshape(4 * B, B), cotangent.reshape(4 * B, B), ln_token.reshape(6, 128),
        w_query.T, w_key.T, w_value.T, w_gate.T, w_output,
    )
    vm = pltpu.VMEM
    dma = pltpu.SemaphoreType.DMA
    scratch = [
        vm((4, 128, 128), BF16),
        vm((128, 128), BF16),
        vm((2 * B, NC * B), F32),
        vm((2 * B, NC * B), F32),
        vm((256, 256), BF16),
        vm((6 * CR, 128), BF16),
        vm((CR, 128), F32),
        vm((G * B, 128), F32),
        vm((G * B, 128), F32),
        vm((CH, 3 * B, 256), BF16),
        vm((CH, 2 * B, 128), BF16),
        vm((CH, NR, RC + 32, 128), BF16),
        vm((CH, 4, 2, RC, 128), BF16),
        vm((CH, 2, 2, RC // 2, 128), BF16),
        vm((CH, 3, 2, RC, 128), BF16),
        vm((CH, RC, 128), F32),
        vm((CH, RC, 128), BF16),
        vm((CH, RC, 128), BF16),
        vm((NC, 2, 4 * B, B), BF16),
        vm((4 * B, B), BF16),
        vm((4, NR * B, B), BF16),
        vm((4, NR * B, B), BF16),
        vm((4 * B, B), F32),
        vm((4 * B, B), BF16),
        vm((NS, CH, 2, 48, 128), BF16),
        vm((NS, CH, 2, 48, 128), BF16),
        vm((64 * 48, 128), F32),
        vm((16 * Q, 128), F32),
        vm((NC, 48, 128), BF16),
        vm((NC, NS, 48, 128), BF16),
        vm((2 * B, NC * B), F32),
        vm((4, 2 * B, NC * B), F32),
        vm((4, 2 * B, NC * B), F32),
        vm((2 * B, NC * B), F32),
        vm((NS, NC, 48, 128), BF16),
        vm((NS, NC, 48, 128), BF16),
        vm((NC, 4 * B, B), BF16),
        vm((3, 2, 4 * B, B), BF16),
        vm((4 * B, B), F32),
        vm((4 * B, B), BF16),
        vm((4 * B, B), BF16),
        vm((NC, 48, 128), BF16),
        vm((NC, 48, 128), BF16),
        vm((16 * Q, 128), F32),
    ]
    sems = [(7,)] * 2 + [(CH, 2, 4)] * 2 + [(CH, 2)] * 2 + [(CH, 3)] * 2 + [(CH,)] * 2
    sems += [(2, 2, 4)] * 2 + [(CH, 4)] * 2 + [(8,)] * 2 + [(4,)] * 2 + [(2, 6)] * 2 + [None] * 2
    sems += [(4, 2)] * 2 + [None] * 2 + [(4,)] * 2 + [(8,)] * 2 + [(4,)] * 2
    scratch += [dma if s is None else dma(s) for s in sems]
    spec = pl.BlockSpec(memory_space=pltpu.VMEM)
    specs = [spec] * len(args)
    specs[1] = pl.BlockSpec(memory_space=pltpu.SMEM)
    pair_rows, token_rows, bg = pl.pallas_call(
        kernel,
        out_shape=(
            jax.ShapeDtypeStruct((B * B, 128), BF16),
            jax.ShapeDtypeStruct((4 * B, B), BF16),
            jax.ShapeDtypeStruct((NS, Q, 16, 128), BF16),
        ),
        in_specs=specs,
        out_specs=(spec,) * 3,
        scratch_shapes=scratch,
        compiler_params=pltpu.CompilerParams(
            collective_id=0, has_side_effects=True, vmem_limit_bytes=56 * 1024 * 1024
        ),
    )(*args)
    rows = pl.BlockSpec((16 * B, 128), lambda i: (i, 0))
    whole = pl.BlockSpec((4 * B, B), lambda i: (0, 0))
    outs = pl.pallas_call(
        finish,
        grid=(B // 16,),
        out_shape=(
            jax.ShapeDtypeStruct((B * B, 128), BF16),
            jax.ShapeDtypeStruct((4 * B, B), BF16),
            jax.ShapeDtypeStruct((B * B, 128), F32),
        ),
        in_specs=[
            rows,
            whole,
            pl.BlockSpec((16, 16, 128), lambda i: (i, 0, 0)),
            pl.BlockSpec((1, 128), lambda i: (0, 0)),
            pl.BlockSpec((16, 128), lambda i: (0, 0)),
        ],
        out_specs=(rows, whole, rows),
    )(pair_rows, token_rows, bg.reshape(B, 16, 128), lnb, wpbt)
    return (
        outs[0].reshape(B, B, 128),
        outs[1].reshape(4, B, B),
        outs[2].reshape(B, B, 128),
    )


def solution(mesh):
    placed = (
        P("row", "col", None),
        P(), P(), P(), P(), P(), P(), P(), P(), P(), P(), P(), P(), P(),
        P("samp", "row", "col"),
        P(),
        P(None, "col"),
        P(None, "col"),
        P(None, "col"),
        P(None, "col"),
        P("col", None),
        P("samp", "row", "col"),
    )
    return jax.shard_map(
        per_device,
        mesh=mesh,
        in_specs=placed,
        out_specs=(P("row", "col", None), P("samp", "row", "col"), P("row", "col", None)),
        check_vma=False,
    )
```

```python
import math

import jax
import jax.numpy as jnp
from jax import lax
from jax.experimental import pallas as pl
from jax.experimental.pallas import tpu as pltpu
from jax.sharding import PartitionSpec as P

F32 = jnp.float32
BF16 = jnp.bfloat16
MESH = pl.DeviceIdType.MESH
NR = 8
NC = 8
NS = 4
B = 96
Q = 24
G = 24
CH = 8
RC = 3 * B
CR = 16 * B


def nt(a, b):
    return lax.dot_general(a, b, (((1,), (1,)), ((), ())), preferred_element_type=F32)


def nn(a, b):
    return lax.dot_general(a, b, (((1,), (0,)), ((), ())), preferred_element_type=F32)


def tn(a, b):
    return lax.dot_general(a, b, (((0,), (0,)), ((), ())), preferred_element_type=F32)


def row_means(values, ones):
    half = values.shape[0] // 2
    out = nn(jnp.concatenate([values[:half], values[half:]], axis=1), ones)
    return jnp.concatenate([out[:, :128], out[:, 128:]], axis=0)


def centered(values, ones):
    center = values.astype(F32) - row_means(values, ones)
    return center, lax.rsqrt(row_means((center * center).astype(BF16), ones) + 1e-05)


def normalize(values, ones):
    center, inv = centered(values, ones)
    return center * inv


def mean_weights():
    first = lax.broadcasted_iota(jnp.int32, (256, 256), 0) < 128
    second = lax.broadcasted_iota(jnp.int32, (256, 256), 1) < 128
    return jnp.where(first == second, 1.0 / 128.0, 0.0).astype(BF16)


def kernel(
    pair, crop_s, crop_v, w_ag, w_av, w_bg, w_bv, lnp, w_outgate, w_outproj, w_tg, w_tu, w_td,
    lnb, wpbt, tokens, cot, lnt, wq, wk, wv, wg, wo,
    pair_out, tokens_out, bg,
    wt, w_op, xd, cd,
    ones_ref, normed, made, lf, rf, lm, rslab, part, z_recv, y_recv, own_sum, x_send, x_recv, slab, q_s, kslab,
    vslab, gate_s, datt_s, tri_send, tri_recv, tri_f, hb_f, hb_send, hb, bias, raw, d_probs, acc, g_send, g_recv,
    pj_send, py_recv, px_own, px_send, px_recv, sg, cg, cg_f,
    slab_ss, slab_rs, ring_ss, ring_rs, z_ss, z_rs, y_ss, y_rs, x_ss, x_rs,
    kv_ss, kv_rs, t_ss, t_rs, h_ss, h_rs, hg_ss, hg_rs, po_ss, po_rs, pr_ss, pr_rs,
    py_ss, py_rs, px_ss, px_rs, g_ss, g_rs, c_ss, c_rs, b_ss, b_rs,
):
    row = lax.axis_index("row")
    col = lax.axis_index("col")
    samp = lax.axis_index("samp")
    xh = col // 4
    yy = col % 4
    xp = (1 - xh) * 4 + yy
    ones_ref[...] = mean_weights()
    ones = ones_ref[...]
    right = (row + 1) % NR
    left = (row + NR - 1) % NR

    def copy(src, dst, ss, rs, **where):
        return pltpu.make_async_remote_copy(
            src_ref=src, dst_ref=dst, send_sem=ss, recv_sem=rs, device_id=where, device_id_type=MESH
        )

    barrier = pltpu.get_barrier_semaphore()
    for d in range(1, NC):
        pl.semaphore_signal(barrier, inc=1, device_id={"col": (col + d) % NC}, device_id_type=MESH)
    for d in range(1, NR):
        pl.semaphore_signal(barrier, inc=1, device_id={"row": (row + d) % NR}, device_id_type=MESH)
    for d in range(1, NS):
        pl.semaphore_signal(
            barrier, inc=1, device_id={"samp": (samp + d) % NS}, device_id_type=MESH
        )

    def around(d):
        return (yy + d) % 4

    def slab_copy(block, k, there):
        at = slab.at[block]
        return copy(at, at, slab_ss.at[k], slab_rs.at[k], col=there)

    slab_own = [slab_copy(col, d, xh * 4 + around(d)) for d in range(1, 4)]
    slab_own_in = [slab_copy(xh * 4 + around(4 - d), d, xh * 4 + around(d)) for d in range(1, 4)]
    slab_x = slab_copy(col, 0, xp)
    slab_x_in = slab_copy(xp, 0, xp)
    slab_on = [slab_copy(xp, 3 + d, xh * 4 + around(d)) for d in range(1, 4)]
    slab_on_in = [
        slab_copy((1 - xh) * 4 + around(4 - d), 3 + d, xh * 4 + around(d)) for d in range(1, 4)
    ]
    slab[col, 0] = tokens[...]
    slab[col, 1] = cot[...]

    for n, w in enumerate((w_ag, w_av, w_bg, w_bv)):
        wt[n] = w[...].astype(F32).T.astype(BF16)
    wp = jnp.concatenate([wt[n, pl.ds(pl.multiple_of(samp * 32, 32), 32), :] for n in range(4)], axis=0)
    tri_f[0:128, :] = w_outproj[...].astype(F32)
    w_op[...] = jnp.concatenate(
        [tri_f[pl.ds(0, 64, stride=2), :], tri_f[pl.ds(1, 64, stride=2), :]], axis=0
    ).astype(BF16)
    crop = jnp.concatenate([crop_v[i : i + 1, :] for i in range(6)], axis=1).astype(F32)
    token_gain = jnp.concatenate([lnt[i : i + 1, :] for i in range(6)], axis=1)

    def keep_lanes(block):
        kept = jnp.zeros((1, B), F32)
        for b in range(NC):
            kept = jnp.where(block == b, crop[:, b * B : b * B + B], kept)
        return jnp.concatenate([kept, jnp.zeros((1, 32), F32)], axis=1)

    keep_rows, keep_cols = keep_lanes(row), keep_lanes(col)

    made[B * B : B * B + 32, :] = jnp.zeros((32, 128), F32)
    lane = lax.broadcasted_iota(jnp.int32, (8, 128), 1)
    wide = lane < B

    def norm_chunk(m):
        src = pl.ds(pl.multiple_of(m * (16 * B), 16 * B), 16 * B)
        dst = pl.ds(pl.multiple_of(m * CR, 32), 16 * B)
        normed[dst, :] = (normalize(pair[src, :], ones) * lnp[...]).astype(BF16)

    def made_chunk(m):
        at = pl.ds(pl.multiple_of(m * CR, CR), CR)
        made[at, :] = nt(normed[at, :], wp)

    def edge(o, first, kept):
        return jax.nn.sigmoid(o[first : first + 32]) * o[first + 32 : first + 64] * kept

    def right_step(m, carry):
        for e in range(8):
            k = m * 8 + e
            rows = jnp.concatenate([made[pl.ds(k, B, stride=B), :], jnp.zeros((32, 128), F32)], axis=0)
            v = edge(rows.T, 64, keep_rows * crop_s[col * B + k].astype(F32))
            for q in range(3):
                packed = jnp.where(wide, v[8 * q : 8 * q + 8], pltpu.roll(v[24:32], 96 - 32 * q, 1))
                rf[pl.ds(k + 8 * B * q, 8, stride=B), :] = packed
        return carry

    def left_step(m, carry):
        for e in range(8):
            i = m * 8 + e
            rows = made[pl.ds(pl.multiple_of(i * B, B), 128), :]
            v = edge(rows.T, 0, keep_cols * crop_s[row * B + i].astype(F32))
            for q in range(4):
                lf[pl.ds(i + 8 * B * q, 8, stride=B), :] = v[8 * q : 8 * q + 8]
        return carry

    norm_chunk(0)

    pl.semaphore_wait(barrier, NC + NR + NS - 3)
    for c in [slab_x] + slab_own:
        c.start()

    def front_step(m, carry):
        made_chunk(m)
        norm_chunk(m + 1)
        return carry

    lax.fori_loop(0, 5, front_step, 0)
    made_chunk(5)
    lax.fori_loop(0, B // 8, right_step, 0)
    slab_x_in.wait_recv()
    for c in slab_on:
        c.start()
    own = lax.broadcasted_iota(jnp.int32, (B, 128), 1) < B
    carriers = [(n, k, pl.ds((k * 8 + n) * B, B)) for n in range(CH) for k in range(3)]
    for n, k, at in carriers:
        rslab[n, row, k * B : k * B + B, :] = rf[at, :].astype(BF16)

    ring = (right, left)
    step_of = (-1, 1)

    def rcopy(n, t, s, inward):
        back = t if inward else t - 1
        block = (row + NR + step_of[s] * back) % NR
        rows = pl.ds(0, RC) if t < 4 else pl.ds(s * (RC // 2), RC // 2)
        at = rslab.at[n, block, rows]
        return copy(at, at, ring_ss.at[n, s, t - 1], ring_rs.at[n, s, t - 1], row=ring[s])

    for n in range(3):
        for s in range(2):
            rcopy(n, 1, s, False).start()
    lax.fori_loop(0, B // 8, left_step, 0)
    for n in range(CH):
        for q in range(3):
            for half, c in enumerate((q * 8 + n, 24 + n)):
                lm[n, q, half * B : half * B + B, :] = lf[c * B : c * B + B, 0:B].astype(BF16)

    def token_rows(pair_of):
        at = pl.ds(pair_of * 2 * B, 2 * B)
        x = [slab[b, 0, at, :].astype(F32) for b in range(NC)]
        total = x[0]
        for b in range(1, NC):
            total = total + x[b]
        mean = jnp.sum(total, axis=-1, keepdims=True) * (1.0 / (NC * B))
        x = [v - mean for v in x]
        total = x[0] * x[0]
        for b in range(1, NC):
            total = total + x[b] * x[b]
        inv = lax.rsqrt(jnp.sum(total, axis=-1, keepdims=True) * (1.0 / (NC * B)) + 1e-05)
        for b in range(NC):
            xd[:, b * B : b * B + B] = x[b] * inv
            cd[:, b * B : b * B + B] = slab[b, 1, at, :].astype(F32)

    def token_keys(pair_of):
        normal = (xd[...] * token_gain).astype(BF16)
        tokens_at = pl.ds(pl.multiple_of(row * B, B), B)
        for w, dest in ((wk, kslab), (wv, vslab)):
            out = nt(normal, w[...]).astype(BF16)
            for e in range(2):
                dest[pair_of * 2 + e, tokens_at, :] = out[e * B : e * B + B]

    def token_queries(pair_of):
        at = pl.ds(pair_of * 2 * B, 2 * B)
        normal = (xd[...] * token_gain).astype(BF16)
        q_s[at, :] = nt(normal, wq[...]).astype(BF16)
        gate = jax.nn.sigmoid(nt(normal, wg[...]))
        gate_s[at, :] = gate
        d = nt(cd[...].astype(BF16), wo[...])
        datt_s[at, :] = (d * gate).astype(BF16)

    def products(n, back):
        if back in (0, 4):
            blocks = [(row + back) % NR]
        else:
            blocks = [(row + NR + step * back) % NR for step in (-1, 1)]
        for q in range(3):
            rights = [rslab[n, j, q * B : q * B + B, :] for j in blocks]
            o = nn(lm[n, q], jnp.concatenate(rights, axis=1))
            for e, j in enumerate(blocks):
                at = slice(e * 128, e * 128 + 128)
                packed = jnp.where(own, o[0:B, at], o[B : 2 * B, at]).astype(BF16)
                part[n, j % 4, j // 4, q * B : q * B + B, :] = packed

    sides = (xh * 4 + (yy + 1) % 4, xh * 4 + (yy + 3) % 4)

    def zcopy(n, s):
        src = part.at[n, (yy + 2) % 4, :, pl.ds(s * (RC // 2), RC // 2)]
        return copy(src, z_recv.at[n, s], z_ss.at[n, s], z_rs.at[n, s], col=sides[s])

    def ycopy(n, s):
        there = (yy + (1, 3, 2)[s]) % 4
        return copy(
            part.at[n, there], y_recv.at[n, s], y_ss.at[n, s], y_rs.at[n, s], col=xh * 4 + there
        )

    def y_ways(n):
        return (0, 1, 2) if n >= CH - 2 else (0, 1)

    def z_start(n):
        for s in range(2):
            zcopy(n, s).start()

    def y_start(n):
        for s in range(2):
            zcopy(n, s).wait_recv()
            for x in range(2):
                at = pl.ds(s * (RC // 2), RC // 2)
                more = z_recv[n, s, x].astype(F32)
                there = (yy + 1 + 2 * s) % 4
                part[n, there, x, at, :] = (part[n, there, x, at, :].astype(F32) + more).astype(BF16)
            ycopy(n, s).start()

    def y_sum(n):
        for s in y_ways(n):
            ycopy(n, s).wait_recv()

        def one(k, carry):
            at = pl.ds(pl.multiple_of(k * B, B), B)

            def total(x):
                v = part[n, yy, x, at, :].astype(F32)
                for s in y_ways(n):
                    v = v + y_recv[n, s, x, at, :].astype(F32)
                return v

            own_sum[n, at, :] = total(xh)
            x_send[n, at, :] = total(1 - xh).astype(BF16)
            return carry

        lax.fori_loop(0, 3, one, 0)
        xcopy(n).start()

    def xcopy(n):
        return copy(x_send.at[n], x_recv.at[n], x_ss.at[n], x_rs.at[n], col=xp)

    def samp_copy(src_of, dst_of, ss, rs, d, inward):
        there, here = (samp + d) % NS, (samp + NS - d) % NS
        return copy(src_of(there), dst_of(here if inward else samp), ss.at[d], rs.at[d], samp=there)

    def tcopy(n, d, inward):
        return samp_copy(
            lambda m: tri_send.at[m, n], lambda m: tri_recv.at[m, n], t_ss.at[n], t_rs.at[n], d, inward
        )

    lane96 = lax.broadcasted_iota(jnp.int32, (B, 128), 1)

    def triangle(n):
        xcopy(n).wait_recv()
        c = []
        for q in range(3):
            at = pl.ds(q * B, B)
            c.append(own_sum[n, at, :] + x_recv[n, at, :].astype(F32))
        tail = jnp.where(
            lane96 < 32,
            pltpu.roll(c[0], 32, 1),
            jnp.where(lane96 < 64, pltpu.roll(c[1], 64, 1), pltpu.roll(c[2], 96, 1)),
        )
        c.append(tail)
        for h in range(2):
            for m in range(NS):
                both = [v[m * Q : m * Q + Q] for v in c[2 * h : 2 * h + 2]]
                tri_send[m, n, h] = jnp.concatenate(both, axis=0).astype(BF16)
        for d in range(1, NS):
            tcopy(n, d, False).start()

    def kvcopies(t, s, inward):
        back = t if inward else t - 1
        block = (row + NR + step_of[s] * back) % NR
        rows = pl.ds(pl.multiple_of(block * B, B), B)
        both = [(0, kslab), (1, vslab)]
        return [
            copy(v.at[:, rows, :], v.at[:, rows, :], kv_ss.at[n, s, t - 1], kv_rs.at[n, s, t - 1], row=ring[s])
            for n, v in (both if t < 4 else both[s : s + 1])
        ]

    def ring_slot(n, t):
        for s in range(2):
            if t > 1:
                rcopy(n, t - 1, s, True).wait_recv()
            if t < 5 and not (t == 1 and n < 3):
                rcopy(n, t, s, False).start()
        products(n, t - 1)
        if t == 5 and n >= CH - 2:
            for s in y_ways(n):
                ycopy(n, s).start()
        elif t == 5:
            z_start(n)

    def kv_slot(t):
        for s in range(2):
            if t > 1:
                for c in kvcopies(t - 1, s, True):
                    c.wait_recv()
            if t < 5:
                for c in kvcopies(t, s, False):
                    c.start()

    def token_wait(_):
        for c in slab_own_in + slab_on_in:
            c.wait_recv()

    for k in range(CH + 6):
        between = []
        for n in range(CH):
            t = k - n + 1 + (n >= CH - 2)
            if t == 8:
                between.append((triangle, n))
            elif t == 7:
                between.append((y_sum, n))
            elif t == 6 and n < CH - 2:
                between.append((y_start, n))
        if k == 4:
            between.append((token_wait, 0))
        if k in (4, 5):
            between += [(f, k - 4) for f in (token_rows, token_keys, token_queries)]
        for n in range(CH):
            if 1 <= k - n + 1 <= 5:
                ring_slot(n, k - n + 1)
                if between:
                    f, arg = between.pop(0)
                    f(arg)
        if 1 <= k - CH + 1 <= 5:
            kv_slot(k - CH + 1)
        for f, arg in between:
            f(arg)

    def unpack(m):
        for n in range(CH):
            for h in range(2):
                both = tri_recv[m, n, h].astype(F32)
                for e in range(2):
                    c = (2 * h + e) * 8 + n
                    r0 = pl.multiple_of(m * 768, 768) + c // 2 * 48 + c % 2 * Q
                    tri_f[pl.ds(r0, Q), :] = both[e * Q : e * Q + Q]

    tri_recv[samp] = tri_send[samp]
    unpack(samp)
    for d in range(1, NS):
        for n in range(CH):
            tcopy(n, d, True).wait_recv()
        unpack((samp + NS - d) % NS)

    row0 = samp * Q
    sib, oth = samp + 1 - 2 * (samp % 2), (samp + 2) % NS
    diag = (sib + 2) % NS

    def part_of(n, m):
        return pair_out.at[pl.ds(pl.multiple_of((n * Q + m * 4) * B, 4 * B), 4 * B)]

    def pocopy(k, m, inward):
        there = (sib, oth)[k]
        at = part_of(there if inward else samp, m)
        return copy(at, at, po_ss.at[k, m], po_rs.at[k, m], samp=there)

    def prcopy(inward):
        n = diag if inward else oth
        at = pair_out.at[pl.ds(pl.multiple_of(n * (Q * B), Q * B), Q * B)]
        return copy(at, at, pr_ss, pr_rs, samp=sib)


    def post_rows(m):
        cols = []
        for e in range(4):
            i = m * 4 + e
            cols.append(
                jnp.concatenate(
                    [tri_f[pl.ds(i, 64, stride=48), :], tri_f[pl.ds(Q + i, 64, stride=48), :]], axis=0
                )
            )
        t = jnp.concatenate(cols, axis=1)
        center = t - jnp.mean(t, axis=0, keepdims=True)
        t = center * lax.rsqrt(jnp.mean(center * center, axis=0, keepdims=True) + 1e-05)
        proj = tn(t.astype(BF16), w_op[...])
        proj = jnp.concatenate([proj[e * 128 : e * 128 + B] for e in range(4)], axis=0)
        first = row0 + m * 4
        at = pl.ds(pl.multiple_of(first * B, 4 * B), 4 * B)
        norm_at = pl.ds(pl.multiple_of(first // 16 * CR + first % 16 * B, 32), 4 * B)
        gate = jax.nn.sigmoid(nn(normed[norm_at, :], w_outgate[...]))
        updated = (pair[at, :].astype(F32) + gate * proj).astype(BF16)
        trans_in = normalize(updated, ones).astype(BF16)
        total = updated.astype(F32)
        for n in range(2):
            a = nn(trans_in, w_tg[:, n * 256 : n * 256 + 256])
            u = nn(trans_in, w_tu[:, n * 256 : n * 256 + 256])
            hidden = (a * jax.nn.sigmoid(a) * u).astype(BF16)
            total = total + nn(hidden, w_td[n * 256 : n * 256 + 256, :])
        out = total.astype(BF16)
        bias_in = (normalize(out, ones) * lnb[...]).astype(BF16)
        return at, out, nt(wpbt[...], bias_in)

    def post_step(m, carry):
        done = [post_rows(m * 2 + n) for n in range(2)]
        for n, (at, out, heads) in enumerate(done):
            pair_out[at, :] = out
            for e in range(4):
                hb_f[pl.ds((m * 2 + n) * 4 + e, 16, stride=Q), 0:B] = heads[:, e * B : e * B + B]
        for n in range(2):
            for k in range(2):
                pocopy(k, m * 2 + n, False).start()
        return carry

    lax.fori_loop(0, Q // 8, post_step, 0)
    for c in range(NC):
        hb_send[c] = hb_f[c * 48 : c * 48 + 48, :].astype(BF16)

    def hcopy(d, inward):
        there, here = (col + d) % NC, (col + NC - d) % NC
        dst = hb.at[here if inward else col, samp]
        return copy(hb_send.at[there], dst, h_ss.at[d], h_rs.at[d], col=there)

    for d in range(1, NC):
        hcopy(d, False).start()
    hb[col, samp] = hb_send[col]

    feature = lax.broadcasted_iota(jnp.int32, (1, B), 1)
    head_masks = [(feature < 48).astype(F32), (feature >= 48).astype(F32)]
    scale = 1.0 / math.sqrt(48)

    def per_head(v):
        return jnp.concatenate([v * m.astype(BF16) for m in head_masks], axis=0)

    def before_bias(s):
        at = slice(s * B, s * B + B)
        raw[s] = nt(per_head(q_s[at, :]), kslab[s]) * scale
        d_probs[s] = nt(per_head(datt_s[at, :]), vslab[s])

    before_bias(0)
    before_bias(1)
    for d in range(1, NC):
        hcopy(d, True).wait_recv()

    def hgcopy(d, inward):
        return samp_copy(lambda _: hb.at[:, samp], lambda n: hb.at[:, n], hg_ss, hg_rs, d, inward)

    for d in range(1, NS):
        hgcopy(d, False).start()
    before_bias(2)
    before_bias(3)
    for d in range(1, NS):
        hgcopy(d, True).wait_recv()

    for b in range(NC):
        key_mask = (crop[:, b * B : b * B + B] - 1.0) * 10000.0
        quarters = [hb[b, n].astype(F32) for n in range(NS)]
        for h in range(2):
            whole = jnp.concatenate([v[h * Q : h * Q + Q, 0:B] for v in quarters], axis=0)
            bias[h * B : h * B + B, b * B : b * B + B] = whole + key_mask
    acc[...] = jnp.zeros((2 * B, NC * B), F32)
    def att_rows(s):
        at = pl.ds(pl.multiple_of(s * B, B), B)
        scores = raw[s] + bias[...]
        shifted = jnp.exp(scores - jnp.max(scores, axis=-1, keepdims=True))
        probs = shifted * (1.0 / jnp.sum(shifted, axis=-1, keepdims=True))
        got = nn(probs.astype(BF16), vslab[s])
        delta = jnp.sum(per_head(datt_s[at, :]).astype(F32) * got, axis=-1, keepdims=True)
        attended = got[0:B] * head_masks[0] + got[B : 2 * B] * head_masks[1]
        return (gate_s[at, :] * attended).astype(BF16), probs * (d_probs[s] - delta)

    def att_step(m, carry):
        done = [att_rows(m * 2 + e) for e in range(2)]
        acc[...] = acc[...] + (done[0][1] + done[1][1])
        gated = jnp.concatenate([v for v, _ in done], axis=0)
        at = pl.ds(pl.multiple_of(m * 2 * B, 2 * B), 2 * B)
        xd[...] = nn(gated, wo[...])
        for b in range(NC):
            pj_send[b, at, :] = xd[:, b * B : b * B + B].astype(BF16)
        return carry

    lax.fori_loop(0, 2, att_step, 0)
    for m in range(6):
        pocopy(1, m, True).wait_recv()
    prcopy(False).start()

    for b in range(NC):
        heads = [acc[h * B : h * B + B, b * B : b * B + B] for h in range(2)]
        for n in range(NS):
            both = jnp.concatenate([v[n * Q : n * Q + Q] for v in heads], axis=0)
            g_send[n, b, :, 0:B] = both.astype(BF16)

    def gcopy(d, inward):
        return samp_copy(lambda n: g_send.at[n], lambda n: g_recv.at[n], g_ss, g_rs, d, inward)

    for d in range(1, NS):
        gcopy(d, False).start()

    def pycopy(d, x):
        src = pj_send.at[x * 4 + around(d)]
        return copy(src, py_recv.at[d - 1, x], py_ss.at[d, x], py_rs.at[d, x], col=xh * 4 + around(d))

    pys = [(d, x) for d in range(1, 4) for x in range(2)]
    for d, x in pys:
        pycopy(d, x).start()
    g_recv[samp] = g_send[samp]
    for d in range(1, NS):
        gcopy(d, True).wait_recv()

    def sum_step(b, carry):
        total = g_recv[0, b].astype(F32)
        for n in range(1, NS):
            total = total + g_recv[n, b].astype(F32)
        sg[b] = total.astype(BF16)
        return carry

    lax.fori_loop(0, NC, sum_step, 0)

    def ccopy(d, inward):
        there, here = (col + d) % NC, (col + NC - d) % NC
        return copy(sg.at[there], cg.at[here if inward else col], c_ss.at[d], c_rs.at[d], col=there)

    for d in range(1, NC):
        ccopy(d, False).start()
    cg[col] = sg[col]

    for d, x in pys:
        pycopy(d, x).wait_recv()

    def py_step(s, carry):
        at = pl.ds(pl.multiple_of(s * B, B), B)

        def total(x):
            v = pj_send[x * 4 + yy, at, :].astype(F32)
            for d in range(3):
                v = v + py_recv[d, x, at, :].astype(F32)
            return v

        px_own[at, :] = total(xh) + tokens[at, :].astype(F32)
        px_send[at, :] = total(1 - xh).astype(BF16)
        return carry

    lax.fori_loop(0, 4, py_step, 0)
    px = copy(px_send, px_recv, px_ss, px_rs, col=xp)
    px.start()
    for d in range(1, NC):
        ccopy(d, True).wait_recv()
    for c in range(NC):
        cg_f[c * 48 : c * 48 + 48, :] = cg[c].astype(F32)
    for i in range(Q):
        bg[samp, i] = cg_f[pl.ds(i, 16, stride=Q), :].astype(BF16)

    def bcopy(d, inward):
        return samp_copy(lambda _: bg.at[samp], lambda n: bg.at[n], b_ss, b_rs, d, inward)

    for d in range(1, NS):
        bcopy(d, False).start()
    px.wait_recv()
    tokens_out[...] = (px_own[...] + px_recv[...].astype(F32)).astype(BF16)
    for m in range(6):
        pocopy(0, m, True).wait_recv()
    prcopy(True).wait_recv()
    for d in range(1, NS):
        bcopy(d, True).wait_recv()

    for c in [slab_x, px, prcopy(False)] + slab_own + slab_on:
        c.wait_send()
    for d, x in pys:
        pycopy(d, x).wait_send()
    for m in range(6):
        for k in range(2):
            pocopy(k, m, False).wait_send()

    for n in range(CH):
        for s in range(2):
            for t in range(1, 5):
                rcopy(n, t, s, False).wait_send()
        for s in y_ways(n):
            ycopy(n, s).wait_send()
        if n < CH - 2:
            for s in range(2):
                zcopy(n, s).wait_send()
        for d in range(1, NS):
            tcopy(n, d, False).wait_send()
        xcopy(n).wait_send()
    for t in range(1, 5):
        for s in range(2):
            for c in kvcopies(t, s, False):
                c.wait_send()
    for d in range(1, NC):
        hcopy(d, False).wait_send()
        ccopy(d, False).wait_send()
    for d in range(1, NS):
        hgcopy(d, False).wait_send()
        gcopy(d, False).wait_send()
        bcopy(d, False).wait_send()


def split(v):
    high = v.astype(BF16)
    rest = v - high.astype(F32)
    mid = rest.astype(BF16)
    return high, mid, (rest - mid.astype(F32)).astype(BF16)


def finish(pair_rows, token_rows, bg, lnb, wpbt, pair_out, tokens_out, pair_grad):
    @pl.when(pl.program_id(0) == 0)
    def _():
        tokens_out[...] = token_rows[...]

    pair_out[...] = pair_rows[...]
    ones = mean_weights()
    weights = wpbt[...].astype(F32) * lnb[...]
    weights = weights - jnp.mean(weights, axis=-1, keepdims=True)
    weights = jnp.concatenate(split(weights), axis=0)
    empty = jnp.zeros((48, 128), BF16)
    weights = jnp.concatenate(
        [jnp.concatenate([weights, empty], axis=1), jnp.concatenate([empty, weights], axis=1)], axis=0
    )
    for e in range(4):
        at = slice(e * 4 * B, e * 4 * B + 4 * B)
        even, odd = [
            jnp.concatenate([bg[e * 4 + n], bg[e * 4 + 2 + n]], axis=1) for n in range(2)
        ]
        both = tn(jnp.concatenate([even] * 3 + [odd] * 3, axis=0), weights)
        scaled = jnp.concatenate(
            [both[0:B, :128], both[0:B, 128:], both[128 : 128 + B, :128], both[128 : 128 + B, 128:]], axis=0
        )
        center, inv = centered(pair_rows[at, :], ones)
        unit = center * inv
        pair_grad[at, :] = inv * (scaled - unit * row_means((scaled * unit).astype(BF16), ones))


def per_device(
    pair, crop_mask, w_agate, w_aval, w_bgate, w_bval, w_outgate, w_outproj, ln_pair,
    w_trans_gate, w_trans_up, w_trans_down, ln_bias, w_pairbias, tokens, ln_token,
    w_query, w_key, w_value, w_gate, w_output, cotangent,
):
    wpbt = w_pairbias.T
    lnb = ln_bias.reshape(1, 128)
    args = (
        pair.reshape(B * B, 128), crop_mask, crop_mask.reshape(6, 128),
        w_agate, w_aval, w_bgate, w_bval, ln_pair.reshape(1, 128), w_outgate, w_outproj,
        w_trans_gate, w_trans_up, w_trans_down, lnb, wpbt,
        tokens.reshape(4 * B, B), cotangent.reshape(4 * B, B), ln_token.reshape(6, 128),
        w_query.T, w_key.T, w_value.T, w_gate.T, w_output,
    )
    vm = pltpu.VMEM
    dma = pltpu.SemaphoreType.DMA
    scratch = [
        vm((4, 128, 128), BF16),
        vm((128, 128), BF16),
        vm((2 * B, NC * B), F32),
        vm((2 * B, NC * B), F32),
        vm((256, 256), BF16),
        vm((6 * CR, 128), BF16),
        vm((B * B + 32, 128), F32),
        vm((32 * B, 128), F32),
        vm((G * B, 128), F32),
        vm((CH, 3, 2 * B, B), BF16),
        vm((CH, NR, RC, 128), BF16),
        vm((CH, 4, 2, RC, 128), BF16),
        vm((CH, 2, 2, RC // 2, 128), BF16),
        vm((CH, 3, 2, RC, 128), BF16),
        vm((CH, RC, 128), F32),
        vm((CH, RC, 128), BF16),
        vm((CH, RC, 128), BF16),
        vm((NC, 2, 4 * B, B), BF16),
        vm((4 * B, B), BF16),
        vm((4, NR * B, B), BF16),
        vm((4, NR * B, B), BF16),
        vm((4 * B, B), F32),
        vm((4 * B, B), BF16),
        vm((NS, CH, 2, 48, 128), BF16),
        vm((NS, CH, 2, 48, 128), BF16),
        vm((64 * 48, 128), F32),
        vm((16 * Q, 128), F32),
        vm((NC, 48, 128), BF16),
        vm((NC, NS, 48, 128), BF16),
        vm((2 * B, NC * B), F32),
        vm((4, 2 * B, NC * B), F32),
        vm((4, 2 * B, NC * B), F32),
        vm((2 * B, NC * B), F32),
        vm((NS, NC, 48, 128), BF16),
        vm((NS, NC, 48, 128), BF16),
        vm((NC, 4 * B, B), BF16),
        vm((3, 2, 4 * B, B), BF16),
        vm((4 * B, B), F32),
        vm((4 * B, B), BF16),
        vm((4 * B, B), BF16),
        vm((NC, 48, 128), BF16),
        vm((NC, 48, 128), BF16),
        vm((16 * Q, 128), F32),
    ]
    sems = [(7,)] * 2 + [(CH, 2, 4)] * 2 + [(CH, 2)] * 2 + [(CH, 3)] * 2 + [(CH,)] * 2
    sems += [(2, 2, 4)] * 2 + [(CH, 4)] * 2 + [(8,)] * 2 + [(4,)] * 2 + [(2, 6)] * 2 + [None] * 2
    sems += [(4, 2)] * 2 + [None] * 2 + [(4,)] * 2 + [(8,)] * 2 + [(4,)] * 2
    scratch += [dma if s is None else dma(s) for s in sems]
    spec = pl.BlockSpec(memory_space=pltpu.VMEM)
    specs = [spec] * len(args)
    specs[1] = pl.BlockSpec(memory_space=pltpu.SMEM)
    pair_rows, token_rows, bg = pl.pallas_call(
        kernel,
        out_shape=(
            jax.ShapeDtypeStruct((B * B, 128), BF16),
            jax.ShapeDtypeStruct((4 * B, B), BF16),
            jax.ShapeDtypeStruct((NS, Q, 16, 128), BF16),
        ),
        in_specs=specs,
        out_specs=(spec,) * 3,
        scratch_shapes=scratch,
        compiler_params=pltpu.CompilerParams(
            collective_id=0, has_side_effects=True, vmem_limit_bytes=56 * 1024 * 1024
        ),
    )(*args)
    rows = pl.BlockSpec((16 * B, 128), lambda i: (i, 0))
    whole = pl.BlockSpec((4 * B, B), lambda i: (0, 0))
    outs = pl.pallas_call(
        finish,
        grid=(B // 16,),
        out_shape=(
            jax.ShapeDtypeStruct((B * B, 128), BF16),
            jax.ShapeDtypeStruct((4 * B, B), BF16),
            jax.ShapeDtypeStruct((B * B, 128), F32),
        ),
        in_specs=[
            rows,
            whole,
            pl.BlockSpec((16, 16, 128), lambda i: (i, 0, 0)),
            pl.BlockSpec((1, 128), lambda i: (0, 0)),
            pl.BlockSpec((16, 128), lambda i: (0, 0)),
        ],
        out_specs=(rows, whole, rows),
    )(pair_rows, token_rows, bg.reshape(B, 16, 128), lnb, wpbt)
    return (
        outs[0].reshape(B, B, 128),
        outs[1].reshape(4, B, B),
        outs[2].reshape(B, B, 128),
    )


def solution(mesh):
    placed = (
        P("row", "col", None),
        P(), P(), P(), P(), P(), P(), P(), P(), P(), P(), P(), P(), P(),
        P("samp", "row", "col"),
        P(),
        P(None, "col"),
        P(None, "col"),
        P(None, "col"),
        P(None, "col"),
        P("col", None),
        P("samp", "row", "col"),
    )
    return jax.shard_map(
        per_device,
        mesh=mesh,
        in_specs=placed,
        out_specs=(P("row", "col", None), P("samp", "row", "col"), P("row", "col", None)),
        check_vma=False,
    )
```

```python
import math

import jax
import jax.numpy as jnp
from jax import lax
from jax.experimental import pallas as pl
from jax.experimental.pallas import tpu as pltpu
from jax.sharding import PartitionSpec as P

F32 = jnp.float32
BF16 = jnp.bfloat16
MESH = pl.DeviceIdType.MESH
NR = 8
NC = 8
NS = 4
B = 96
Q = 24
G = 24
CH = 8
RC = 3 * B
EARLY = 5
CR = 16 * B


def nt(a, b):
    return lax.dot_general(a, b, (((1,), (1,)), ((), ())), preferred_element_type=F32)


def nn(a, b):
    return lax.dot_general(a, b, (((1,), (0,)), ((), ())), preferred_element_type=F32)


def tn(a, b):
    return lax.dot_general(a, b, (((0,), (0,)), ((), ())), preferred_element_type=F32)


def row_means(values, ones):
    half = values.shape[0] // 2
    out = nn(jnp.concatenate([values[:half], values[half:]], axis=1), ones)
    return jnp.concatenate([out[:, :128], out[:, 128:]], axis=0)


def centered(values, ones):
    center = values.astype(F32) - row_means(values, ones)
    return center, lax.rsqrt(row_means((center * center).astype(BF16), ones) + 1e-05)


def normalize(values, ones):
    center, inv = centered(values, ones)
    return center * inv


def mean_weights():
    first = lax.broadcasted_iota(jnp.int32, (256, 256), 0) < 128
    second = lax.broadcasted_iota(jnp.int32, (256, 256), 1) < 128
    return jnp.where(first == second, 1.0 / 128.0, 0.0).astype(BF16)


def kernel(
    pair, crop_s, crop_v, w_ag, w_av, w_bg, w_bv, lnp, w_outgate, w_outproj, w_tg, w_tu, w_td,
    lnb, wpbt, tokens, cot, lnt, wq, wk, wv, wg, wo,
    pair_out, tokens_out, bg,
    wt, w_op, xd, cd,
    ones_ref, normed, made, lf, rf, lm, rslab, part, z_recv, y_recv, own_sum, x_send, x_recv, slab, q_s, kslab,
    vslab, gate_s, datt_s, tri_send, tri_recv, tri_f, hb_f, hb_send, hb, bias, raw, d_probs, acc, g_send, g_recv,
    pj_send, py_recv, px_own, px_send, px_recv, sg, cg, cg_f,
    slab_ss, slab_rs, ring_ss, ring_rs, z_ss, z_rs, y_ss, y_rs, x_ss, x_rs,
    kv_ss, kv_rs, t_ss, t_rs, h_ss, h_rs, hg_ss, hg_rs, po_ss, po_rs, pr_ss, pr_rs,
    py_ss, py_rs, px_ss, px_rs, g_ss, g_rs, c_ss, c_rs, b_ss, b_rs,
):
    row = lax.axis_index("row")
    col = lax.axis_index("col")
    samp = lax.axis_index("samp")
    xh = col // 4
    yy = col % 4
    xp = (1 - xh) * 4 + yy
    ones_ref[...] = mean_weights()
    ones = ones_ref[...]
    right = (row + 1) % NR
    left = (row + NR - 1) % NR

    def copy(src, dst, ss, rs, **where):
        return pltpu.make_async_remote_copy(
            src_ref=src, dst_ref=dst, send_sem=ss, recv_sem=rs, device_id=where, device_id_type=MESH
        )

    barrier = pltpu.get_barrier_semaphore()
    for d in range(1, NC):
        pl.semaphore_signal(barrier, inc=1, device_id={"col": (col + d) % NC}, device_id_type=MESH)
    for d in range(1, NR):
        pl.semaphore_signal(barrier, inc=1, device_id={"row": (row + d) % NR}, device_id_type=MESH)
    for d in range(1, NS):
        pl.semaphore_signal(
            barrier, inc=1, device_id={"samp": (samp + d) % NS}, device_id_type=MESH
        )

    def around(d):
        return (yy + d) % 4

    def slab_copy(block, k, there):
        at = slab.at[block]
        return copy(at, at, slab_ss.at[k], slab_rs.at[k], col=there)

    slab_own = [slab_copy(col, d, xh * 4 + around(d)) for d in range(1, 4)]
    slab_own_in = [slab_copy(xh * 4 + around(4 - d), d, xh * 4 + around(d)) for d in range(1, 4)]
    slab_x = slab_copy(col, 0, xp)
    slab_x_in = slab_copy(xp, 0, xp)
    slab_on = [slab_copy(xp, 3 + d, xh * 4 + around(d)) for d in range(1, 4)]
    slab_on_in = [
        slab_copy((1 - xh) * 4 + around(4 - d), 3 + d, xh * 4 + around(d)) for d in range(1, 4)
    ]
    slab[col, 0] = tokens[...]
    slab[col, 1] = cot[...]

    for n, w in enumerate((w_ag, w_av, w_bg, w_bv)):
        wt[n] = w[...].astype(F32).T.astype(BF16)
    wp = jnp.concatenate([wt[n, pl.ds(pl.multiple_of(samp * 32, 32), 32), :] for n in range(4)], axis=0)
    tri_f[0:128, :] = w_outproj[...].astype(F32)
    w_op[...] = jnp.concatenate(
        [tri_f[pl.ds(0, 64, stride=2), :], tri_f[pl.ds(1, 64, stride=2), :]], axis=0
    ).astype(BF16)
    crop = jnp.concatenate([crop_v[i : i + 1, :] for i in range(6)], axis=1).astype(F32)
    token_gain = jnp.concatenate([lnt[i : i + 1, :] for i in range(6)], axis=1)

    def keep_lanes(block):
        kept = jnp.zeros((1, B), F32)
        for b in range(NC):
            kept = jnp.where(block == b, crop[:, b * B : b * B + B], kept)
        return jnp.concatenate([kept, jnp.zeros((1, 32), F32)], axis=1)

    keep_rows, keep_cols = keep_lanes(row), keep_lanes(col)

    made[B * B : B * B + 32, :] = jnp.zeros((32, 128), F32)
    lane = lax.broadcasted_iota(jnp.int32, (8, 128), 1)
    wide = lane < B

    def norm_chunk(m):
        src = pl.ds(pl.multiple_of(m * (16 * B), 16 * B), 16 * B)
        dst = pl.ds(pl.multiple_of(m * CR, 32), 16 * B)
        normed[dst, :] = (normalize(pair[src, :], ones) * lnp[...]).astype(BF16)

    def made_chunk(m):
        at = pl.ds(pl.multiple_of(m * CR, CR), CR)
        made[at, :] = nt(normed[at, :], wp)

    def edge(o, first, kept):
        return jax.nn.sigmoid(o[first : first + 32]) * o[first + 32 : first + 64] * kept

    def right_step(m, carry):
        for e in range(8):
            k = m * 8 + e
            rows = jnp.concatenate([made[pl.ds(k, B, stride=B), :], jnp.zeros((32, 128), F32)], axis=0)
            v = edge(rows.T, 64, keep_rows * crop_s[col * B + k].astype(F32))
            for q in range(3):
                packed = jnp.where(wide, v[8 * q : 8 * q + 8], pltpu.roll(v[24:32], 96 - 32 * q, 1))
                rf[pl.ds(k + 8 * B * q, 8, stride=B), :] = packed
        return carry

    def left_step(m, carry):
        for e in range(8):
            i = m * 8 + e
            rows = made[pl.ds(pl.multiple_of(i * B, B), 128), :]
            v = edge(rows.T, 0, keep_cols * crop_s[row * B + i].astype(F32))
            for q in range(4):
                lf[pl.ds(i + 8 * B * q, 8, stride=B), :] = v[8 * q : 8 * q + 8]
        return carry

    norm_chunk(0)

    pl.semaphore_wait(barrier, NC + NR + NS - 3)
    for c in [slab_x] + slab_own:
        c.start()

    def front_step(m, carry):
        made_chunk(m)
        norm_chunk(m + 1)
        return carry

    lax.fori_loop(0, 5, front_step, 0)
    made_chunk(5)
    lax.fori_loop(0, B // 8, right_step, 0)
    slab_x_in.wait_recv()
    for c in slab_on:
        c.start()
    own = lax.broadcasted_iota(jnp.int32, (B, 128), 1) < B
    carriers = [(n, k, pl.ds((k * 8 + n) * B, B)) for n in range(CH) for k in range(3)]
    for n, k, at in carriers:
        rslab[n, row, k * B : k * B + B, :] = rf[at, :].astype(BF16)

    ring = (right, left)
    step_of = (-1, 1)

    def rcopy(n, t, s, inward):
        back = t if inward else t - 1
        block = (row + NR + step_of[s] * back) % NR
        rows = pl.ds(0, RC) if t < 4 else pl.ds(s * (RC // 2), RC // 2)
        at = rslab.at[n, block, rows]
        return copy(at, at, ring_ss.at[n, s, t - 1], ring_rs.at[n, s, t - 1], row=ring[s])

    for n in range(EARLY):
        for s in range(2):
            rcopy(n, 1, s, False).start()
    lax.fori_loop(0, B // 8, left_step, 0)
    for n in range(CH):
        for q in range(3):
            for half, c in enumerate((q * 8 + n, 24 + n)):
                lm[n, q, half * B : half * B + B, :] = lf[c * B : c * B + B, 0:B].astype(BF16)

    def token_rows(pair_of):
        at = pl.ds(pair_of * 2 * B, 2 * B)
        x = [slab[b, 0, at, :].astype(F32) for b in range(NC)]
        total = x[0]
        for b in range(1, NC):
            total = total + x[b]
        mean = jnp.sum(total, axis=-1, keepdims=True) * (1.0 / (NC * B))
        x = [v - mean for v in x]
        total = x[0] * x[0]
        for b in range(1, NC):
            total = total + x[b] * x[b]
        inv = lax.rsqrt(jnp.sum(total, axis=-1, keepdims=True) * (1.0 / (NC * B)) + 1e-05)
        for b in range(NC):
            xd[:, b * B : b * B + B] = x[b] * inv
            cd[:, b * B : b * B + B] = slab[b, 1, at, :].astype(F32)

    def token_keys(pair_of):
        normal = (xd[...] * token_gain).astype(BF16)
        tokens_at = pl.ds(pl.multiple_of(row * B, B), B)
        for w, dest in ((wk, kslab), (wv, vslab)):
            out = nt(normal, w[...]).astype(BF16)
            for e in range(2):
                dest[pair_of * 2 + e, tokens_at, :] = out[e * B : e * B + B]

    def token_queries(pair_of):
        at = pl.ds(pair_of * 2 * B, 2 * B)
        normal = (xd[...] * token_gain).astype(BF16)
        q_s[at, :] = nt(normal, wq[...]).astype(BF16)
        gate = jax.nn.sigmoid(nt(normal, wg[...]))
        gate_s[at, :] = gate
        d = nt(cd[...].astype(BF16), wo[...])
        datt_s[at, :] = (d * gate).astype(BF16)

    def products(n, back):
        if back in (0, 4):
            blocks = [(row + back) % NR]
        else:
            blocks = [(row + NR + step * back) % NR for step in (-1, 1)]
        for q in range(3):
            rights = [rslab[n, j, q * B : q * B + B, :] for j in blocks]
            o = nn(lm[n, q], jnp.concatenate(rights, axis=1))
            for e, j in enumerate(blocks):
                at = slice(e * 128, e * 128 + 128)
                packed = jnp.where(own, o[0:B, at], o[B : 2 * B, at]).astype(BF16)
                part[n, j % 4, j // 4, q * B : q * B + B, :] = packed

    sides = (xh * 4 + (yy + 1) % 4, xh * 4 + (yy + 3) % 4)

    def zcopy(n, s):
        src = part.at[n, (yy + 2) % 4, :, pl.ds(s * (RC // 2), RC // 2)]
        return copy(src, z_recv.at[n, s], z_ss.at[n, s], z_rs.at[n, s], col=sides[s])

    def ycopy(n, s):
        there = (yy + (1, 3, 2)[s]) % 4
        return copy(
            part.at[n, there], y_recv.at[n, s], y_ss.at[n, s], y_rs.at[n, s], col=xh * 4 + there
        )

    def y_ways(n):
        return (0, 1, 2) if n >= CH - 2 else (0, 1)

    def z_start(n):
        for s in range(2):
            zcopy(n, s).start()

    def y_start(n):
        for s in range(2):
            zcopy(n, s).wait_recv()
            for x in range(2):
                at = pl.ds(s * (RC // 2), RC // 2)
                more = z_recv[n, s, x].astype(F32)
                there = (yy + 1 + 2 * s) % 4
                part[n, there, x, at, :] = (part[n, there, x, at, :].astype(F32) + more).astype(BF16)
            ycopy(n, s).start()

    def y_sum(n):
        for s in y_ways(n):
            ycopy(n, s).wait_recv()

        def one(k, carry):
            at = pl.ds(pl.multiple_of(k * B, B), B)

            def total(x):
                v = part[n, yy, x, at, :].astype(F32)
                for s in y_ways(n):
                    v = v + y_recv[n, s, x, at, :].astype(F32)
                return v

            own_sum[n, at, :] = total(xh)
            x_send[n, at, :] = total(1 - xh).astype(BF16)
            return carry

        lax.fori_loop(0, 3, one, 0)
        xcopy(n).start()

    def xcopy(n):
        return copy(x_send.at[n], x_recv.at[n], x_ss.at[n], x_rs.at[n], col=xp)

    def samp_copy(src_of, dst_of, ss, rs, d, inward):
        there, here = (samp + d) % NS, (samp + NS - d) % NS
        return copy(src_of(there), dst_of(here if inward else samp), ss.at[d], rs.at[d], samp=there)

    def tcopy(n, d, inward):
        return samp_copy(
            lambda m: tri_send.at[m, n], lambda m: tri_recv.at[m, n], t_ss.at[n], t_rs.at[n], d, inward
        )

    lane96 = lax.broadcasted_iota(jnp.int32, (B, 128), 1)

    def triangle(n):
        xcopy(n).wait_recv()
        c = []
        for q in range(3):
            at = pl.ds(q * B, B)
            c.append(own_sum[n, at, :] + x_recv[n, at, :].astype(F32))
        tail = jnp.where(
            lane96 < 32,
            pltpu.roll(c[0], 32, 1),
            jnp.where(lane96 < 64, pltpu.roll(c[1], 64, 1), pltpu.roll(c[2], 96, 1)),
        )
        c.append(tail)
        for h in range(2):
            for m in range(NS):
                both = [v[m * Q : m * Q + Q] for v in c[2 * h : 2 * h + 2]]
                tri_send[m, n, h] = jnp.concatenate(both, axis=0).astype(BF16)
        for d in range(1, NS):
            tcopy(n, d, False).start()

    def kvcopies(t, s, inward):
        back = t if inward else t - 1
        block = (row + NR + step_of[s] * back) % NR
        rows = pl.ds(pl.multiple_of(block * B, B), B)
        both = [(0, kslab), (1, vslab)]
        return [
            copy(v.at[:, rows, :], v.at[:, rows, :], kv_ss.at[n, s, t - 1], kv_rs.at[n, s, t - 1], row=ring[s])
            for n, v in (both if t < 4 else both[s : s + 1])
        ]

    def ring_slot(n, t):
        for s in range(2):
            if t > 1:
                rcopy(n, t - 1, s, True).wait_recv()
            if t < 5 and not (t == 1 and n < EARLY):
                rcopy(n, t, s, False).start()
        products(n, t - 1)
        if t == 5 and n >= CH - 2:
            for s in y_ways(n):
                ycopy(n, s).start()
        elif t == 5:
            z_start(n)

    def kv_slot(t):
        for s in range(2):
            if t > 1:
                for c in kvcopies(t - 1, s, True):
                    c.wait_recv()
            if t < 5:
                for c in kvcopies(t, s, False):
                    c.start()

    def token_wait(_):
        for c in slab_own_in + slab_on_in:
            c.wait_recv()

    for k in range(CH + 6):
        between = []
        for n in range(CH):
            t = k - n + 1 + (n >= CH - 2)
            if t == 8:
                between.append((triangle, n))
            elif t == 7:
                between.append((y_sum, n))
            elif t == 6 and n < CH - 2:
                between.append((y_start, n))
        if k == 4:
            between.append((token_wait, 0))
        if k in (4, 5):
            between += [(f, k - 4) for f in (token_rows, token_keys, token_queries)]
        for n in range(CH):
            if 1 <= k - n + 1 <= 5:
                ring_slot(n, k - n + 1)
                if between:
                    f, arg = between.pop(0)
                    f(arg)
        if k == CH + 2:
            kv_slot(1)
        for f, arg in between:
            f(arg)

    def unpack(m):
        for n in range(CH):
            for h in range(2):
                both = tri_recv[m, n, h].astype(F32)
                for e in range(2):
                    c = (2 * h + e) * 8 + n
                    r0 = pl.multiple_of(m * 768, 768) + c // 2 * 48 + c % 2 * Q
                    tri_f[pl.ds(r0, Q), :] = both[e * Q : e * Q + Q]

    kv_slot(2)
    tri_recv[samp] = tri_send[samp]
    unpack(samp)
    for d in range(1, NS):
        for n in range(CH):
            tcopy(n, d, True).wait_recv()
        unpack((samp + NS - d) % NS)
    kv_slot(3)

    row0 = samp * Q
    sib, oth = samp + 1 - 2 * (samp % 2), (samp + 2) % NS
    diag = (sib + 2) % NS

    def part_of(n, m):
        return pair_out.at[pl.ds(pl.multiple_of((n * Q + m * 4) * B, 4 * B), 4 * B)]

    def pocopy(k, m, inward):
        there = (sib, oth)[k]
        at = part_of(there if inward else samp, m)
        return copy(at, at, po_ss.at[k, m], po_rs.at[k, m], samp=there)

    def prcopy(inward):
        n = diag if inward else oth
        at = pair_out.at[pl.ds(pl.multiple_of(n * (Q * B), Q * B), Q * B)]
        return copy(at, at, pr_ss, pr_rs, samp=sib)


    def post_rows(m):
        cols = []
        for e in range(4):
            i = m * 4 + e
            cols.append(
                jnp.concatenate(
                    [tri_f[pl.ds(i, 64, stride=48), :], tri_f[pl.ds(Q + i, 64, stride=48), :]], axis=0
                )
            )
        t = jnp.concatenate(cols, axis=1)
        center = t - jnp.mean(t, axis=0, keepdims=True)
        t = center * lax.rsqrt(jnp.mean(center * center, axis=0, keepdims=True) + 1e-05)
        proj = tn(t.astype(BF16), w_op[...])
        proj = jnp.concatenate([proj[e * 128 : e * 128 + B] for e in range(4)], axis=0)
        first = row0 + m * 4
        at = pl.ds(pl.multiple_of(first * B, 4 * B), 4 * B)
        norm_at = pl.ds(pl.multiple_of(first // 16 * CR + first % 16 * B, 32), 4 * B)
        gate = jax.nn.sigmoid(nn(normed[norm_at, :], w_outgate[...]))
        updated = (pair[at, :].astype(F32) + gate * proj).astype(BF16)
        trans_in = normalize(updated, ones).astype(BF16)
        total = updated.astype(F32)
        for n in range(2):
            a = nn(trans_in, w_tg[:, n * 256 : n * 256 + 256])
            u = nn(trans_in, w_tu[:, n * 256 : n * 256 + 256])
            hidden = (a * jax.nn.sigmoid(a) * u).astype(BF16)
            total = total + nn(hidden, w_td[n * 256 : n * 256 + 256, :])
        out = total.astype(BF16)
        bias_in = (normalize(out, ones) * lnb[...]).astype(BF16)
        return at, out, nt(wpbt[...], bias_in)

    for m in range(3):
        done = [post_rows(m * 2 + n) for n in range(2)]
        for n, (at, out, heads) in enumerate(done):
            pair_out[at, :] = out
            for e in range(4):
                hb_f[pl.ds((m * 2 + n) * 4 + e, 16, stride=Q), 0:B] = heads[:, e * B : e * B + B]
        if m < 2:
            for n in range(2):
                pocopy(0, m * 2 + n, False).start()
                pocopy(1, m * 2 + n, False).start()
        if m == 1:
            kv_slot(4)

    for c in range(NC):
        hb_send[c] = hb_f[c * 48 : c * 48 + 48, :].astype(BF16)

    def hcopy(d, inward):
        there, here = (col + d) % NC, (col + NC - d) % NC
        dst = hb.at[here if inward else col, samp]
        return copy(hb_send.at[there], dst, h_ss.at[d], h_rs.at[d], col=there)

    for d in range(1, NC):
        hcopy(d, False).start()
    hb[col, samp] = hb_send[col]

    feature = lax.broadcasted_iota(jnp.int32, (1, B), 1)
    head_masks = [(feature < 48).astype(F32), (feature >= 48).astype(F32)]
    scale = 1.0 / math.sqrt(48)

    def per_head(v):
        return jnp.concatenate([v * m.astype(BF16) for m in head_masks], axis=0)

    def before_bias(s):
        at = slice(s * B, s * B + B)
        raw[s] = nt(per_head(q_s[at, :]), kslab[s]) * scale
        d_probs[s] = nt(per_head(datt_s[at, :]), vslab[s])

    kv_slot(5)
    before_bias(0)
    before_bias(1)
    for d in range(1, NC):
        hcopy(d, True).wait_recv()

    def hgcopy(d, inward):
        return samp_copy(lambda _: hb.at[:, samp], lambda n: hb.at[:, n], hg_ss, hg_rs, d, inward)

    for d in range(1, NS):
        hgcopy(d, False).start()
    for n in range(4, 6):
        pocopy(0, n, False).start()
        pocopy(1, n, False).start()
    before_bias(2)
    before_bias(3)
    for d in range(1, NS):
        hgcopy(d, True).wait_recv()

    for b in range(NC):
        key_mask = (crop[:, b * B : b * B + B] - 1.0) * 10000.0
        quarters = [hb[b, n].astype(F32) for n in range(NS)]
        for h in range(2):
            whole = jnp.concatenate([v[h * Q : h * Q + Q, 0:B] for v in quarters], axis=0)
            bias[h * B : h * B + B, b * B : b * B + B] = whole + key_mask
    acc[...] = jnp.zeros((2 * B, NC * B), F32)
    def att_rows(s):
        at = pl.ds(pl.multiple_of(s * B, B), B)
        scores = raw[s] + bias[...]
        shifted = jnp.exp(scores - jnp.max(scores, axis=-1, keepdims=True))
        probs = shifted * (1.0 / jnp.sum(shifted, axis=-1, keepdims=True))
        got = nn(probs.astype(BF16), vslab[s])
        delta = jnp.sum(per_head(datt_s[at, :]).astype(F32) * got, axis=-1, keepdims=True)
        attended = got[0:B] * head_masks[0] + got[B : 2 * B] * head_masks[1]
        return (gate_s[at, :] * attended).astype(BF16), probs * (d_probs[s] - delta)

    def att_step(m, carry):
        done = [att_rows(m * 2 + e) for e in range(2)]
        acc[...] = acc[...] + (done[0][1] + done[1][1])
        gated = jnp.concatenate([v for v, _ in done], axis=0)
        at = pl.ds(pl.multiple_of(m * 2 * B, 2 * B), 2 * B)
        xd[...] = nn(gated, wo[...])
        for b in range(NC):
            pj_send[b, at, :] = xd[:, b * B : b * B + B].astype(BF16)
        return carry

    lax.fori_loop(0, 2, att_step, 0)
    for m in range(6):
        pocopy(1, m, True).wait_recv()
    prcopy(False).start()

    for b in range(NC):
        heads = [acc[h * B : h * B + B, b * B : b * B + B] for h in range(2)]
        for n in range(NS):
            both = jnp.concatenate([v[n * Q : n * Q + Q] for v in heads], axis=0)
            g_send[n, b, :, 0:B] = both.astype(BF16)

    def gcopy(d, inward):
        return samp_copy(lambda n: g_send.at[n], lambda n: g_recv.at[n], g_ss, g_rs, d, inward)

    for d in range(1, NS):
        gcopy(d, False).start()

    def pycopy(d, x):
        src = pj_send.at[x * 4 + around(d)]
        return copy(src, py_recv.at[d - 1, x], py_ss.at[d, x], py_rs.at[d, x], col=xh * 4 + around(d))

    pys = [(d, x) for d in range(1, 4) for x in range(2)]
    for d, x in pys:
        pycopy(d, x).start()
    g_recv[samp] = g_send[samp]
    for d in range(1, NS):
        gcopy(d, True).wait_recv()

    def sum_step(b, carry):
        total = g_recv[0, b].astype(F32)
        for n in range(1, NS):
            total = total + g_recv[n, b].astype(F32)
        sg[b] = total.astype(BF16)
        return carry

    lax.fori_loop(0, NC, sum_step, 0)

    def ccopy(d, inward):
        there, here = (col + d) % NC, (col + NC - d) % NC
        return copy(sg.at[there], cg.at[here if inward else col], c_ss.at[d], c_rs.at[d], col=there)

    for d in range(1, NC):
        ccopy(d, False).start()
    cg[col] = sg[col]

    for d, x in pys:
        pycopy(d, x).wait_recv()

    def py_step(s, carry):
        at = pl.ds(pl.multiple_of(s * B, B), B)

        def total(x):
            v = pj_send[x * 4 + yy, at, :].astype(F32)
            for d in range(3):
                v = v + py_recv[d, x, at, :].astype(F32)
            return v

        px_own[at, :] = total(xh) + tokens[at, :].astype(F32)
        px_send[at, :] = total(1 - xh).astype(BF16)
        return carry

    lax.fori_loop(0, 4, py_step, 0)
    px = copy(px_send, px_recv, px_ss, px_rs, col=xp)
    px.start()
    for d in range(1, NC):
        ccopy(d, True).wait_recv()
    for c in range(NC):
        cg_f[c * 48 : c * 48 + 48, :] = cg[c].astype(F32)
    for i in range(Q):
        bg[samp, i] = cg_f[pl.ds(i, 16, stride=Q), :].astype(BF16)

    def bcopy(d, inward):
        return samp_copy(lambda _: bg.at[samp], lambda n: bg.at[n], b_ss, b_rs, d, inward)

    for d in range(1, NS):
        bcopy(d, False).start()
    px.wait_recv()
    tokens_out[...] = (px_own[...] + px_recv[...].astype(F32)).astype(BF16)
    for m in range(6):
        pocopy(0, m, True).wait_recv()
    prcopy(True).wait_recv()
    for d in range(1, NS):
        bcopy(d, True).wait_recv()

    for c in [slab_x, px, prcopy(False)] + slab_own + slab_on:
        c.wait_send()
    for d, x in pys:
        pycopy(d, x).wait_send()
    for m in range(6):
        for k in range(2):
            pocopy(k, m, False).wait_send()

    for n in range(CH):
        for s in range(2):
            for t in range(1, 5):
                rcopy(n, t, s, False).wait_send()
        for s in y_ways(n):
            ycopy(n, s).wait_send()
        if n < CH - 2:
            for s in range(2):
                zcopy(n, s).wait_send()
        for d in range(1, NS):
            tcopy(n, d, False).wait_send()
        xcopy(n).wait_send()
    for t in range(1, 5):
        for s in range(2):
            for c in kvcopies(t, s, False):
                c.wait_send()
    for d in range(1, NC):
        hcopy(d, False).wait_send()
        ccopy(d, False).wait_send()
    for d in range(1, NS):
        hgcopy(d, False).wait_send()
        gcopy(d, False).wait_send()
        bcopy(d, False).wait_send()


def split(v):
    high = v.astype(BF16)
    rest = v - high.astype(F32)
    mid = rest.astype(BF16)
    return high, mid, (rest - mid.astype(F32)).astype(BF16)


def finish(pair_rows, token_rows, bg, lnb, wpbt, pair_out, tokens_out, pair_grad):
    @pl.when(pl.program_id(0) == 0)
    def _():
        tokens_out[...] = token_rows[...]

    pair_out[...] = pair_rows[...]
    ones = mean_weights()
    weights = wpbt[...].astype(F32) * lnb[...]
    weights = weights - jnp.mean(weights, axis=-1, keepdims=True)
    weights = jnp.concatenate(split(weights), axis=0)
    empty = jnp.zeros((48, 128), BF16)
    weights = jnp.concatenate(
        [jnp.concatenate([weights, empty], axis=1), jnp.concatenate([empty, weights], axis=1)], axis=0
    )
    for e in range(4):
        at = slice(e * 4 * B, e * 4 * B + 4 * B)
        even, odd = [
            jnp.concatenate([bg[e * 4 + n], bg[e * 4 + 2 + n]], axis=1) for n in range(2)
        ]
        both = tn(jnp.concatenate([even] * 3 + [odd] * 3, axis=0), weights)
        scaled = jnp.concatenate(
            [both[0:B, :128], both[0:B, 128:], both[128 : 128 + B, :128], both[128 : 128 + B, 128:]], axis=0
        )
        center, inv = centered(pair_rows[at, :], ones)
        unit = center * inv
        pair_grad[at, :] = inv * (scaled - unit * row_means((scaled * unit).astype(BF16), ones))


def per_device(
    pair, crop_mask, w_agate, w_aval, w_bgate, w_bval, w_outgate, w_outproj, ln_pair,
    w_trans_gate, w_trans_up, w_trans_down, ln_bias, w_pairbias, tokens, ln_token,
    w_query, w_key, w_value, w_gate, w_output, cotangent,
):
    wpbt = w_pairbias.T
    lnb = ln_bias.reshape(1, 128)
    args = (
        pair.reshape(B * B, 128), crop_mask, crop_mask.reshape(6, 128),
        w_agate, w_aval, w_bgate, w_bval, ln_pair.reshape(1, 128), w_outgate, w_outproj,
        w_trans_gate, w_trans_up, w_trans_down, lnb, wpbt,
        tokens.reshape(4 * B, B), cotangent.reshape(4 * B, B), ln_token.reshape(6, 128),
        w_query.T, w_key.T, w_value.T, w_gate.T, w_output,
    )
    vm = pltpu.VMEM
    dma = pltpu.SemaphoreType.DMA
    scratch = [
        vm((4, 128, 128), BF16),
        vm((128, 128), BF16),
        vm((2 * B, NC * B), F32),
        vm((2 * B, NC * B), F32),
        vm((256, 256), BF16),
        vm((6 * CR, 128), BF16),
        vm((B * B + 32, 128), F32),
        vm((32 * B, 128), F32),
        vm((G * B, 128), F32),
        vm((CH, 3, 2 * B, B), BF16),
        vm((CH, NR, RC, 128), BF16),
        vm((CH, 4, 2, RC, 128), BF16),
        vm((CH, 2, 2, RC // 2, 128), BF16),
        vm((CH, 3, 2, RC, 128), BF16),
        vm((CH, RC, 128), F32),
        vm((CH, RC, 128), BF16),
        vm((CH, RC, 128), BF16),
        vm((NC, 2, 4 * B, B), BF16),
        vm((4 * B, B), BF16),
        vm((4, NR * B, B), BF16),
        vm((4, NR * B, B), BF16),
        vm((4 * B, B), F32),
        vm((4 * B, B), BF16),
        vm((NS, CH, 2, 48, 128), BF16),
        vm((NS, CH, 2, 48, 128), BF16),
        vm((64 * 48, 128), F32),
        vm((16 * Q, 128), F32),
        vm((NC, 48, 128), BF16),
        vm((NC, NS, 48, 128), BF16),
        vm((2 * B, NC * B), F32),
        vm((4, 2 * B, NC * B), F32),
        vm((4, 2 * B, NC * B), F32),
        vm((2 * B, NC * B), F32),
        vm((NS, NC, 48, 128), BF16),
        vm((NS, NC, 48, 128), BF16),
        vm((NC, 4 * B, B), BF16),
        vm((3, 2, 4 * B, B), BF16),
        vm((4 * B, B), F32),
        vm((4 * B, B), BF16),
        vm((4 * B, B), BF16),
        vm((NC, 48, 128), BF16),
        vm((NC, 48, 128), BF16),
        vm((16 * Q, 128), F32),
    ]
    sems = [(7,)] * 2 + [(CH, 2, 4)] * 2 + [(CH, 2)] * 2 + [(CH, 3)] * 2 + [(CH,)] * 2
    sems += [(2, 2, 4)] * 2 + [(CH, 4)] * 2 + [(8,)] * 2 + [(4,)] * 2 + [(2, 6)] * 2 + [None] * 2
    sems += [(4, 2)] * 2 + [None] * 2 + [(4,)] * 2 + [(8,)] * 2 + [(4,)] * 2
    scratch += [dma if s is None else dma(s) for s in sems]
    spec = pl.BlockSpec(memory_space=pltpu.VMEM)
    specs = [spec] * len(args)
    specs[1] = pl.BlockSpec(memory_space=pltpu.SMEM)
    pair_rows, token_rows, bg = pl.pallas_call(
        kernel,
        out_shape=(
            jax.ShapeDtypeStruct((B * B, 128), BF16),
            jax.ShapeDtypeStruct((4 * B, B), BF16),
            jax.ShapeDtypeStruct((NS, Q, 16, 128), BF16),
        ),
        in_specs=specs,
        out_specs=(spec,) * 3,
        scratch_shapes=scratch,
        compiler_params=pltpu.CompilerParams(
            collective_id=0, has_side_effects=True, vmem_limit_bytes=56 * 1024 * 1024
        ),
    )(*args)
    rows = pl.BlockSpec((16 * B, 128), lambda i: (i, 0))
    whole = pl.BlockSpec((4 * B, B), lambda i: (0, 0))
    outs = pl.pallas_call(
        finish,
        grid=(B // 16,),
        out_shape=(
            jax.ShapeDtypeStruct((B * B, 128), BF16),
            jax.ShapeDtypeStruct((4 * B, B), BF16),
            jax.ShapeDtypeStruct((B * B, 128), F32),
        ),
        in_specs=[
            rows,
            whole,
            pl.BlockSpec((16, 16, 128), lambda i: (i, 0, 0)),
            pl.BlockSpec((1, 128), lambda i: (0, 0)),
            pl.BlockSpec((16, 128), lambda i: (0, 0)),
        ],
        out_specs=(rows, whole, rows),
    )(pair_rows, token_rows, bg.reshape(B, 16, 128), lnb, wpbt)
    return (
        outs[0].reshape(B, B, 128),
        outs[1].reshape(4, B, B),
        outs[2].reshape(B, B, 128),
    )


def solution(mesh):
    placed = (
        P("row", "col", None),
        P(), P(), P(), P(), P(), P(), P(), P(), P(), P(), P(), P(), P(),
        P("samp", "row", "col"),
        P(),
        P(None, "col"),
        P(None, "col"),
        P(None, "col"),
        P(None, "col"),
        P("col", None),
        P("samp", "row", "col"),
    )
    return jax.shard_map(
        per_device,
        mesh=mesh,
        in_specs=placed,
        out_specs=(P("row", "col", None), P("samp", "row", "col"), P("row", "col", None)),
        check_vma=False,
    )
```

```python
import math

import jax
import jax.numpy as jnp
from jax import lax
from jax.experimental import pallas as pl
from jax.experimental.pallas import tpu as pltpu
from jax.sharding import PartitionSpec as P

F32 = jnp.float32
BF16 = jnp.bfloat16
MESH = pl.DeviceIdType.MESH
NR = 8
NC = 8
NS = 4
B = 96
Q = 24
G = 24
CH = 8
RC = 3 * B
EARLY = 5
CR = 16 * B


def nt(a, b):
    return lax.dot_general(a, b, (((1,), (1,)), ((), ())), preferred_element_type=F32)


def nn(a, b):
    return lax.dot_general(a, b, (((1,), (0,)), ((), ())), preferred_element_type=F32)


def tn(a, b):
    return lax.dot_general(a, b, (((0,), (0,)), ((), ())), preferred_element_type=F32)


def row_means(values, ones):
    half = values.shape[0] // 2
    out = nn(jnp.concatenate([values[:half], values[half:]], axis=1), ones)
    return jnp.concatenate([out[:, :128], out[:, 128:]], axis=0)


def centered(values, ones):
    values = values.astype(F32)
    center = values - jnp.mean(values, axis=-1, keepdims=True)
    return center, lax.rsqrt(row_means((center * center).astype(BF16), ones) + 1e-05)


def normalize(values, ones):
    center, inv = centered(values, ones)
    return center * inv


def mean_weights():
    first = lax.broadcasted_iota(jnp.int32, (256, 256), 0) < 128
    second = lax.broadcasted_iota(jnp.int32, (256, 256), 1) < 128
    return jnp.where(first == second, 1.0 / 128.0, 0.0).astype(BF16)


def kernel(
    pair, crop_s, crop_v, w_ag, w_av, w_bg, w_bv, lnp, w_outgate, w_outproj, w_tg, w_tu, w_td,
    lnb, wpbt, tokens, cot, lnt, wq, wk, wv, wg, wo,
    pair_out, tokens_out, bg,
    wt, w_op, xd, cd,
    ones_ref, wp2, normed, made, lf, rf, lm, rslab, part, z_recv, y_recv, own_sum, x_send, x_recv, slab, q_s, kslab,
    vslab, gate_s, datt_s, tri_send, tri_recv, tri_f, hb_f, hb_send, hb, bias, raw, d_probs, acc, g_send, g_recv,
    pj_send, py_recv, px_own, px_send, px_recv, sg, cg, cg_f,
    slab_ss, slab_rs, ring_ss, ring_rs, z_ss, z_rs, y_ss, y_rs, x_ss, x_rs,
    kv_ss, kv_rs, t_ss, t_rs, h_ss, h_rs, hg_ss, hg_rs, po_ss, po_rs, pr_ss, pr_rs,
    py_ss, py_rs, px_ss, px_rs, g_ss, g_rs, c_ss, c_rs, b_ss, b_rs,
):
    row = lax.axis_index("row")
    col = lax.axis_index("col")
    samp = lax.axis_index("samp")
    xh = col // 4
    yy = col % 4
    xp = (1 - xh) * 4 + yy
    ones_ref[...] = mean_weights()
    ones = ones_ref[...]
    right = (row + 1) % NR
    left = (row + NR - 1) % NR

    def copy(src, dst, ss, rs, **where):
        return pltpu.make_async_remote_copy(
            src_ref=src, dst_ref=dst, send_sem=ss, recv_sem=rs, device_id=where, device_id_type=MESH
        )

    barrier = pltpu.get_barrier_semaphore()
    for d in range(1, NC):
        pl.semaphore_signal(barrier, inc=1, device_id={"col": (col + d) % NC}, device_id_type=MESH)
    for d in range(1, NR):
        pl.semaphore_signal(barrier, inc=1, device_id={"row": (row + d) % NR}, device_id_type=MESH)
    for d in range(1, NS):
        pl.semaphore_signal(
            barrier, inc=1, device_id={"samp": (samp + d) % NS}, device_id_type=MESH
        )

    def around(d):
        return (yy + d) % 4

    def slab_copy(block, k, there):
        at = slab.at[block]
        return copy(at, at, slab_ss.at[k], slab_rs.at[k], col=there)

    slab_own = [slab_copy(col, d, xh * 4 + around(d)) for d in range(1, 4)]
    slab_own_in = [slab_copy(xh * 4 + around(4 - d), d, xh * 4 + around(d)) for d in range(1, 4)]
    slab_x = slab_copy(col, 0, xp)
    slab_x_in = slab_copy(xp, 0, xp)
    slab_on = [slab_copy(xp, 3 + d, xh * 4 + around(d)) for d in range(1, 4)]
    slab_on_in = [
        slab_copy((1 - xh) * 4 + around(4 - d), 3 + d, xh * 4 + around(d)) for d in range(1, 4)
    ]
    slab[col, 0] = tokens[...]
    slab[col, 1] = cot[...]

    for n, w in enumerate((w_ag, w_av, w_bg, w_bv)):
        wt[n] = w[...].astype(F32).T.astype(BF16)
    wp = jnp.concatenate([wt[n, pl.ds(pl.multiple_of(samp * 32, 32), 32), :] for n in range(4)], axis=0)
    wp2[...] = jnp.concatenate(
        [
            jnp.concatenate([wp, jnp.zeros((128, 128), BF16)], axis=1),
            jnp.concatenate([jnp.zeros((128, 128), BF16), wp], axis=1),
        ],
        axis=0,
    )
    tri_f[0:128, :] = w_outproj[...].astype(F32)
    w_op[...] = jnp.concatenate(
        [tri_f[pl.ds(0, 64, stride=2), :], tri_f[pl.ds(1, 64, stride=2), :]], axis=0
    ).astype(BF16)
    crop = jnp.concatenate([crop_v[i : i + 1, :] for i in range(6)], axis=1).astype(F32)
    token_gain = jnp.concatenate([lnt[i : i + 1, :] for i in range(6)], axis=1)

    def keep_lanes(block):
        kept = jnp.zeros((1, B), F32)
        for b in range(NC):
            kept = jnp.where(block == b, crop[:, b * B : b * B + B], kept)
        return jnp.concatenate([kept, jnp.zeros((1, 32), F32)], axis=1)

    keep_rows, keep_cols = keep_lanes(row), keep_lanes(col)

    made[B * B : B * B + 32, :] = jnp.zeros((32, 128), F32)
    lane = lax.broadcasted_iota(jnp.int32, (8, 128), 1)
    wide = lane < B

    def norm_chunk(m):
        src = pl.ds(pl.multiple_of(m * (16 * B), 16 * B), 16 * B)
        dst = pl.ds(pl.multiple_of(m * CR, 32), 16 * B)
        normed[dst, :] = (normalize(pair[src, :], ones) * lnp[...]).astype(BF16)

    def made_chunk(m):
        halves = [pl.ds(pl.multiple_of(m * CR + n * (CR // 2), CR // 2), CR // 2) for n in range(2)]
        o = nt(jnp.concatenate([normed[at, :] for at in halves], axis=1), wp2[...])
        for n, at in enumerate(halves):
            made[at, :] = o[:, n * 128 : n * 128 + 128]

    def edge(o, first, kept):
        return jax.nn.sigmoid(o[first : first + 32]) * o[first + 32 : first + 64] * kept

    def right_step(m, carry):
        for e in range(8):
            k = m * 8 + e
            rows = jnp.concatenate([made[pl.ds(k, B, stride=B), :], jnp.zeros((32, 128), F32)], axis=0)
            v = edge(rows.T, 64, keep_rows * crop_s[col * B + k].astype(F32))
            for q in range(3):
                packed = jnp.where(wide, v[8 * q : 8 * q + 8], pltpu.roll(v[24:32], 96 - 32 * q, 1))
                rf[pl.ds(k + 8 * B * q, 8, stride=B), :] = packed
        return carry

    def left_step(m, carry):
        for e in range(8):
            i = m * 8 + e
            rows = made[pl.ds(pl.multiple_of(i * B, B), 128), :]
            v = edge(rows.T, 0, keep_cols * crop_s[row * B + i].astype(F32))
            for q in range(4):
                lf[pl.ds(i + 8 * B * q, 8, stride=B), :] = v[8 * q : 8 * q + 8]
        return carry

    norm_chunk(0)

    pl.semaphore_wait(barrier, NC + NR + NS - 3)
    for c in [slab_x] + slab_own:
        c.start()

    def front_step(m, carry):
        made_chunk(m)
        norm_chunk(m + 1)
        return carry

    lax.fori_loop(0, 5, front_step, 0)
    made_chunk(5)
    lax.fori_loop(0, B // 8, right_step, 0)
    slab_x_in.wait_recv()
    for c in slab_on:
        c.start()
    own = lax.broadcasted_iota(jnp.int32, (B, 128), 1) < B
    carriers = [(n, k, pl.ds((k * 8 + n) * B, B)) for n in range(CH) for k in range(3)]
    for n, k, at in carriers:
        rslab[n, row, k * B : k * B + B, :] = rf[at, :].astype(BF16)

    ring = (right, left)
    step_of = (-1, 1)

    def rcopy(n, t, s, inward):
        back = t if inward else t - 1
        block = (row + NR + step_of[s] * back) % NR
        rows = pl.ds(0, RC) if t < 4 else pl.ds(s * (RC // 2), RC // 2)
        at = rslab.at[n, block, rows]
        return copy(at, at, ring_ss.at[n, s, t - 1], ring_rs.at[n, s, t - 1], row=ring[s])

    for n in range(EARLY):
        for s in range(2):
            rcopy(n, 1, s, False).start()
    lax.fori_loop(0, B // 8, left_step, 0)
    for n in range(CH):
        for q in range(3):
            for half, c in enumerate((q * 8 + n, 24 + n)):
                lm[n, q, half * B : half * B + B, :] = lf[c * B : c * B + B, 0:B].astype(BF16)

    def token_rows(pair_of):
        at = pl.ds(pair_of * 2 * B, 2 * B)
        x = [slab[b, 0, at, :].astype(F32) for b in range(NC)]
        total = x[0]
        for b in range(1, NC):
            total = total + x[b]
        mean = jnp.sum(total, axis=-1, keepdims=True) * (1.0 / (NC * B))
        x = [v - mean for v in x]
        total = x[0] * x[0]
        for b in range(1, NC):
            total = total + x[b] * x[b]
        inv = lax.rsqrt(jnp.sum(total, axis=-1, keepdims=True) * (1.0 / (NC * B)) + 1e-05)
        for b in range(NC):
            xd[:, b * B : b * B + B] = x[b] * inv
            cd[:, b * B : b * B + B] = slab[b, 1, at, :].astype(F32)

    def token_keys(pair_of):
        normal = (xd[...] * token_gain).astype(BF16)
        tokens_at = pl.ds(pl.multiple_of(row * B, B), B)
        for w, dest in ((wk, kslab), (wv, vslab)):
            out = nt(normal, w[...]).astype(BF16)
            for e in range(2):
                dest[pair_of * 2 + e, tokens_at, :] = out[e * B : e * B + B]

    def token_queries(pair_of):
        at = pl.ds(pair_of * 2 * B, 2 * B)
        normal = (xd[...] * token_gain).astype(BF16)
        q_s[at, :] = nt(normal, wq[...]).astype(BF16)
        gate = jax.nn.sigmoid(nt(normal, wg[...]))
        gate_s[at, :] = gate
        d = nt(cd[...].astype(BF16), wo[...])
        datt_s[at, :] = (d * gate).astype(BF16)

    def products(n, back):
        if back in (0, 4):
            blocks = [(row + back) % NR]
        else:
            blocks = [(row + NR + step * back) % NR for step in (-1, 1)]
        for q in range(3):
            rights = [rslab[n, j, q * B : q * B + B, :] for j in blocks]
            o = nn(lm[n, q], jnp.concatenate(rights, axis=1))
            for e, j in enumerate(blocks):
                at = slice(e * 128, e * 128 + 128)
                packed = jnp.where(own, o[0:B, at], o[B : 2 * B, at]).astype(BF16)
                part[n, j % 4, j // 4, q * B : q * B + B, :] = packed

    sides = (xh * 4 + (yy + 1) % 4, xh * 4 + (yy + 3) % 4)

    def zcopy(n, s):
        src = part.at[n, (yy + 2) % 4, :, pl.ds(s * (RC // 2), RC // 2)]
        return copy(src, z_recv.at[n, s], z_ss.at[n, s], z_rs.at[n, s], col=sides[s])

    def ycopy(n, s):
        there = (yy + (1, 3, 2)[s]) % 4
        return copy(
            part.at[n, there], y_recv.at[n, s], y_ss.at[n, s], y_rs.at[n, s], col=xh * 4 + there
        )

    def y_ways(n):
        return (0, 1, 2) if n >= CH - 2 else (0, 1)

    def z_start(n):
        for s in range(2):
            zcopy(n, s).start()

    def y_start(n):
        for s in range(2):
            zcopy(n, s).wait_recv()
            for x in range(2):
                at = pl.ds(s * (RC // 2), RC // 2)
                more = z_recv[n, s, x].astype(F32)
                there = (yy + 1 + 2 * s) % 4
                part[n, there, x, at, :] = (part[n, there, x, at, :].astype(F32) + more).astype(BF16)
            ycopy(n, s).start()

    def y_sum(n):
        for s in y_ways(n):
            ycopy(n, s).wait_recv()

        def one(k, carry):
            at = pl.ds(pl.multiple_of(k * B, B), B)

            def total(x):
                v = part[n, yy, x, at, :].astype(F32)
                for s in y_ways(n):
                    v = v + y_recv[n, s, x, at, :].astype(F32)
                return v

            own_sum[n, at, :] = total(xh)
            x_send[n, at, :] = total(1 - xh).astype(BF16)
            return carry

        lax.fori_loop(0, 3, one, 0)
        xcopy(n).start()

    def xcopy(n):
        return copy(x_send.at[n], x_recv.at[n], x_ss.at[n], x_rs.at[n], col=xp)

    def samp_copy(src_of, dst_of, ss, rs, d, inward):
        there, here = (samp + d) % NS, (samp + NS - d) % NS
        return copy(src_of(there), dst_of(here if inward else samp), ss.at[d], rs.at[d], samp=there)

    def tcopy(n, d, inward):
        return samp_copy(
            lambda m: tri_send.at[m, n], lambda m: tri_recv.at[m, n], t_ss.at[n], t_rs.at[n], d, inward
        )

    lane96 = lax.broadcasted_iota(jnp.int32, (B, 128), 1)

    def triangle(n):
        xcopy(n).wait_recv()
        c = []
        for q in range(3):
            at = pl.ds(q * B, B)
            c.append(own_sum[n, at, :] + x_recv[n, at, :].astype(F32))
        tail = jnp.where(
            lane96 < 32,
            pltpu.roll(c[0], 32, 1),
            jnp.where(lane96 < 64, pltpu.roll(c[1], 64, 1), pltpu.roll(c[2], 96, 1)),
        )
        c.append(tail)
        for h in range(2):
            for m in range(NS):
                both = [v[m * Q : m * Q + Q] for v in c[2 * h : 2 * h + 2]]
                tri_send[m, n, h] = jnp.concatenate(both, axis=0).astype(BF16)
        for d in range(1, NS):
            tcopy(n, d, False).start()

    def kvcopies(t, s, inward):
        back = t if inward else t - 1
        block = (row + NR + step_of[s] * back) % NR
        rows = pl.ds(pl.multiple_of(block * B, B), B)
        both = [(0, kslab), (1, vslab)]
        return [
            copy(v.at[:, rows, :], v.at[:, rows, :], kv_ss.at[n, s, t - 1], kv_rs.at[n, s, t - 1], row=ring[s])
            for n, v in (both if t < 4 else both[s : s + 1])
        ]

    def ring_slot(n, t):
        for s in range(2):
            if t > 1:
                rcopy(n, t - 1, s, True).wait_recv()
            if t < 5 and not (t == 1 and n < EARLY):
                rcopy(n, t, s, False).start()
        products(n, t - 1)
        if t == 5 and n >= CH - 2:
            for s in y_ways(n):
                ycopy(n, s).start()
        elif t == 5:
            z_start(n)

    def kv_slot(t):
        for s in range(2):
            if t > 1:
                for c in kvcopies(t - 1, s, True):
                    c.wait_recv()
            if t < 5:
                for c in kvcopies(t, s, False):
                    c.start()

    def token_wait(_):
        for c in slab_own_in + slab_on_in:
            c.wait_recv()

    for k in range(CH + 6):
        between = []
        for n in range(CH):
            t = k - n + 1 + (n >= CH - 2)
            if t == 8:
                between.append((triangle, n))
            elif t == 7:
                between.append((y_sum, n))
            elif t == 6 and n < CH - 2:
                between.append((y_start, n))
        if k == 4:
            between.append((token_wait, 0))
        if k in (4, 5):
            between += [(f, k - 4) for f in (token_rows, token_keys, token_queries)]
        for n in range(CH):
            if 1 <= k - n + 1 <= 5:
                ring_slot(n, k - n + 1)
                if between:
                    f, arg = between.pop(0)
                    f(arg)
        if k == CH + 2:
            kv_slot(1)
        for f, arg in between:
            f(arg)

    def unpack(m):
        for n in range(CH):
            for h in range(2):
                both = tri_recv[m, n, h].astype(F32)
                for e in range(2):
                    c = (2 * h + e) * 8 + n
                    r0 = pl.multiple_of(m * 768, 768) + c // 2 * 48 + c % 2 * Q
                    tri_f[pl.ds(r0, Q), :] = both[e * Q : e * Q + Q]

    kv_slot(2)
    tri_recv[samp] = tri_send[samp]
    unpack(samp)
    for d in range(1, NS):
        for n in range(CH):
            tcopy(n, d, True).wait_recv()
        unpack((samp + NS - d) % NS)
    kv_slot(3)

    row0 = samp * Q
    sib, oth = samp + 1 - 2 * (samp % 2), (samp + 2) % NS
    diag = (sib + 2) % NS

    def part_of(n, m):
        return pair_out.at[pl.ds(pl.multiple_of((n * Q + m * 4) * B, 4 * B), 4 * B)]

    def pocopy(k, m, inward):
        there = (sib, oth)[k]
        at = part_of(there if inward else samp, m)
        return copy(at, at, po_ss.at[k, m], po_rs.at[k, m], samp=there)

    def prcopy(inward):
        n = diag if inward else oth
        at = pair_out.at[pl.ds(pl.multiple_of(n * (Q * B), Q * B), Q * B)]
        return copy(at, at, pr_ss, pr_rs, samp=sib)


    def post_rows(m):
        cols = []
        for e in range(4):
            i = m * 4 + e
            cols.append(
                jnp.concatenate(
                    [tri_f[pl.ds(i, 64, stride=48), :], tri_f[pl.ds(Q + i, 64, stride=48), :]], axis=0
                )
            )
        t = jnp.concatenate(cols, axis=1)
        center = t - jnp.mean(t, axis=0, keepdims=True)
        t = center * lax.rsqrt(jnp.mean(center * center, axis=0, keepdims=True) + 1e-05)
        proj = tn(t.astype(BF16), w_op[...])
        proj = jnp.concatenate([proj[e * 128 : e * 128 + B] for e in range(4)], axis=0)
        first = row0 + m * 4
        at = pl.ds(pl.multiple_of(first * B, 4 * B), 4 * B)
        norm_at = pl.ds(pl.multiple_of(first // 16 * CR + first % 16 * B, 32), 4 * B)
        gate = jax.nn.sigmoid(nn(normed[norm_at, :], w_outgate[...]))
        updated = (pair[at, :].astype(F32) + gate * proj).astype(BF16)
        trans_in = normalize(updated, ones).astype(BF16)
        total = updated.astype(F32)
        for n in range(2):
            a = nn(trans_in, w_tg[:, n * 256 : n * 256 + 256])
            u = nn(trans_in, w_tu[:, n * 256 : n * 256 + 256])
            hidden = (a * jax.nn.sigmoid(a) * u).astype(BF16)
            total = total + nn(hidden, w_td[n * 256 : n * 256 + 256, :])
        out = total.astype(BF16)
        bias_in = (normalize(out, ones) * lnb[...]).astype(BF16)
        return at, out, nt(wpbt[...], bias_in)

    for m in range(3):
        done = [post_rows(m * 2 + n) for n in range(2)]
        for n, (at, out, heads) in enumerate(done):
            pair_out[at, :] = out
            for e in range(4):
                hb_f[pl.ds((m * 2 + n) * 4 + e, 16, stride=Q), 0:B] = heads[:, e * B : e * B + B]
        if m < 2:
            for n in range(2):
                pocopy(0, m * 2 + n, False).start()
                pocopy(1, m * 2 + n, False).start()
        if m == 1:
            kv_slot(4)

    for c in range(NC):
        hb_send[c] = hb_f[c * 48 : c * 48 + 48, :].astype(BF16)

    def hcopy(d, inward):
        there, here = (col + d) % NC, (col + NC - d) % NC
        dst = hb.at[here if inward else col, samp]
        return copy(hb_send.at[there], dst, h_ss.at[d], h_rs.at[d], col=there)

    for d in range(1, NC):
        hcopy(d, False).start()
    hb[col, samp] = hb_send[col]

    feature = lax.broadcasted_iota(jnp.int32, (1, B), 1)
    head_masks = [(feature < 48).astype(F32), (feature >= 48).astype(F32)]
    scale = 1.0 / math.sqrt(48)

    def per_head(v):
        return jnp.concatenate([v * m.astype(BF16) for m in head_masks], axis=0)

    def before_bias(s):
        at = slice(s * B, s * B + B)
        raw[s] = nt(per_head(q_s[at, :]), kslab[s]) * scale
        d_probs[s] = nt(per_head(datt_s[at, :]), vslab[s])

    kv_slot(5)
    before_bias(0)
    before_bias(1)
    for d in range(1, NC):
        hcopy(d, True).wait_recv()

    def hgcopy(d, inward):
        return samp_copy(lambda _: hb.at[:, samp], lambda n: hb.at[:, n], hg_ss, hg_rs, d, inward)

    for d in range(1, NS):
        hgcopy(d, False).start()
    for n in range(4, 6):
        pocopy(0, n, False).start()
        pocopy(1, n, False).start()
    before_bias(2)
    before_bias(3)
    for d in range(1, NS):
        hgcopy(d, True).wait_recv()

    for b in range(NC):
        key_mask = (crop[:, b * B : b * B + B] - 1.0) * 10000.0
        quarters = [hb[b, n].astype(F32) for n in range(NS)]
        for h in range(2):
            whole = jnp.concatenate([v[h * Q : h * Q + Q, 0:B] for v in quarters], axis=0)
            bias[h * B : h * B + B, b * B : b * B + B] = whole + key_mask
    acc[...] = jnp.zeros((2 * B, NC * B), F32)
    def att_rows(s):
        at = pl.ds(pl.multiple_of(s * B, B), B)
        scores = raw[s] + bias[...]
        shifted = jnp.exp(scores - jnp.max(scores, axis=-1, keepdims=True))
        probs = shifted * (1.0 / jnp.sum(shifted, axis=-1, keepdims=True))
        got = nn(probs.astype(BF16), vslab[s])
        delta = jnp.sum(per_head(datt_s[at, :]).astype(F32) * got, axis=-1, keepdims=True)
        attended = got[0:B] * head_masks[0] + got[B : 2 * B] * head_masks[1]
        return (gate_s[at, :] * attended).astype(BF16), probs * (d_probs[s] - delta)

    def att_step(m, carry):
        done = [att_rows(m * 2 + e) for e in range(2)]
        acc[...] = acc[...] + (done[0][1] + done[1][1])
        gated = jnp.concatenate([v for v, _ in done], axis=0)
        at = pl.ds(pl.multiple_of(m * 2 * B, 2 * B), 2 * B)
        xd[...] = nn(gated, wo[...])
        for b in range(NC):
            pj_send[b, at, :] = xd[:, b * B : b * B + B].astype(BF16)
        return carry

    lax.fori_loop(0, 2, att_step, 0)
    for m in range(6):
        pocopy(1, m, True).wait_recv()
    prcopy(False).start()

    for b in range(NC):
        heads = [acc[h * B : h * B + B, b * B : b * B + B] for h in range(2)]
        for n in range(NS):
            both = jnp.concatenate([v[n * Q : n * Q + Q] for v in heads], axis=0)
            g_send[n, b, :, 0:B] = both.astype(BF16)

    def gcopy(d, inward):
        return samp_copy(lambda n: g_send.at[n], lambda n: g_recv.at[n], g_ss, g_rs, d, inward)

    for d in range(1, NS):
        gcopy(d, False).start()

    def pycopy(d, x):
        src = pj_send.at[x * 4 + around(d)]
        return copy(src, py_recv.at[d - 1, x], py_ss.at[d, x], py_rs.at[d, x], col=xh * 4 + around(d))

    pys = [(d, x) for d in range(1, 4) for x in range(2)]
    for d, x in pys:
        pycopy(d, x).start()
    g_recv[samp] = g_send[samp]
    for d in range(1, NS):
        gcopy(d, True).wait_recv()

    def sum_step(b, carry):
        total = g_recv[0, b].astype(F32)
        for n in range(1, NS):
            total = total + g_recv[n, b].astype(F32)
        sg[b] = total.astype(BF16)
        return carry

    lax.fori_loop(0, NC, sum_step, 0)

    def ccopy(d, inward):
        there, here = (col + d) % NC, (col + NC - d) % NC
        return copy(sg.at[there], cg.at[here if inward else col], c_ss.at[d], c_rs.at[d], col=there)

    for d in range(1, NC):
        ccopy(d, False).start()
    cg[col] = sg[col]

    for d, x in pys:
        pycopy(d, x).wait_recv()

    def py_step(s, carry):
        at = pl.ds(pl.multiple_of(s * B, B), B)

        def total(x):
            v = pj_send[x * 4 + yy, at, :].astype(F32)
            for d in range(3):
                v = v + py_recv[d, x, at, :].astype(F32)
            return v

        px_own[at, :] = total(xh) + tokens[at, :].astype(F32)
        px_send[at, :] = total(1 - xh).astype(BF16)
        return carry

    lax.fori_loop(0, 4, py_step, 0)
    px = copy(px_send, px_recv, px_ss, px_rs, col=xp)
    px.start()
    for d in range(1, NC):
        ccopy(d, True).wait_recv()
    for c in range(NC):
        cg_f[c * 48 : c * 48 + 48, :] = cg[c].astype(F32)
    for i in range(Q):
        bg[samp, i] = cg_f[pl.ds(i, 16, stride=Q), :].astype(BF16)

    def bcopy(d, inward):
        return samp_copy(lambda _: bg.at[samp], lambda n: bg.at[n], b_ss, b_rs, d, inward)

    for d in range(1, NS):
        bcopy(d, False).start()
    px.wait_recv()
    tokens_out[...] = (px_own[...] + px_recv[...].astype(F32)).astype(BF16)
    for m in range(6):
        pocopy(0, m, True).wait_recv()
    prcopy(True).wait_recv()
    for d in range(1, NS):
        bcopy(d, True).wait_recv()

    for c in [slab_x, px, prcopy(False)] + slab_own + slab_on:
        c.wait_send()
    for d, x in pys:
        pycopy(d, x).wait_send()
    for m in range(6):
        for k in range(2):
            pocopy(k, m, False).wait_send()

    for n in range(CH):
        for s in range(2):
            for t in range(1, 5):
                rcopy(n, t, s, False).wait_send()
        for s in y_ways(n):
            ycopy(n, s).wait_send()
        if n < CH - 2:
            for s in range(2):
                zcopy(n, s).wait_send()
        for d in range(1, NS):
            tcopy(n, d, False).wait_send()
        xcopy(n).wait_send()
    for t in range(1, 5):
        for s in range(2):
            for c in kvcopies(t, s, False):
                c.wait_send()
    for d in range(1, NC):
        hcopy(d, False).wait_send()
        ccopy(d, False).wait_send()
    for d in range(1, NS):
        hgcopy(d, False).wait_send()
        gcopy(d, False).wait_send()
        bcopy(d, False).wait_send()


def split(v):
    high = v.astype(BF16)
    rest = v - high.astype(F32)
    mid = rest.astype(BF16)
    return high, mid, (rest - mid.astype(F32)).astype(BF16)


def finish(pair_rows, token_rows, bg, lnb, wpbt, pair_out, tokens_out, pair_grad):
    @pl.when(pl.program_id(0) == 0)
    def _():
        tokens_out[...] = token_rows[...]

    pair_out[...] = pair_rows[...]
    ones = mean_weights()
    weights = wpbt[...].astype(F32) * lnb[...]
    weights = weights - jnp.mean(weights, axis=-1, keepdims=True)
    weights = jnp.concatenate(split(weights), axis=0)
    empty = jnp.zeros((48, 128), BF16)
    weights = jnp.concatenate(
        [jnp.concatenate([weights, empty], axis=1), jnp.concatenate([empty, weights], axis=1)], axis=0
    )
    for e in range(4):
        at = slice(e * 4 * B, e * 4 * B + 4 * B)
        even, odd = [
            jnp.concatenate([bg[e * 4 + n], bg[e * 4 + 2 + n]], axis=1) for n in range(2)
        ]
        both = tn(jnp.concatenate([even] * 3 + [odd] * 3, axis=0), weights)
        scaled = jnp.concatenate(
            [both[0:B, :128], both[0:B, 128:], both[128 : 128 + B, :128], both[128 : 128 + B, 128:]], axis=0
        )
        center, inv = centered(pair_rows[at, :], ones)
        unit = center * inv
        pair_grad[at, :] = inv * (scaled - unit * row_means((scaled * unit).astype(BF16), ones))


def per_device(
    pair, crop_mask, w_agate, w_aval, w_bgate, w_bval, w_outgate, w_outproj, ln_pair,
    w_trans_gate, w_trans_up, w_trans_down, ln_bias, w_pairbias, tokens, ln_token,
    w_query, w_key, w_value, w_gate, w_output, cotangent,
):
    wpbt = w_pairbias.T
    lnb = ln_bias.reshape(1, 128)
    args = (
        pair.reshape(B * B, 128), crop_mask, crop_mask.reshape(6, 128),
        w_agate, w_aval, w_bgate, w_bval, ln_pair.reshape(1, 128), w_outgate, w_outproj,
        w_trans_gate, w_trans_up, w_trans_down, lnb, wpbt,
        tokens.reshape(4 * B, B), cotangent.reshape(4 * B, B), ln_token.reshape(6, 128),
        w_query.T, w_key.T, w_value.T, w_gate.T, w_output,
    )
    vm = pltpu.VMEM
    dma = pltpu.SemaphoreType.DMA
    scratch = [
        vm((4, 128, 128), BF16),
        vm((128, 128), BF16),
        vm((2 * B, NC * B), F32),
        vm((2 * B, NC * B), F32),
        vm((256, 256), BF16),
        vm((256, 256), BF16),
        vm((6 * CR, 128), BF16),
        vm((B * B + 32, 128), F32),
        vm((32 * B, 128), F32),
        vm((G * B, 128), F32),
        vm((CH, 3, 2 * B, B), BF16),
        vm((CH, NR, RC, 128), BF16),
        vm((CH, 4, 2, RC, 128), BF16),
        vm((CH, 2, 2, RC // 2, 128), BF16),
        vm((CH, 3, 2, RC, 128), BF16),
        vm((CH, RC, 128), F32),
        vm((CH, RC, 128), BF16),
        vm((CH, RC, 128), BF16),
        vm((NC, 2, 4 * B, B), BF16),
        vm((4 * B, B), BF16),
        vm((4, NR * B, B), BF16),
        vm((4, NR * B, B), BF16),
        vm((4 * B, B), F32),
        vm((4 * B, B), BF16),
        vm((NS, CH, 2, 48, 128), BF16),
        vm((NS, CH, 2, 48, 128), BF16),
        vm((64 * 48, 128), F32),
        vm((16 * Q, 128), F32),
        vm((NC, 48, 128), BF16),
        vm((NC, NS, 48, 128), BF16),
        vm((2 * B, NC * B), F32),
        vm((4, 2 * B, NC * B), F32),
        vm((4, 2 * B, NC * B), F32),
        vm((2 * B, NC * B), F32),
        vm((NS, NC, 48, 128), BF16),
        vm((NS, NC, 48, 128), BF16),
        vm((NC, 4 * B, B), BF16),
        vm((3, 2, 4 * B, B), BF16),
        vm((4 * B, B), F32),
        vm((4 * B, B), BF16),
        vm((4 * B, B), BF16),
        vm((NC, 48, 128), BF16),
        vm((NC, 48, 128), BF16),
        vm((16 * Q, 128), F32),
    ]
    sems = [(7,)] * 2 + [(CH, 2, 4)] * 2 + [(CH, 2)] * 2 + [(CH, 3)] * 2 + [(CH,)] * 2
    sems += [(2, 2, 4)] * 2 + [(CH, 4)] * 2 + [(8,)] * 2 + [(4,)] * 2 + [(2, 6)] * 2 + [None] * 2
    sems += [(4, 2)] * 2 + [None] * 2 + [(4,)] * 2 + [(8,)] * 2 + [(4,)] * 2
    scratch += [dma if s is None else dma(s) for s in sems]
    spec = pl.BlockSpec(memory_space=pltpu.VMEM)
    specs = [spec] * len(args)
    specs[1] = pl.BlockSpec(memory_space=pltpu.SMEM)
    pair_rows, token_rows, bg = pl.pallas_call(
        kernel,
        out_shape=(
            jax.ShapeDtypeStruct((B * B, 128), BF16),
            jax.ShapeDtypeStruct((4 * B, B), BF16),
            jax.ShapeDtypeStruct((NS, Q, 16, 128), BF16),
        ),
        in_specs=specs,
        out_specs=(spec,) * 3,
        scratch_shapes=scratch,
        compiler_params=pltpu.CompilerParams(
            collective_id=0, has_side_effects=True, vmem_limit_bytes=56 * 1024 * 1024
        ),
    )(*args)
    rows = pl.BlockSpec((16 * B, 128), lambda i: (i, 0))
    whole = pl.BlockSpec((4 * B, B), lambda i: (0, 0))
    outs = pl.pallas_call(
        finish,
        grid=(B // 16,),
        out_shape=(
            jax.ShapeDtypeStruct((B * B, 128), BF16),
            jax.ShapeDtypeStruct((4 * B, B), BF16),
            jax.ShapeDtypeStruct((B * B, 128), F32),
        ),
        in_specs=[
            rows,
            whole,
            pl.BlockSpec((16, 16, 128), lambda i: (i, 0, 0)),
            pl.BlockSpec((1, 128), lambda i: (0, 0)),
            pl.BlockSpec((16, 128), lambda i: (0, 0)),
        ],
        out_specs=(rows, whole, rows),
    )(pair_rows, token_rows, bg.reshape(B, 16, 128), lnb, wpbt)
    return (
        outs[0].reshape(B, B, 128),
        outs[1].reshape(4, B, B),
        outs[2].reshape(B, B, 128),
    )


def solution(mesh):
    placed = (
        P("row", "col", None),
        P(), P(), P(), P(), P(), P(), P(), P(), P(), P(), P(), P(), P(),
        P("samp", "row", "col"),
        P(),
        P(None, "col"),
        P(None, "col"),
        P(None, "col"),
        P(None, "col"),
        P("col", None),
        P("samp", "row", "col"),
    )
    return jax.shard_map(
        per_device,
        mesh=mesh,
        in_specs=placed,
        out_specs=(P("row", "col", None), P("samp", "row", "col"), P("row", "col", None)),
        check_vma=False,
    )
```

```python
import math

import jax
import jax.numpy as jnp
from jax import lax
from jax.experimental import pallas as pl
from jax.experimental.pallas import tpu as pltpu
from jax.sharding import PartitionSpec as P

F32 = jnp.float32
BF16 = jnp.bfloat16
MESH = pl.DeviceIdType.MESH
NR = 8
NC = 8
NS = 4
B = 96
Q = 24
G = 24
CH = 8
RC = 3 * B
EARLY = 5
CR = 16 * B


def nt(a, b):
    return lax.dot_general(a, b, (((1,), (1,)), ((), ())), preferred_element_type=F32)


def nn(a, b):
    return lax.dot_general(a, b, (((1,), (0,)), ((), ())), preferred_element_type=F32)


def tn(a, b):
    return lax.dot_general(a, b, (((0,), (0,)), ((), ())), preferred_element_type=F32)


def row_means(values, ones):
    half = values.shape[0] // 2
    out = nn(jnp.concatenate([values[:half], values[half:]], axis=1), ones)
    return jnp.concatenate([out[:, :128], out[:, 128:]], axis=0)


def centered(values, ones):
    values = values.astype(F32)
    center = values - jnp.mean(values, axis=-1, keepdims=True)
    return center, lax.rsqrt(row_means((center * center).astype(BF16), ones) + 1e-05)


def normalize(values, ones):
    center, inv = centered(values, ones)
    return center * inv


def mean_weights():
    first = lax.broadcasted_iota(jnp.int32, (256, 256), 0) < 128
    second = lax.broadcasted_iota(jnp.int32, (256, 256), 1) < 128
    return jnp.where(first == second, 1.0 / 128.0, 0.0).astype(BF16)


def kernel(
    pair, crop_s, crop_v, w_ag, w_av, w_bg, w_bv, lnp, w_outgate, w_outproj, w_tg, w_tu, w_td,
    lnb, wpbt, tokens, cot, lnt, wq, wk, wv, wg, wo,
    pair_out, tokens_out, bg,
    wt, w_op, xd, cd,
    ones_ref, wp2, normed, made, lf, rf, lm, rslab, part, z_recv, y_recv, own_sum, x_send, x_recv, slab, q_s, kslab,
    vslab, gate_s, datt_s, tri_send, tri_recv, tri_f, hb_f, hb_send, hb, bias, raw, d_probs, acc, g_send, g_recv,
    pj_send, py_recv, px_own, px_send, px_recv, sg, cg, cg_f,
    slab_ss, slab_rs, ring_ss, ring_rs, z_ss, z_rs, y_ss, y_rs, x_ss, x_rs,
    kv_ss, kv_rs, t_ss, t_rs, h_ss, h_rs, hg_ss, hg_rs, po_ss, po_rs, pr_ss, pr_rs,
    py_ss, py_rs, px_ss, px_rs, g_ss, g_rs, c_ss, c_rs, b_ss, b_rs,
):
    row = lax.axis_index("row")
    col = lax.axis_index("col")
    samp = lax.axis_index("samp")
    xh = col // 4
    yy = col % 4
    xp = (1 - xh) * 4 + yy
    ones_ref[...] = mean_weights()
    ones = ones_ref[...]
    right = (row + 1) % NR
    left = (row + NR - 1) % NR

    def copy(src, dst, ss, rs, **where):
        return pltpu.make_async_remote_copy(
            src_ref=src, dst_ref=dst, send_sem=ss, recv_sem=rs, device_id=where, device_id_type=MESH
        )

    barrier = pltpu.get_barrier_semaphore()
    for d in range(1, NC):
        pl.semaphore_signal(barrier, inc=1, device_id={"col": (col + d) % NC}, device_id_type=MESH)
    for d in range(1, NR):
        pl.semaphore_signal(barrier, inc=1, device_id={"row": (row + d) % NR}, device_id_type=MESH)
    for d in range(1, NS):
        pl.semaphore_signal(
            barrier, inc=1, device_id={"samp": (samp + d) % NS}, device_id_type=MESH
        )

    def around(d):
        return (yy + d) % 4

    def slab_copy(block, k, there):
        at = slab.at[block]
        return copy(at, at, slab_ss.at[k], slab_rs.at[k], col=there)

    slab_own = [slab_copy(col, d, xh * 4 + around(d)) for d in range(1, 4)]
    slab_own_in = [slab_copy(xh * 4 + around(4 - d), d, xh * 4 + around(d)) for d in range(1, 4)]
    slab_x = slab_copy(col, 0, xp)
    slab_x_in = slab_copy(xp, 0, xp)
    slab_on = [slab_copy(xp, 3 + d, xh * 4 + around(d)) for d in range(1, 4)]
    slab_on_in = [
        slab_copy((1 - xh) * 4 + around(4 - d), 3 + d, xh * 4 + around(d)) for d in range(1, 4)
    ]
    slab[col, 0] = tokens[...]
    slab[col, 1] = cot[...]

    for n, w in enumerate((w_ag, w_av, w_bg, w_bv)):
        wt[n] = w[...].astype(F32).T.astype(BF16)
    wp = jnp.concatenate([wt[n, pl.ds(pl.multiple_of(samp * 32, 32), 32), :] for n in range(4)], axis=0)
    wp2[...] = jnp.concatenate(
        [
            jnp.concatenate([wp, jnp.zeros((128, 128), BF16)], axis=1),
            jnp.concatenate([jnp.zeros((128, 128), BF16), wp], axis=1),
        ],
        axis=0,
    )
    tri_f[0:128, :] = w_outproj[...].astype(F32)
    w_op[0:128, 0:128] = jnp.concatenate(
        [tri_f[pl.ds(0, 64, stride=2), :], tri_f[pl.ds(1, 64, stride=2), :]], axis=0
    ).astype(BF16)
    w_op[0:128, 128:256] = jnp.zeros((128, 128), BF16)
    w_op[128:256, 0:128] = jnp.zeros((128, 128), BF16)
    w_op[128:256, 128:256] = w_outgate[...]
    crop = jnp.concatenate([crop_v[i : i + 1, :] for i in range(6)], axis=1).astype(F32)
    token_gain = jnp.concatenate([lnt[i : i + 1, :] for i in range(6)], axis=1)

    def keep_lanes(block):
        kept = jnp.zeros((1, B), F32)
        for b in range(NC):
            kept = jnp.where(block == b, crop[:, b * B : b * B + B], kept)
        return jnp.concatenate([kept, jnp.zeros((1, 32), F32)], axis=1)

    keep_rows, keep_cols = keep_lanes(row), keep_lanes(col)

    made[B * B : B * B + 32, :] = jnp.zeros((32, 128), F32)
    lane = lax.broadcasted_iota(jnp.int32, (8, 128), 1)
    wide = lane < B

    def norm_chunk(m):
        src = pl.ds(pl.multiple_of(m * (16 * B), 16 * B), 16 * B)
        dst = pl.ds(pl.multiple_of(m * CR, 32), 16 * B)
        normed[dst, :] = (normalize(pair[src, :], ones) * lnp[...]).astype(BF16)

    def made_chunk(m):
        halves = [pl.ds(pl.multiple_of(m * CR + n * (CR // 2), CR // 2), CR // 2) for n in range(2)]
        o = nt(jnp.concatenate([normed[at, :] for at in halves], axis=1), wp2[...])
        for n, at in enumerate(halves):
            made[at, :] = o[:, n * 128 : n * 128 + 128]

    def edge(o, first, kept):
        return jax.nn.sigmoid(o[first : first + 32]) * o[first + 32 : first + 64] * kept

    def right_step(m, carry):
        for e in range(8):
            k = m * 8 + e
            rows = jnp.concatenate([made[pl.ds(k, B, stride=B), :], jnp.zeros((32, 128), F32)], axis=0)
            v = edge(rows.T, 64, keep_rows * crop_s[col * B + k].astype(F32))
            for q in range(3):
                packed = jnp.where(wide, v[8 * q : 8 * q + 8], pltpu.roll(v[24:32], 96 - 32 * q, 1))
                rf[pl.ds(k + 8 * B * q, 8, stride=B), :] = packed
        return carry

    def left_step(m, carry):
        for e in range(8):
            i = m * 8 + e
            rows = made[pl.ds(pl.multiple_of(i * B, B), 128), :]
            v = edge(rows.T, 0, keep_cols * crop_s[row * B + i].astype(F32))
            for q in range(4):
                lf[pl.ds(i + 8 * B * q, 8, stride=B), :] = v[8 * q : 8 * q + 8]
        return carry

    norm_chunk(0)

    pl.semaphore_wait(barrier, NC + NR + NS - 3)
    for c in [slab_x] + slab_own:
        c.start()

    def front_step(m, carry):
        made_chunk(m)
        norm_chunk(m + 1)
        return carry

    lax.fori_loop(0, 5, front_step, 0)
    made_chunk(5)
    lax.fori_loop(0, B // 8, right_step, 0)
    slab_x_in.wait_recv()
    for c in slab_on:
        c.start()
    own = lax.broadcasted_iota(jnp.int32, (B, 128), 1) < B
    carriers = [(n, k, pl.ds((k * 8 + n) * B, B)) for n in range(CH) for k in range(3)]
    for n, k, at in carriers:
        rslab[n, row, k * B : k * B + B, :] = rf[at, :].astype(BF16)

    ring = (right, left)
    step_of = (-1, 1)

    def rcopy(n, t, s, inward):
        back = t if inward else t - 1
        block = (row + NR + step_of[s] * back) % NR
        rows = pl.ds(0, RC) if t < 4 else pl.ds(s * (RC // 2), RC // 2)
        at = rslab.at[n, block, rows]
        return copy(at, at, ring_ss.at[n, s, t - 1], ring_rs.at[n, s, t - 1], row=ring[s])

    for n in range(EARLY):
        for s in range(2):
            rcopy(n, 1, s, False).start()
    lax.fori_loop(0, B // 8, left_step, 0)
    for n in range(CH):
        for q in range(3):
            for half, c in enumerate((q * 8 + n, 24 + n)):
                lm[n, q, half * B : half * B + B, :] = lf[c * B : c * B + B, 0:B].astype(BF16)

    def token_rows(pair_of):
        at = pl.ds(pair_of * 2 * B, 2 * B)
        x = [slab[b, 0, at, :].astype(F32) for b in range(NC)]
        total = x[0]
        for b in range(1, NC):
            total = total + x[b]
        mean = jnp.sum(total, axis=-1, keepdims=True) * (1.0 / (NC * B))
        x = [v - mean for v in x]
        total = x[0] * x[0]
        for b in range(1, NC):
            total = total + x[b] * x[b]
        inv = lax.rsqrt(jnp.sum(total, axis=-1, keepdims=True) * (1.0 / (NC * B)) + 1e-05)
        for b in range(NC):
            xd[:, b * B : b * B + B] = x[b] * inv
            cd[:, b * B : b * B + B] = slab[b, 1, at, :].astype(F32)

    def token_keys(pair_of):
        normal = (xd[...] * token_gain).astype(BF16)
        tokens_at = pl.ds(pl.multiple_of(row * B, B), B)
        for w, dest in ((wk, kslab), (wv, vslab)):
            out = nt(normal, w[...]).astype(BF16)
            for e in range(2):
                dest[pair_of * 2 + e, tokens_at, :] = out[e * B : e * B + B]

    def token_queries(pair_of):
        at = pl.ds(pair_of * 2 * B, 2 * B)
        normal = (xd[...] * token_gain).astype(BF16)
        q_s[at, :] = nt(normal, wq[...]).astype(BF16)
        gate = jax.nn.sigmoid(nt(normal, wg[...]))
        gate_s[at, :] = gate
        d = nt(cd[...].astype(BF16), wo[...])
        datt_s[at, :] = (d * gate).astype(BF16)

    def products(n, back):
        if back in (0, 4):
            blocks = [(row + back) % NR]
        else:
            blocks = [(row + NR + step * back) % NR for step in (-1, 1)]
        for q in range(3):
            rights = [rslab[n, j, q * B : q * B + B, :] for j in blocks]
            o = nn(lm[n, q], jnp.concatenate(rights, axis=1))
            for e, j in enumerate(blocks):
                at = slice(e * 128, e * 128 + 128)
                packed = jnp.where(own, o[0:B, at], o[B : 2 * B, at]).astype(BF16)
                part[n, j % 4, j // 4, q * B : q * B + B, :] = packed

    sides = (xh * 4 + (yy + 1) % 4, xh * 4 + (yy + 3) % 4)

    def zcopy(n, s):
        src = part.at[n, (yy + 2) % 4, :, pl.ds(s * (RC // 2), RC // 2)]
        return copy(src, z_recv.at[n, s], z_ss.at[n, s], z_rs.at[n, s], col=sides[s])

    def ycopy(n, s):
        there = (yy + (1, 3, 2)[s]) % 4
        return copy(
            part.at[n, there], y_recv.at[n, s], y_ss.at[n, s], y_rs.at[n, s], col=xh * 4 + there
        )

    def y_ways(n):
        return (0, 1, 2) if n >= CH - 2 else (0, 1)

    def z_start(n):
        for s in range(2):
            zcopy(n, s).start()

    def y_start(n):
        for s in range(2):
            zcopy(n, s).wait_recv()
            for x in range(2):
                at = pl.ds(s * (RC // 2), RC // 2)
                more = z_recv[n, s, x].astype(F32)
                there = (yy + 1 + 2 * s) % 4
                part[n, there, x, at, :] = (part[n, there, x, at, :].astype(F32) + more).astype(BF16)
            ycopy(n, s).start()

    def y_sum(n):
        for s in y_ways(n):
            ycopy(n, s).wait_recv()

        def one(k, carry):
            at = pl.ds(pl.multiple_of(k * B, B), B)

            def total(x):
                v = part[n, yy, x, at, :].astype(F32)
                for s in y_ways(n):
                    v = v + y_recv[n, s, x, at, :].astype(F32)
                return v

            own_sum[n, at, :] = total(xh)
            x_send[n, at, :] = total(1 - xh).astype(BF16)
            return carry

        lax.fori_loop(0, 3, one, 0)
        xcopy(n).start()

    def xcopy(n):
        return copy(x_send.at[n], x_recv.at[n], x_ss.at[n], x_rs.at[n], col=xp)

    def samp_copy(src_of, dst_of, ss, rs, d, inward):
        there, here = (samp + d) % NS, (samp + NS - d) % NS
        return copy(src_of(there), dst_of(here if inward else samp), ss.at[d], rs.at[d], samp=there)

    def tcopy(n, d, inward):
        return samp_copy(
            lambda m: tri_send.at[m, n], lambda m: tri_recv.at[m, n], t_ss.at[n], t_rs.at[n], d, inward
        )

    lane96 = lax.broadcasted_iota(jnp.int32, (B, 128), 1)

    def triangle(n):
        xcopy(n).wait_recv()
        c = []
        for q in range(3):
            at = pl.ds(q * B, B)
            c.append(own_sum[n, at, :] + x_recv[n, at, :].astype(F32))
        tail = jnp.where(
            lane96 < 32,
            pltpu.roll(c[0], 32, 1),
            jnp.where(lane96 < 64, pltpu.roll(c[1], 64, 1), pltpu.roll(c[2], 96, 1)),
        )
        c.append(tail)
        for h in range(2):
            for m in range(NS):
                both = [v[m * Q : m * Q + Q] for v in c[2 * h : 2 * h + 2]]
                tri_send[m, n, h] = jnp.concatenate(both, axis=0).astype(BF16)
        for d in range(1, NS):
            tcopy(n, d, False).start()

    def kvcopies(t, s, inward):
        back = t if inward else t - 1
        block = (row + NR + step_of[s] * back) % NR
        rows = pl.ds(pl.multiple_of(block * B, B), B)
        both = [(0, kslab), (1, vslab)]
        return [
            copy(v.at[:, rows, :], v.at[:, rows, :], kv_ss.at[n, s, t - 1], kv_rs.at[n, s, t - 1], row=ring[s])
            for n, v in (both if t < 4 else both[s : s + 1])
        ]

    def ring_slot(n, t):
        for s in range(2):
            if t > 1:
                rcopy(n, t - 1, s, True).wait_recv()
            if t < 5 and not (t == 1 and n < EARLY):
                rcopy(n, t, s, False).start()
        products(n, t - 1)
        if t == 5 and n >= CH - 2:
            for s in y_ways(n):
                ycopy(n, s).start()
        elif t == 5:
            z_start(n)

    def kv_slot(t):
        for s in range(2):
            if t > 1:
                for c in kvcopies(t - 1, s, True):
                    c.wait_recv()
            if t < 5:
                for c in kvcopies(t, s, False):
                    c.start()

    def token_wait(_):
        for c in slab_own_in + slab_on_in:
            c.wait_recv()

    for k in range(CH + 6):
        between = []
        for n in range(CH):
            t = k - n + 1 + (n >= CH - 2)
            if t == 8:
                between.append((triangle, n))
            elif t == 7:
                between.append((y_sum, n))
            elif t == 6 and n < CH - 2:
                between.append((y_start, n))
        if k == 4:
            between.append((token_wait, 0))
        if k in (4, 5):
            between += [(f, k - 4) for f in (token_rows, token_keys, token_queries)]
        for n in range(CH):
            if 1 <= k - n + 1 <= 5:
                ring_slot(n, k - n + 1)
                if between:
                    f, arg = between.pop(0)
                    f(arg)
        if k == CH + 2:
            kv_slot(1)
        for f, arg in between:
            f(arg)

    def unpack(m):
        for n in range(CH):
            for h in range(2):
                both = tri_recv[m, n, h].astype(F32)
                for e in range(2):
                    c = (2 * h + e) * 8 + n
                    r0 = pl.multiple_of(m * 768, 768) + c // 2 * 48 + c % 2 * Q
                    tri_f[pl.ds(r0, Q), :] = both[e * Q : e * Q + Q]

    kv_slot(2)
    tri_recv[samp] = tri_send[samp]
    unpack(samp)
    for d in range(1, NS):
        for n in range(CH):
            tcopy(n, d, True).wait_recv()
        unpack((samp + NS - d) % NS)
    kv_slot(3)

    row0 = samp * Q
    sib, oth = samp + 1 - 2 * (samp % 2), (samp + 2) % NS
    diag = (sib + 2) % NS

    def part_of(n, m):
        return pair_out.at[pl.ds(pl.multiple_of((n * Q + m * 4) * B, 4 * B), 4 * B)]

    def pocopy(k, m, inward):
        there = (sib, oth)[k]
        at = part_of(there if inward else samp, m)
        return copy(at, at, po_ss.at[k, m], po_rs.at[k, m], samp=there)

    def prcopy(inward):
        n = diag if inward else oth
        at = pair_out.at[pl.ds(pl.multiple_of(n * (Q * B), Q * B), Q * B)]
        return copy(at, at, pr_ss, pr_rs, samp=sib)


    def post_rows(m):
        cols = []
        for e in range(4):
            i = m * 4 + e
            cols.append(
                jnp.concatenate(
                    [tri_f[pl.ds(i, 64, stride=48), :], tri_f[pl.ds(Q + i, 64, stride=48), :]], axis=0
                )
            )
        t = jnp.concatenate(cols, axis=1)
        center = t - jnp.mean(t, axis=0, keepdims=True)
        t = center * lax.rsqrt(jnp.mean(center * center, axis=0, keepdims=True) + 1e-05)
        t = t.T.astype(BF16)
        t = jnp.concatenate([t[e * 128 : e * 128 + B] for e in range(4)], axis=0)
        first = row0 + m * 4
        at = pl.ds(pl.multiple_of(first * B, 4 * B), 4 * B)
        norm_at = pl.ds(pl.multiple_of(first // 16 * CR + first % 16 * B, 32), 4 * B)
        o = nn(jnp.concatenate([t, normed[norm_at, :]], axis=1), w_op[...])
        updated = (pair[at, :].astype(F32) + jax.nn.sigmoid(o[:, 128:]) * o[:, :128]).astype(BF16)
        trans_in = normalize(updated, ones).astype(BF16)
        total = updated.astype(F32)
        for n in range(2):
            a = nn(trans_in, w_tg[:, n * 256 : n * 256 + 256])
            u = nn(trans_in, w_tu[:, n * 256 : n * 256 + 256])
            hidden = (a * jax.nn.sigmoid(a) * u).astype(BF16)
            total = total + nn(hidden, w_td[n * 256 : n * 256 + 256, :])
        out = total.astype(BF16)
        bias_in = (normalize(out, ones) * lnb[...]).astype(BF16)
        return at, out, nt(wpbt[...], bias_in)

    for m in range(3):
        done = [post_rows(m * 2 + n) for n in range(2)]
        for n, (at, out, heads) in enumerate(done):
            pair_out[at, :] = out
            for e in range(4):
                hb_f[pl.ds((m * 2 + n) * 4 + e, 16, stride=Q), 0:B] = heads[:, e * B : e * B + B]
        if m < 2:
            for n in range(2):
                pocopy(0, m * 2 + n, False).start()
                pocopy(1, m * 2 + n, False).start()
        if m == 1:
            kv_slot(4)

    for c in range(NC):
        hb_send[c] = hb_f[c * 48 : c * 48 + 48, :].astype(BF16)

    def hcopy(d, inward):
        there, here = (col + d) % NC, (col + NC - d) % NC
        dst = hb.at[here if inward else col, samp]
        return copy(hb_send.at[there], dst, h_ss.at[d], h_rs.at[d], col=there)

    for d in range(1, NC):
        hcopy(d, False).start()
    hb[col, samp] = hb_send[col]

    feature = lax.broadcasted_iota(jnp.int32, (1, B), 1)
    head_masks = [(feature < 48).astype(F32), (feature >= 48).astype(F32)]
    scale = 1.0 / math.sqrt(48)

    def per_head(v):
        return jnp.concatenate([v * m.astype(BF16) for m in head_masks], axis=0)

    def before_bias(s):
        at = slice(s * B, s * B + B)
        raw[s] = nt(per_head(q_s[at, :]), kslab[s]) * scale
        d_probs[s] = nt(per_head(datt_s[at, :]), vslab[s])

    kv_slot(5)
    before_bias(0)
    before_bias(1)
    for d in range(1, NC):
        hcopy(d, True).wait_recv()

    def hgcopy(d, inward):
        return samp_copy(lambda _: hb.at[:, samp], lambda n: hb.at[:, n], hg_ss, hg_rs, d, inward)

    for d in range(1, NS):
        hgcopy(d, False).start()
    for n in range(4, 6):
        pocopy(0, n, False).start()
        pocopy(1, n, False).start()
    before_bias(2)
    before_bias(3)
    for d in range(1, NS):
        hgcopy(d, True).wait_recv()

    for b in range(NC):
        key_mask = (crop[:, b * B : b * B + B] - 1.0) * 10000.0
        quarters = [hb[b, n].astype(F32) for n in range(NS)]
        for h in range(2):
            whole = jnp.concatenate([v[h * Q : h * Q + Q, 0:B] for v in quarters], axis=0)
            bias[h * B : h * B + B, b * B : b * B + B] = whole + key_mask
    acc[...] = jnp.zeros((2 * B, NC * B), F32)
    def att_rows(s):
        at = pl.ds(pl.multiple_of(s * B, B), B)
        scores = raw[s] + bias[...]
        shifted = jnp.exp(scores - jnp.max(scores, axis=-1, keepdims=True))
        probs = shifted * (1.0 / jnp.sum(shifted, axis=-1, keepdims=True))
        got = nn(probs.astype(BF16), vslab[s])
        delta = jnp.sum(per_head(datt_s[at, :]).astype(F32) * got, axis=-1, keepdims=True)
        attended = got[0:B] * head_masks[0] + got[B : 2 * B] * head_masks[1]
        return (gate_s[at, :] * attended).astype(BF16), probs * (d_probs[s] - delta)

    def att_step(m, carry):
        done = [att_rows(m * 2 + e) for e in range(2)]
        acc[...] = acc[...] + (done[0][1] + done[1][1])
        gated = jnp.concatenate([v for v, _ in done], axis=0)
        at = pl.ds(pl.multiple_of(m * 2 * B, 2 * B), 2 * B)
        xd[...] = nn(gated, wo[...])
        for b in range(NC):
            pj_send[b, at, :] = xd[:, b * B : b * B + B].astype(BF16)
        return carry

    lax.fori_loop(0, 2, att_step, 0)
    for m in range(6):
        pocopy(1, m, True).wait_recv()
    prcopy(False).start()

    for b in range(NC):
        heads = [acc[h * B : h * B + B, b * B : b * B + B] for h in range(2)]
        for n in range(NS):
            both = jnp.concatenate([v[n * Q : n * Q + Q] for v in heads], axis=0)
            g_send[n, b, :, 0:B] = both.astype(BF16)

    def gcopy(d, inward):
        return samp_copy(lambda n: g_send.at[n], lambda n: g_recv.at[n], g_ss, g_rs, d, inward)

    for d in range(1, NS):
        gcopy(d, False).start()

    def pycopy(d, x):
        src = pj_send.at[x * 4 + around(d)]
        return copy(src, py_recv.at[d - 1, x], py_ss.at[d, x], py_rs.at[d, x], col=xh * 4 + around(d))

    pys = [(d, x) for d in range(1, 4) for x in range(2)]
    for d, x in pys:
        pycopy(d, x).start()
    g_recv[samp] = g_send[samp]
    for d in range(1, NS):
        gcopy(d, True).wait_recv()

    def sum_step(b, carry):
        total = g_recv[0, b].astype(F32)
        for n in range(1, NS):
            total = total + g_recv[n, b].astype(F32)
        sg[b] = total.astype(BF16)
        return carry

    lax.fori_loop(0, NC, sum_step, 0)

    def ccopy(d, inward):
        there, here = (col + d) % NC, (col + NC - d) % NC
        return copy(sg.at[there], cg.at[here if inward else col], c_ss.at[d], c_rs.at[d], col=there)

    for d in range(1, NC):
        ccopy(d, False).start()
    cg[col] = sg[col]

    for d, x in pys:
        pycopy(d, x).wait_recv()

    def py_step(s, carry):
        at = pl.ds(pl.multiple_of(s * B, B), B)

        def total(x):
            v = pj_send[x * 4 + yy, at, :].astype(F32)
            for d in range(3):
                v = v + py_recv[d, x, at, :].astype(F32)
            return v

        px_own[at, :] = total(xh) + tokens[at, :].astype(F32)
        px_send[at, :] = total(1 - xh).astype(BF16)
        return carry

    lax.fori_loop(0, 4, py_step, 0)
    px = copy(px_send, px_recv, px_ss, px_rs, col=xp)
    px.start()
    for d in range(1, NC):
        ccopy(d, True).wait_recv()
    for c in range(NC):
        cg_f[c * 48 : c * 48 + 48, :] = cg[c].astype(F32)
    for i in range(Q):
        bg[samp, i] = cg_f[pl.ds(i, 16, stride=Q), :].astype(BF16)

    def bcopy(d, inward):
        return samp_copy(lambda _: bg.at[samp], lambda n: bg.at[n], b_ss, b_rs, d, inward)

    for d in range(1, NS):
        bcopy(d, False).start()
    px.wait_recv()
    tokens_out[...] = (px_own[...] + px_recv[...].astype(F32)).astype(BF16)
    for m in range(6):
        pocopy(0, m, True).wait_recv()
    prcopy(True).wait_recv()
    for d in range(1, NS):
        bcopy(d, True).wait_recv()

    for c in [slab_x, px, prcopy(False)] + slab_own + slab_on:
        c.wait_send()
    for d, x in pys:
        pycopy(d, x).wait_send()
    for m in range(6):
        for k in range(2):
            pocopy(k, m, False).wait_send()

    for n in range(CH):
        for s in range(2):
            for t in range(1, 5):
                rcopy(n, t, s, False).wait_send()
        for s in y_ways(n):
            ycopy(n, s).wait_send()
        if n < CH - 2:
            for s in range(2):
                zcopy(n, s).wait_send()
        for d in range(1, NS):
            tcopy(n, d, False).wait_send()
        xcopy(n).wait_send()
    for t in range(1, 5):
        for s in range(2):
            for c in kvcopies(t, s, False):
                c.wait_send()
    for d in range(1, NC):
        hcopy(d, False).wait_send()
        ccopy(d, False).wait_send()
    for d in range(1, NS):
        hgcopy(d, False).wait_send()
        gcopy(d, False).wait_send()
        bcopy(d, False).wait_send()


def split(v):
    high = v.astype(BF16)
    rest = v - high.astype(F32)
    mid = rest.astype(BF16)
    return high, mid, (rest - mid.astype(F32)).astype(BF16)


def finish(pair_rows, token_rows, bg, lnb, wpbt, pair_out, tokens_out, pair_grad):
    @pl.when(pl.program_id(0) == 0)
    def _():
        tokens_out[...] = token_rows[...]

    pair_out[...] = pair_rows[...]
    ones = mean_weights()
    weights = wpbt[...].astype(F32) * lnb[...]
    weights = weights - jnp.mean(weights, axis=-1, keepdims=True)
    weights = jnp.concatenate(split(weights), axis=0)
    empty = jnp.zeros((48, 128), BF16)
    weights = jnp.concatenate(
        [jnp.concatenate([weights, empty], axis=1), jnp.concatenate([empty, weights], axis=1)], axis=0
    )
    for e in range(4):
        at = slice(e * 4 * B, e * 4 * B + 4 * B)
        even, odd = [
            jnp.concatenate([bg[e * 4 + n], bg[e * 4 + 2 + n]], axis=1) for n in range(2)
        ]
        both = tn(jnp.concatenate([even] * 3 + [odd] * 3, axis=0), weights)
        scaled = jnp.concatenate(
            [both[0:B, :128], both[0:B, 128:], both[128 : 128 + B, :128], both[128 : 128 + B, 128:]], axis=0
        )
        center, inv = centered(pair_rows[at, :], ones)
        unit = center * inv
        pair_grad[at, :] = inv * (scaled - unit * jnp.mean(scaled * unit, axis=-1, keepdims=True))


def per_device(
    pair, crop_mask, w_agate, w_aval, w_bgate, w_bval, w_outgate, w_outproj, ln_pair,
    w_trans_gate, w_trans_up, w_trans_down, ln_bias, w_pairbias, tokens, ln_token,
    w_query, w_key, w_value, w_gate, w_output, cotangent,
):
    wpbt = w_pairbias.T
    lnb = ln_bias.reshape(1, 128)
    args = (
        pair.reshape(B * B, 128), crop_mask, crop_mask.reshape(6, 128),
        w_agate, w_aval, w_bgate, w_bval, ln_pair.reshape(1, 128), w_outgate, w_outproj,
        w_trans_gate, w_trans_up, w_trans_down, lnb, wpbt,
        tokens.reshape(4 * B, B), cotangent.reshape(4 * B, B), ln_token.reshape(6, 128),
        w_query.T, w_key.T, w_value.T, w_gate.T, w_output,
    )
    vm = pltpu.VMEM
    dma = pltpu.SemaphoreType.DMA
    scratch = [
        vm((4, 128, 128), BF16),
        vm((256, 256), BF16),
        vm((2 * B, NC * B), F32),
        vm((2 * B, NC * B), F32),
        vm((256, 256), BF16),
        vm((256, 256), BF16),
        vm((6 * CR, 128), BF16),
        vm((B * B + 32, 128), F32),
        vm((32 * B, 128), F32),
        vm((G * B, 128), F32),
        vm((CH, 3, 2 * B, B), BF16),
        vm((CH, NR, RC, 128), BF16),
        vm((CH, 4, 2, RC, 128), BF16),
        vm((CH, 2, 2, RC // 2, 128), BF16),
        vm((CH, 3, 2, RC, 128), BF16),
        vm((CH, RC, 128), F32),
        vm((CH, RC, 128), BF16),
        vm((CH, RC, 128), BF16),
        vm((NC, 2, 4 * B, B), BF16),
        vm((4 * B, B), BF16),
        vm((4, NR * B, B), BF16),
        vm((4, NR * B, B), BF16),
        vm((4 * B, B), F32),
        vm((4 * B, B), BF16),
        vm((NS, CH, 2, 48, 128), BF16),
        vm((NS, CH, 2, 48, 128), BF16),
        vm((64 * 48, 128), F32),
        vm((16 * Q, 128), F32),
        vm((NC, 48, 128), BF16),
        vm((NC, NS, 48, 128), BF16),
        vm((2 * B, NC * B), F32),
        vm((4, 2 * B, NC * B), F32),
        vm((4, 2 * B, NC * B), F32),
        vm((2 * B, NC * B), F32),
        vm((NS, NC, 48, 128), BF16),
        vm((NS, NC, 48, 128), BF16),
        vm((NC, 4 * B, B), BF16),
        vm((3, 2, 4 * B, B), BF16),
        vm((4 * B, B), F32),
        vm((4 * B, B), BF16),
        vm((4 * B, B), BF16),
        vm((NC, 48, 128), BF16),
        vm((NC, 48, 128), BF16),
        vm((16 * Q, 128), F32),
    ]
    sems = [(7,)] * 2 + [(CH, 2, 4)] * 2 + [(CH, 2)] * 2 + [(CH, 3)] * 2 + [(CH,)] * 2
    sems += [(2, 2, 4)] * 2 + [(CH, 4)] * 2 + [(8,)] * 2 + [(4,)] * 2 + [(2, 6)] * 2 + [None] * 2
    sems += [(4, 2)] * 2 + [None] * 2 + [(4,)] * 2 + [(8,)] * 2 + [(4,)] * 2
    scratch += [dma if s is None else dma(s) for s in sems]
    spec = pl.BlockSpec(memory_space=pltpu.VMEM)
    specs = [spec] * len(args)
    specs[1] = pl.BlockSpec(memory_space=pltpu.SMEM)
    pair_rows, token_rows, bg = pl.pallas_call(
        kernel,
        out_shape=(
            jax.ShapeDtypeStruct((B * B, 128), BF16),
            jax.ShapeDtypeStruct((4 * B, B), BF16),
            jax.ShapeDtypeStruct((NS, Q, 16, 128), BF16),
        ),
        in_specs=specs,
        out_specs=(spec,) * 3,
        scratch_shapes=scratch,
        compiler_params=pltpu.CompilerParams(
            collective_id=0, has_side_effects=True, vmem_limit_bytes=56 * 1024 * 1024
        ),
    )(*args)
    rows = pl.BlockSpec((16 * B, 128), lambda i: (i, 0))
    whole = pl.BlockSpec((4 * B, B), lambda i: (0, 0))
    outs = pl.pallas_call(
        finish,
        grid=(B // 16,),
        out_shape=(
            jax.ShapeDtypeStruct((B * B, 128), BF16),
            jax.ShapeDtypeStruct((4 * B, B), BF16),
            jax.ShapeDtypeStruct((B * B, 128), F32),
        ),
        in_specs=[
            rows,
            whole,
            pl.BlockSpec((16, 16, 128), lambda i: (i, 0, 0)),
            pl.BlockSpec((1, 128), lambda i: (0, 0)),
            pl.BlockSpec((16, 128), lambda i: (0, 0)),
        ],
        out_specs=(rows, whole, rows),
    )(pair_rows, token_rows, bg.reshape(B, 16, 128), lnb, wpbt)
    return (
        outs[0].reshape(B, B, 128),
        outs[1].reshape(4, B, B),
        outs[2].reshape(B, B, 128),
    )


def solution(mesh):
    placed = (
        P("row", "col", None),
        P(), P(), P(), P(), P(), P(), P(), P(), P(), P(), P(), P(), P(),
        P("samp", "row", "col"),
        P(),
        P(None, "col"),
        P(None, "col"),
        P(None, "col"),
        P(None, "col"),
        P("col", None),
        P("samp", "row", "col"),
    )
    return jax.shard_map(
        per_device,
        mesh=mesh,
        in_specs=placed,
        out_specs=(P("row", "col", None), P("samp", "row", "col"), P("row", "col", None)),
        check_vma=False,
    )
```
